32 devices in a mesh: dp: 8 (over z, y), expert: 4 (over x, core).
Axes of the slice: x: 2, y: 2, z: 4, core: 2. Of those that a mesh axis runs over, the one named last changes fastest.
Arguments:
- hidden_in: bfloat16 [32768, 768], P(('dp', 'expert')), may hold values from -6 to 6
- gate_prior: float32 [32768, 8], P(('dp', 'expert')), may hold values from -6 to 6
- routes: int32 [32768, 2], P(('dp', 'expert')), may hold values from 0 to 7, all different within a row
- priority: int32 [32, 1024], P(('dp', 'expert')), may hold values from 0 to 1023, each once within a row
- segments: int32 [32, 1024], P(('dp', 'expert')), may hold values from 0 to 5, never falling along the last dimension, each value on 1 to 768 neighbouring positions
- cotangent: bfloat16 [32768, 768], P(('dp', 'expert')), may hold values from -6 to 6
- attend_in: float32 [768, 2304], P(('dp', 'expert')), may hold values from -0.21875 to 0.21875
- first_attend_in: float32 [768, 2304], P(('dp', 'expert')), may hold values from -0.0029296875 to 0.0029296875
- second_attend_in: float32 [768, 2304], P(('dp', 'expert')), may hold values from 1e-08 to 1e-07
- attend_out: float32 [768, 768], P(('dp', 'expert')), may hold values from -1.25 to 1.25
- first_attend_out: float32 [768, 768], P(('dp', 'expert')), may hold values from -0.0029296875 to 0.0029296875
- second_attend_out: float32 [768, 768], P(('dp', 'expert')), may hold values from 1e-08 to 1e-07
- router: float32 [768, 8], P(('dp', 'expert')), may hold values from -0.109375 to 0.109375
- first_router: float32 [768, 8], P(('dp', 'expert')), may hold values from -0.0029296875 to 0.0029296875
- second_router: float32 [768, 8], P(('dp', 'expert')), may hold values from 1e-08 to 1e-07
- gate_mix: float32 [8, 8], replicated, may hold values from -1 to 1
- first_gate_mix: float32 [8, 8], replicated, may hold values from -0.0029296875 to 0.0029296875
- second_gate_mix: float32 [8, 8], replicated, may hold values from 1e-08 to 1e-07
- constants: float32 [768, 6], P(('dp', 'expert')), may hold values from -0.4375 to 0.4375
- first_constants: float32 [768, 6], P(('dp', 'expert')), may hold values from -0.0029296875 to 0.0029296875
- second_constants: float32 [768, 6], P(('dp', 'expert')), may hold values from 1e-08 to 1e-07
- norm_gains: float32 [2, 768], P(None, ('dp', 'expert')), may hold values from 0.5 to 1.5
- first_norm_gains: float32 [2, 768], P(None, ('dp', 'expert')), may hold values from -0.0029296875 to 0.0029296875
- second_norm_gains: float32 [2, 768], P(None, ('dp', 'expert')), may hold values from 1e-08 to 1e-05
- expert_in: float32 [4, 768, 4096], P('expert', 'dp'), may hold values from -0.21875 to 0.21875
- first_expert_in: float32 [4, 768, 4096], P('expert', 'dp'), may hold values from -0.0029296875 to 0.0029296875
- second_expert_in: float32 [4, 768, 4096], P('expert', 'dp'), may hold values from 1e-08 to 1e-07
- expert_out: float32 [4, 2048, 768], P('expert', 'dp'), may hold values from -0.5 to 0.5
- first_expert_out: float32 [4, 2048, 768], P('expert', 'dp'), may hold values from -0.0029296875 to 0.0029296875
- second_expert_out: float32 [4, 2048, 768], P('expert', 'dp'), may hold values from 1e-11 to 1e-08
Outputs:
- activations: bfloat16 [32768, 768], P(('dp', 'expert'))
- input_grad: float32 [32768, 768], P(('dp', 'expert'))
- grad_norm: float32 [], replicated
- grad_attend_in: float32 [768, 2304], P(('dp', 'expert'))
- new_attend_in: float32 [768, 2304], P(('dp', 'expert'))
- new_first_attend_in: float32 [768, 2304], P(('dp', 'expert'))
- new_second_attend_in: float32 [768, 2304], P(('dp', 'expert'))
- copy_attend_in: bfloat16 [768, 2304], P(('dp', 'expert'))
- grad_attend_out: float32 [768, 768], P(('dp', 'expert'))
- new_attend_out: float32 [768, 768], P(('dp', 'expert'))
- new_first_attend_out: float32 [768, 768], P(('dp', 'expert'))
- new_second_attend_out: float32 [768, 768], P(('dp', 'expert'))
- copy_attend_out: bfloat16 [768, 768], P(('dp', 'expert'))
- grad_router: float32 [768, 8], P(('dp', 'expert'))
- new_router: float32 [768, 8], P(('dp', 'expert'))
- new_first_router: float32 [768, 8], P(('dp', 'expert'))
- new_second_router: float32 [768, 8], P(('dp', 'expert'))
- copy_router: bfloat16 [768, 8], P(('dp', 'expert'))
- grad_gate_mix: float32 [8, 8], replicated
- new_gate_mix: float32 [8, 8], replicated
- new_first_gate_mix: float32 [8, 8], replicated
- new_second_gate_mix: float32 [8, 8], replicated
- copy_gate_mix: bfloat16 [8, 8], replicated
- grad_constants: float32 [768, 6], P(('dp', 'expert'))
- new_constants: float32 [768, 6], P(('dp', 'expert'))
- new_first_constants: float32 [768, 6], P(('dp', 'expert'))
- new_second_constants: float32 [768, 6], P(('dp', 'expert'))
- copy_constants: bfloat16 [768, 6], P(('dp', 'expert'))
- grad_norm_gains: float32 [2, 768], P(None, ('dp', 'expert'))
- new_norm_gains: float32 [2, 768], P(None, ('dp', 'expert'))
- new_first_norm_gains: float32 [2, 768], P(None, ('dp', 'expert'))
- new_second_norm_gains: float32 [2, 768], P(None, ('dp', 'expert'))
- copy_norm_gains: bfloat16 [2, 768], P(None, ('dp', 'expert'))
- grad_expert_in: float32 [4, 768, 4096], P('expert', 'dp')
- new_expert_in: float32 [4, 768, 4096], P('expert', 'dp')
- new_first_expert_in: float32 [4, 768, 4096], P('expert', 'dp')
- new_second_expert_in: float32 [4, 768, 4096], P('expert', 'dp')
- copy_expert_in: bfloat16 [4, 768, 4096], P('expert', 'dp')
- grad_expert_out: float32 [4, 2048, 768], P('expert', 'dp')
- new_expert_out: float32 [4, 2048, 768], P('expert', 'dp')
- new_first_expert_out: float32 [4, 2048, 768], P('expert', 'dp')
- new_second_expert_out: float32 [4, 2048, 768], P('expert', 'dp')
- copy_expert_out: bfloat16 [4, 2048, 768], P('expert', 'dp')
The draws below stay inside these ranges and needn't reach their ends.
Inputs may be any that keep to these rules, and one draw needn't show every extreme that they name: `routes`: each row names 2 different kinds; kinds below 4 are feed-forward experts, 4 the zero expert, 5 the copy expert, the rest constant experts. `priority`: each row is a permutation. `segments`: numbers never fall along a sequence; a document has 1 to 768 tokens.
All inputs are finite; a program needn't handle non-finite values.
Results may differ from the reference program's by a relative error of at most 0.013.
The reference program's roundings to bfloat16 on the way count: a program that leaves them out, or rounds other values in their place, can miss the bound.
Values may be sent and summed in bfloat16 or wider, within the bound.
No kernel may reach another device: no remote copies, remote signals or barrier semaphores. Data moves between devices by JAX's collectives and lax.ppermute only.
A program may use at most 320 MiB of HBM per device.

```python
import math
import jax
import jax.numpy as jnp
import numpy as np
from jax import lax

D = 768
FF = 2048
HEADS = 12
HEAD_DIM = 64
TOP = 2
NCONST = 2
SEQ = 1024
EXPERTS = 4
NE = 8
TOK_DEV = 1024
NSEQ = 32
TOKENS = 32768
CAP = 256
DOCS = 6
DOC_MOST = 768
N_DP = 8
N_EXPERT = 4
DEVICES = 32


def shard_levels(key, extent, pieces, low, top_value):
    gain = 1.0
    for dim, blocks in pieces:
        steps = jax.random.uniform(jax.random.fold_in(jax.random.fold_in(key, 6), dim), (blocks,), jnp.float32, low / len(pieces), top_value / len(pieces))
        gain = gain * jnp.repeat(jnp.exp(steps), extent[dim] // blocks).reshape((-1,) + (1,) * (len(extent) - 1 - dim))
    return gain


def different_ones(rng, rows, number_of, top, lift):
    order = jax.random.permutation(jax.random.fold_in(rng, 1), number_of)
    favour = order
    for power in range(3):
        favour = favour * favour // number_of
    favour = favour * lift // number_of
    tickets = jax.random.randint(jax.random.fold_in(rng, 2), (rows, number_of), 0, 4096) + favour
    holders = jax.random.permutation(jax.random.fold_in(rng, 3), rows)[jnp.arange(number_of) % rows]
    tickets = jnp.where(jnp.arange(rows)[:, None] == holders[None, :], 1 << 14, tickets)
    score = tickets * number_of + jnp.arange(number_of)
    return lax.top_k(score.astype(jnp.int32), top)[1].astype(jnp.int32)


def profile(count, total, bound, lean):
    loads = [(1 << 20) // math.isqrt(standing ** lean) + 1 for standing in range(2, count + 1)]
    surplus, given = total - bound - (count - 1), [1] * (count - 1)
    while surplus > 0:
        candidates = [i for i in range(count - 1) if given[i] < bound]
        pool, left = sum([loads[i] for i in candidates]), surplus
        for i in candidates:
            more = min(bound - given[i], max(1, left * loads[i] // pool), surplus)
            given[i] = given[i] + more
            surplus = surplus - more
    return np.array([bound] + given)


def ragged(own_key, number_of, total, most, slope):
    if number_of == 2:
        one = jax.random.randint(own_key, (), max(1, total - most), min(most, total - 1) + 1)
        return jnp.stack([one, total - one])
    tallies = jnp.asarray(profile(number_of, total, most, slope), jnp.int32)
    couples = (number_of - 1) // 2
    donor, sink = tallies[1:1 + 2 * couples:2], tallies[2:2 + 2 * couples:2]
    margin = jnp.minimum(donor - 1, most - sink)
    moved = jax.random.randint(jax.random.fold_in(own_key, 1), (couples,), 0, 1 << 20) % (margin + 1)
    tallies = tallies.at[1:1 + 2 * couples:2].set(donor - moved).at[2:2 + 2 * couples:2].set(sink + moved)
    return tallies[jax.random.permutation(jax.random.fold_in(own_key, 2), number_of)]


def normal_values(rng, shape, spread, bound, cuts=(), kind=jnp.bfloat16):
    values = jax.random.normal(rng, shape, jnp.float32) * spread
    if len(cuts) > 0:
        values = shard_levels(rng, shape, cuts, -0.22, 0.18) * values
    return jnp.clip(values, min=-bound, max=bound).astype(kind)


def setup_inputs(seed: int = 0) -> dict:
    keys = jax.random.split(jax.random.key(seed), 31)
    hidden_in = normal_values(keys[0], (TOKENS, D), 1.0, 6.0, ((0, 32),))
    gate_prior = normal_values(keys[1], (TOKENS, NE), 1.0, 6.0, ((0, 32),), jnp.float32)
    routes = different_ones(keys[2], TOKENS, NE, TOP, 4096)
    priority = jax.vmap(lambda own: jax.random.permutation(own, TOK_DEV))(jax.random.split(keys[3], DEVICES)).reshape((DEVICES, TOK_DEV)).astype(jnp.int32)
    segments = jax.vmap(lambda own: jnp.searchsorted(jnp.cumsum(ragged(own, DOCS, SEQ, DOC_MOST, 1)), jnp.arange(SEQ), side="right"))(jax.random.split(keys[4], NSEQ)).reshape((NSEQ, SEQ)).astype(jnp.int32)
    cotangent = normal_values(keys[5], (TOKENS, D), 1.0, 6.0, ((0, 32),))
    attend_in = normal_values(keys[6], (D, 3 * D), D ** -0.5, 0.21875, ((0, 32),), jnp.float32)
    first_attend_in = normal_values(keys[7], (D, 3 * D), 0.0002, 0.0029296875, ((0, 32),), jnp.float32)
    second_attend_in = jnp.clip(jnp.exp(math.log(1.0000000116860974e-07) - 2.3025851 * jax.random.uniform(keys[8], (D, 3 * D), jnp.float32) ** shard_levels(keys[8], (D, 3 * D), ((0, 32),), -0.2, 0.2)), 9.99999993922529e-09, 1.0000000116860974e-07)
    attend_out = normal_values(keys[9], (D, D), (D // 32) ** -0.5, 1.25, ((0, 32),), jnp.float32)
    first_attend_out = normal_values(keys[10], (D, D), 0.0002, 0.0029296875, ((0, 32),), jnp.float32)
    second_attend_out = jnp.clip(jnp.exp(math.log(1.0000000116860974e-07) - 2.3025851 * jax.random.uniform(keys[11], (D, D), jnp.float32) ** shard_levels(keys[11], (D, D), ((0, 32),), -0.2, 0.2)), 9.99999993922529e-09, 1.0000000116860974e-07)
    router = normal_values(keys[12], (D, NE), (4 * D) ** -0.5, 0.109375, ((0, 32),), jnp.float32)
    first_router = normal_values(keys[13], (D, NE), 0.0002, 0.0029296875, ((0, 32),), jnp.float32)
    second_router = jnp.clip(jnp.exp(math.log(1.0000000116860974e-07) - 2.3025851 * jax.random.uniform(keys[14], (D, NE), jnp.float32) ** shard_levels(keys[14], (D, NE), ((0, 32),), -0.2, 0.2)), 9.99999993922529e-09, 1.0000000116860974e-07)
    gate_mix = normal_values(keys[15], (NE, NE), (4 * NE) ** -0.5, 1.0, (), jnp.float32)
    first_gate_mix = normal_values(keys[16], (NE, NE), 0.0002, 0.0029296875, (), jnp.float32)
    second_gate_mix = jnp.clip(jnp.exp(jax.random.uniform(keys[17], (NE, NE), jnp.float32, math.log(9.99999993922529e-09), math.log(1.0000000116860974e-07))), 9.99999993922529e-09, 1.0000000116860974e-07)
    constants = normal_values(keys[18], (D, 3 * NCONST), (D // 4) ** -0.5, 0.4375, ((0, 32),), jnp.float32)
    first_constants = normal_values(keys[19], (D, 3 * NCONST), 0.0002, 0.0029296875, ((0, 32),), jnp.float32)
    second_constants = jnp.clip(jnp.exp(math.log(1.0000000116860974e-07) - 2.3025851 * jax.random.uniform(keys[20], (D, 3 * NCONST), jnp.float32) ** shard_levels(keys[20], (D, 3 * NCONST), ((0, 32),), -0.2, 0.2)), 9.99999993922529e-09, 1.0000000116860974e-07)
    norm_gains = jnp.clip(1.0 + 0.1 * jax.random.normal(keys[21], (2, D), jnp.float32), 0.5, 1.5)
    first_norm_gains = normal_values(keys[22], (2, D), 0.0002, 0.0029296875, ((1, 32),), jnp.float32)
    second_norm_gains = jnp.clip(jnp.exp(math.log(9.999999747378752e-06) - 6.9077553 * jax.random.uniform(keys[23], (2, D), jnp.float32) ** shard_levels(keys[23], (2, D), ((1, 32),), -0.2, 0.2)), 9.99999993922529e-09, 9.999999747378752e-06)
    expert_in = normal_values(keys[24], (EXPERTS, D, 2 * FF), D ** -0.5, 0.21875, ((0, 4), (1, 8)), jnp.float32)
    first_expert_in = normal_values(keys[25], (EXPERTS, D, 2 * FF), 0.0002, 0.0029296875, ((0, 4), (1, 8)), jnp.float32)
    second_expert_in = jnp.clip(jnp.exp(math.log(1.0000000116860974e-07) - 2.3025851 * jax.random.uniform(keys[26], (EXPERTS, D, 2 * FF), jnp.float32) ** shard_levels(keys[26], (EXPERTS, D, 2 * FF), ((0, 4), (1, 8)), -0.2, 0.2)), 9.99999993922529e-09, 1.0000000116860974e-07)
    expert_out = normal_values(keys[27], (EXPERTS, FF, D), (FF // 16) ** -0.5, 0.5, ((0, 4), (1, 8)), jnp.float32)
    first_expert_out = normal_values(keys[28], (EXPERTS, FF, D), 0.0002, 0.0029296875, ((0, 4), (1, 8)), jnp.float32)
    second_expert_out = jnp.clip(jnp.exp(math.log(9.99999993922529e-09) - 6.9077553 * jax.random.uniform(keys[29], (EXPERTS, FF, D), jnp.float32) ** shard_levels(keys[29], (EXPERTS, FF, D), ((0, 4), (1, 8)), -0.2, 0.2)), 9.999999960041972e-12, 9.99999993922529e-09)
    return {"hidden_in": hidden_in, "gate_prior": gate_prior, "routes": routes, "priority": priority, "segments": segments, "cotangent": cotangent, "attend_in": attend_in, "first_attend_in": first_attend_in, "second_attend_in": second_attend_in, "attend_out": attend_out, "first_attend_out": first_attend_out, "second_attend_out": second_attend_out, "router": router, "first_router": first_router, "second_router": second_router, "gate_mix": gate_mix, "first_gate_mix": first_gate_mix, "second_gate_mix": second_gate_mix, "constants": constants, "first_constants": first_constants, "second_constants": second_constants, "norm_gains": norm_gains, "first_norm_gains": first_norm_gains, "second_norm_gains": second_norm_gains, "expert_in": expert_in, "first_expert_in": first_expert_in, "second_expert_in": second_expert_in, "expert_out": expert_out, "first_expert_out": first_expert_out, "second_expert_out": second_expert_out}


norm_epsilon = 1e-05
adam_epsilon = 1e-08
learn_rates = (0.01, 0.04, 0.01, 0.03, 0.01, 0.1, 0.01, 0.01)
decay_rate = 0.1
beta_moment = 0.5
step_number = 4.0
clip_limit = 1.0
score_scale = 0.125
masked_score = -1e+30
highest = lax.Precision.HIGHEST

@jax.custom_vjp
def low(v):
    return lax.optimization_barrier(v.astype(jnp.bfloat16)).astype(jnp.float32)

@jax.custom_vjp
def low_back(v):
    return v

def low_keep(v):
    return (low(v), None)

def low_pass(kept, grad):
    return (grad,)

def back_keep(v):
    return (v, None)

def back_low(kept, grad):
    return (low(grad),)
low.defvjp(low_keep, low_pass)
low_back.defvjp(back_keep, back_low)

def norm_rows(values, gain_row):
    scaling = lax.rsqrt(lax.optimization_barrier(jnp.mean(values * values, axis=-1, keepdims=True)) + norm_epsilon)
    return values * scaling * gain_row

def pair_tables(routes, priority, experts, total_kinds, capacity):
    tokens_here = routes.shape[0]
    width_top = routes.shape[1]
    kind_ids = jnp.arange(total_kinds, dtype=jnp.int32)
    one_hot = lax.optimization_barrier(jnp.sum((routes[:, :, None] == kind_ids[None, None, :]).astype(jnp.float32), axis=1))
    earlier = (priority[None, :] < priority[:, None]).astype(jnp.float32)
    before = jnp.dot(earlier, one_hot, precision=highest)
    slots = jnp.take_along_axis(before, routes, axis=1).astype(jnp.int32)
    kept_pairs = jnp.logical_and(routes < experts, slots < capacity)
    targets = jnp.where(kept_pairs, routes * capacity + slots, experts * capacity).astype(jnp.int32)
    pair_ids = jnp.arange(tokens_here * width_top, dtype=jnp.int32)
    owners = jnp.full((experts * capacity,), tokens_here * width_top, dtype=jnp.int32)
    owners = owners.at[targets.reshape(-1)].set(pair_ids, mode='drop')
    return (targets, owners)

def mixture(normed, paired, router_w, mixer_w, constant_w, prior, routes, experts):
    logits = jnp.dot(normed, router_w, precision=highest) + jnp.dot(prior, mixer_w, precision=highest)
    probabilities = jax.nn.softmax(logits, axis=-1)
    chosen = jnp.take_along_axis(probabilities, routes, axis=1)
    constant_count = constant_w.shape[1] // 3
    gate_logits = jnp.dot(normed, constant_w[:, :2 * constant_count], precision=highest)
    shares = jax.nn.softmax(gate_logits.reshape(normed.shape[0], constant_count, 2), axis=-1)
    blended = jnp.zeros_like(normed)
    for route_index in range(routes.shape[1]):
        expert_ids = routes[:, route_index:route_index + 1]
        branch_out = paired[:, route_index] + jnp.where(expert_ids == experts + 1, normed, 0.0)
        for const_index in range(constant_count):
            constant_term = shares[:, const_index, 0:1] * normed + shares[:, const_index, 1:2] * constant_w[:, 2 * constant_count + const_index][None, :]
            branch_out = branch_out + jnp.where(expert_ids == experts + 2 + const_index, constant_term, 0.0)
        blended = blended + chosen[:, route_index:route_index + 1] * branch_out
    return blended

def attend(sequence, segment, weight_in, weight_out, gain_row):
    normed = low(norm_rows(sequence, gain_row))
    packed = low_back(low(jnp.dot(normed, weight_in, precision=highest))).reshape(SEQ, 3, HEADS, HEAD_DIM)
    raw = low_back(jnp.einsum('qhd,khd->hqk', packed[:, 0], packed[:, 1], precision=highest))
    places = jnp.arange(SEQ, dtype=jnp.int32)
    allowed = jnp.logical_and(segment[:, None] == segment[None, :], places[None, :] <= places[:, None])
    scores = jnp.where(allowed[None], raw * score_scale, masked_score)
    weights = low(jax.nn.softmax(scores, axis=-1))
    attended = low_back(low(jnp.einsum('hqk,khd->qhd', weights, packed[:, 2], precision=highest))).reshape(SEQ, D)
    return sequence + low_back(jnp.dot(attended, weight_out, precision=highest))

def expert_apply(row_block, weight_inner, weight_outer):
    flat = row_block.reshape(-1, D)
    joined = low_back(jnp.dot(flat, weight_inner, precision=highest))
    activated = low(jax.nn.silu(joined[:, :FF]) * joined[:, FF:])
    return low_back(low(jnp.dot(activated, weight_outer, precision=highest))).reshape(row_block.shape)

def adam_step(master, first, second, grad, factor, step_rate):
    clipped = grad * factor
    first_new = beta_moment * first + (1.0 - beta_moment) * clipped
    second_new = beta_moment * second + (1.0 - beta_moment) * clipped * clipped
    correct = 1.0 - beta_moment ** step_number
    update = first_new / correct / (jnp.sqrt(second_new / correct) + adam_epsilon) + decay_rate * master
    master_new = master - step_rate * update
    return (grad, master_new, first_new, second_new, master_new.astype(jnp.bfloat16))

def reference(hidden_in, gate_prior, routes, priority, segments, cotangent, attend_in, first_attend_in, second_attend_in, attend_out, first_attend_out, second_attend_out, router, first_router, second_router, gate_mix, first_gate_mix, second_gate_mix, constants, first_constants, second_constants, norm_gains, first_norm_gains, second_norm_gains, expert_in, first_expert_in, second_expert_in, expert_out, first_expert_out, second_expert_out):
    device_routes = routes.reshape(DEVICES, TOK_DEV, TOP)
    targets, owners = lax.map(lambda element: pair_tables(element[0], element[1], EXPERTS, NE, CAP), (device_routes, priority))

    def forward(hidden, weight_in, weight_out, router_w, mixer_w, constant_w, gain_w, inner_w, outer_w):
        weight_in = low(weight_in)
        weight_out = low(weight_out)
        router_w = low(router_w)
        mixer_w = low(mixer_w)
        constant_w = low(constant_w)
        gain_rows = low(gain_w)
        inner_w = low(inner_w)
        outer_w = low(outer_w)
        sequences = hidden.reshape(NSEQ, SEQ, D)

        def attend_one(element):
            return attend(element[0], element[1], weight_in, weight_out, gain_rows[0])
        middle = lax.map(jax.checkpoint(attend_one), (sequences, segments)).reshape(TOKENS, D)
        normed = low(norm_rows(middle, gain_rows[1]))
        blocks = normed.reshape(DEVICES, TOK_DEV, D)
        outgoing = jax.vmap(lambda row_block, indices: jnp.take(row_block, indices // TOP, axis=0, mode='fill', fill_value=0.0))(blocks, owners)
        per_expert = low_back(outgoing.reshape(N_DP, N_EXPERT, EXPERTS, CAP, D).transpose(2, 0, 1, 3, 4))

        def expert_one(element):
            return expert_apply(element[0], element[1], element[2])
        produced = lax.map(jax.checkpoint(expert_one), (per_expert, inner_w, outer_w))
        returned = produced.transpose(1, 2, 0, 3, 4).reshape(DEVICES, EXPERTS * CAP, D)
        paired = jax.vmap(lambda row_block, indices: jnp.take(row_block, indices, axis=0, mode='fill', fill_value=0.0))(returned, targets).reshape(TOKENS, TOP, D)
        return middle + mixture(normed, paired, router_w, mixer_w, constant_w, gate_prior, routes, EXPERTS)
    output, pull = jax.vjp(forward, hidden_in.astype(jnp.float32), attend_in, attend_out, router, gate_mix, constants, norm_gains, expert_in, expert_out)
    grads = pull(cotangent.astype(jnp.float32))
    input_grad = grads[0]
    weight_grads = grads[1:]
    grad_norm = jnp.sqrt(sum((jnp.sum(grad * grad) for grad in weight_grads)))
    factor = clip_limit / jnp.maximum(grad_norm, clip_limit)
    masters = (attend_in, attend_out, router, gate_mix, constants, norm_gains, expert_in, expert_out)
    firsts = (first_attend_in, first_attend_out, first_router, first_gate_mix, first_constants, first_norm_gains, first_expert_in, first_expert_out)
    seconds = (second_attend_in, second_attend_out, second_router, second_gate_mix, second_constants, second_norm_gains, second_expert_in, second_expert_out)
    results = (output.astype(jnp.bfloat16), input_grad, grad_norm)
    for index_weight in range(8):
        results = results + adam_step(masters[index_weight], firsts[index_weight], seconds[index_weight], weight_grads[index_weight], factor, learn_rates[index_weight])
    return results
```

```python
import functools

import jax
import jax.numpy as jnp
from jax import lax
from jax.experimental import pallas as pl
from jax.experimental.pallas import tpu as pltpu
from jax.sharding import PartitionSpec as P

D = 768
FF = 2048
HEAD_DIM = 64
PAIR = 2 * HEAD_DIM
BLOCK = 256
LANES = 128
BOTH = ("dp", "expert")

norm_epsilon = 1e-05
adam_epsilon = 1e-08
learn_rates = (0.01, 0.04, 0.01, 0.03, 0.01, 0.1, 0.01, 0.01)
decay_rate = 0.1
beta_moment = 0.5
step_number = 4.0
clip_limit = 1.0
score_scale = 0.125
masked_score = -1e30
highest = lax.Precision.HIGHEST
F32 = jnp.float32
BF16 = jnp.bfloat16

NN = (((1,), (0,)), ((), ()))
NT = (((1,), (1,)), ((), ()))
TN = (((0,), (0,)), ((), ()))

CHOSEN, COEF, SCALE, REST, BETA, GATE_GRAD, PROBS = 0, 2, 3, 4, 8, 16, 32


def dot(left, right, form=NN):
    return lax.dot_general(left, right, form, preferred_element_type=F32)


def iota(shape, dim):
    return lax.broadcasted_iota(jnp.int32, shape, dim)


def row_scale(values):
    return lax.rsqrt(jnp.mean(values * values, axis=-1, keepdims=True) + norm_epsilon)


def params(mebibytes):
    return pltpu.CompilerParams(vmem_limit_bytes=mebibytes << 20)


def whole(shape):
    return pl.BlockSpec(shape, lambda *step: (0,) * len(shape))


def cost(flops, moved, transcendentals=0):
    return pl.CostEstimate(flops=flops, bytes_accessed=moved, transcendentals=transcendentals)


def project_kernel(hidden_ref, gain_ref, weight_ref, normed_ref, packed_ref):
    @pl.when(pl.program_id(0) == 0)
    def _():
        values = hidden_ref[...].astype(F32)
        normed_ref[...] = (values * row_scale(values) * gain_ref[...]).astype(BF16)

    packed_ref[...] = dot(normed_ref[...], weight_ref[...]).astype(BF16)


def project(hidden, gain, weights):
    tokens = hidden.shape[0]
    return pl.pallas_call(
        project_kernel,
        grid=(3,),
        in_specs=[
            whole((tokens, D)),
            whole((1, D)),
            pl.BlockSpec((D, D), lambda step: (0, step)),
        ],
        out_specs=[whole((tokens, D)), pl.BlockSpec((tokens, D), lambda step: (0, step))],
        out_shape=[
            jax.ShapeDtypeStruct((tokens, D), BF16),
            jax.ShapeDtypeStruct((tokens, 3 * D), BF16),
        ],
        compiler_params=params(40),
        cost_estimate=cost(6 * tokens * D * D, 10 * tokens * D + 6 * D * D),
        name="project",
    )(hidden, gain, weights)


def attend_forward_kernel(
    query_ref, key_ref, value_ref, seg_column_ref, seg_row_ref, out_ref, logsum_ref, bias_ref, *, block
):
    length = query_ref.shape[0]

    @pl.when(pl.program_id(0) == 0)
    def _():
        for low in range(0, length, block):
            high = low + block
            rows = low + iota((block, high), 0)
            allowed = jnp.logical_and(
                seg_column_ref[low:high, :] == seg_row_ref[:, :high], iota((block, high), 1) <= rows
            )
            bias_ref[low:high, :high] = jnp.where(allowed, 0.0, masked_score)

    for low in range(0, length, block):
        high = low + block
        for head in range(2):
            lanes = slice(head * HEAD_DIM, (head + 1) * HEAD_DIM)
            queries = query_ref[low:high, lanes] * score_scale
            scores = dot(queries, key_ref[:high, lanes], NT) + bias_ref[low:high, :high]
            maximum = jnp.max(scores, axis=1, keepdims=True)
            powers = jnp.exp(scores - maximum)
            totals = jnp.sum(powers, axis=1, keepdims=True)
            weights = (powers * (1.0 / totals)).astype(BF16)
            out_ref[low:high, lanes] = dot(weights, value_ref[:high, lanes]).astype(BF16)
            logsum_ref[0, low:high, head : head + 1] = maximum + jnp.log(totals)


def attend_forward(packed, seg_column, seg_row):
    length = packed.shape[0]
    pairs = D // PAIR
    return pl.pallas_call(
        functools.partial(attend_forward_kernel, block=2 * BLOCK),
        grid=(pairs,),
        in_specs=[
            pl.BlockSpec((length, PAIR), lambda pair: (0, pair)),
            pl.BlockSpec((length, PAIR), lambda pair: (0, pairs + pair)),
            pl.BlockSpec((length, PAIR), lambda pair: (0, 2 * pairs + pair)),
            whole((length, 1)),
            whole((1, length)),
        ],
        out_specs=[
            pl.BlockSpec((length, PAIR), lambda pair: (0, pair)),
            pl.BlockSpec((1, length, 2), lambda pair: (pair, 0, 0)),
        ],
        out_shape=[
            jax.ShapeDtypeStruct((length, D), BF16),
            jax.ShapeDtypeStruct((pairs, length, 2), F32),
        ],
        scratch_shapes=[pltpu.VMEM((length, length), F32)],
        compiler_params=params(48),
        cost_estimate=cost(8 * length * length * D, 8 * length * D, length * length * 8),
        name="attend_forward",
    )(packed, packed, packed, seg_column, seg_row)


def attend_backward_kernel(
    query_ref,
    key_ref,
    value_ref,
    grad_ref,
    logsum_ref,
    seg_column_ref,
    seg_row_ref,
    out_ref,
    bias_ref,
    key_sum,
    value_sum,
    key_out,
    value_out,
    *,
    block,
):
    length = query_ref.shape[0]
    phase = pl.program_id(1)

    @pl.when(jnp.logical_and(pl.program_id(0) == 0, phase == 0))
    def _():
        for low in range(0, length, block):
            high = low + block
            columns = low + iota((high, block), 1)
            allowed = jnp.logical_and(
                seg_column_ref[:high, :] == seg_row_ref[:, low:high],
                iota((high, block), 0) <= columns,
            )
            bias_ref[:high, low:high] = jnp.where(allowed, 0.0, masked_score)

    @pl.when(phase == 0)
    def _():
        key_sum[...] = jnp.zeros_like(key_sum)
        value_sum[...] = jnp.zeros_like(value_sum)
        for low in range(0, length, block):
            high = low + block
            for head in range(2):
                lanes = slice(head * HEAD_DIM, (head + 1) * HEAD_DIM)
                queries = query_ref[low:high, lanes] * score_scale
                grads = grad_ref[low:high, lanes]
                keys = key_ref[:high, lanes]
                scores = dot(keys, queries, NT) + bias_ref[:high, low:high]
                weights = jnp.exp(scores - logsum_ref[0, head : head + 1, low:high])
                grad_weights = dot(value_ref[:high, lanes], grads, NT)
                value_sum[:high, lanes] += dot(weights.astype(BF16), grads)
                centred = jnp.sum(weights * grad_weights, axis=0, keepdims=True)
                grad_raw = (weights * (grad_weights - centred)).astype(BF16)
                key_sum[:high, lanes] += dot(grad_raw, queries)
                out_ref[low:high, lanes] = dot(grad_raw, keys * score_scale, TN).astype(BF16)
        key_out[...] = key_sum[...].astype(BF16)
        value_out[...] = value_sum[...].astype(BF16)

    @pl.when(phase == 1)
    def _():
        out_ref[...] = key_out[...]

    @pl.when(phase == 2)
    def _():
        out_ref[...] = value_out[...]


def attend_backward(packed, grad, logsum, seg_column, seg_row):
    length = packed.shape[0]
    pairs = D // PAIR
    return pl.pallas_call(
        functools.partial(attend_backward_kernel, block=2 * BLOCK),
        grid=(pairs, 3),
        in_specs=[
            pl.BlockSpec((length, PAIR), lambda pair, phase: (0, pair)),
            pl.BlockSpec((length, PAIR), lambda pair, phase: (0, pairs + pair)),
            pl.BlockSpec((length, PAIR), lambda pair, phase: (0, 2 * pairs + pair)),
            pl.BlockSpec((length, PAIR), lambda pair, phase: (0, pair)),
            pl.BlockSpec((1, 2, length), lambda pair, phase: (pair, 0, 0)),
            whole((length, 1)),
            whole((1, length)),
        ],
        out_specs=pl.BlockSpec((length, PAIR), lambda pair, phase: (0, phase * pairs + pair)),
        out_shape=jax.ShapeDtypeStruct((length, 3 * D), BF16),
        scratch_shapes=[
            pltpu.VMEM((length, length), F32),
            pltpu.VMEM((length, PAIR), F32),
            pltpu.VMEM((length, PAIR), F32),
            pltpu.VMEM((length, PAIR), BF16),
            pltpu.VMEM((length, PAIR), BF16),
        ],
        compiler_params=params(48),
        cost_estimate=cost(20 * length * length * D, 14 * length * D, length * length * 8),
        name="attend_backward",
    )(packed, packed, packed, grad, logsum, seg_column, seg_row)


def route_kernel(
    hidden_ref,
    attended_ref,
    upstream_ref,
    extra_ref,
    routes_ref,
    targets_ref,
    gain_ref,
    weight_ref,
    small_ref,
    middle_ref,
    normed_ref,
    table_ref,
    rows_ref,
    grads_ref,
    normed_all,
    first_all,
    second_all,
    *,
    token_steps,
    experts,
    constant_count,
    slot_block,
):
    step = pl.program_id(0)
    block = hidden_ref.shape[0]
    kinds = extra_ref.shape[1]

    @pl.when(step < token_steps)
    def _():
        middle = hidden_ref[...].astype(F32) + dot(attended_ref[...], weight_ref[...])
        scale = row_scale(middle)
        normed = (middle * scale * gain_ref[...]).astype(BF16)
        middle_ref[...] = middle
        normed_ref[...] = normed
        upstream = upstream_ref[...]
        wide = upstream.astype(F32)
        small = dot(normed, small_ref[...])
        meets = dot(upstream, small_ref[...])
        inner = jnp.sum(wide * normed.astype(F32), axis=1, keepdims=True)
        logits = small[:, :kinds] + extra_ref[...]
        powers = jnp.exp(logits - jnp.max(logits, axis=1, keepdims=True))
        probs = powers / jnp.sum(powers, axis=1, keepdims=True)
        places = iota((block, kinds), 1)
        table_ref[...] = jnp.zeros_like(table_ref)
        table_ref[:, PROBS : PROBS + kinds] = probs
        table_ref[:, SCALE : SCALE + 1] = scale
        shares = []
        for which in range(constant_count):
            left = small[:, kinds + 2 * which : kinds + 2 * which + 1]
            right = small[:, kinds + 2 * which + 1 : kinds + 2 * which + 2]
            top = jnp.maximum(left, right)
            left, right = jnp.exp(left - top), jnp.exp(right - top)
            both = left + right
            shares.append((left / both, right / both))
        coef = jnp.zeros((block, 1), F32)
        betas = [jnp.zeros((block, 1), F32)] * constant_count
        amounts = [jnp.zeros((block, 1), F32)] * constant_count
        start = kinds + 2 * constant_count
        met = [meets[:, start + which : start + which + 1] for which in range(constant_count)]
        for route in range(2):
            kind = routes_ref[:, route : route + 1]
            chosen = jnp.sum(jnp.where(places == kind, probs, 0.0), axis=1, keepdims=True)
            table_ref[:, CHOSEN + route : CHOSEN + route + 1] = chosen
            part = jnp.where(kind == experts + 1, 1.0, 0.0)
            rest = jnp.zeros((block, 1), F32)
            for which in range(constant_count):
                here = kind == experts + 2 + which
                part = part + jnp.where(here, shares[which][0], 0.0)
                rest = rest + jnp.where(here, shares[which][1] * met[which], 0.0)
                betas[which] = betas[which] + jnp.where(here, chosen * shares[which][1], 0.0)
                amounts[which] = amounts[which] + jnp.where(here, chosen, 0.0)
            coef = coef + chosen * part
            table_ref[:, REST + route : REST + route + 1] = rest + part * inner
            grads = (chosen * wide).astype(BF16)
            rows = pl.ds(pl.multiple_of(step * block, block), block)
            (first_all if route == 0 else second_all)[rows, :] = grads
        normed_all[pl.ds(pl.multiple_of(step * block, block), block), :] = normed
        table_ref[:, COEF : COEF + 1] = coef
        for which in range(constant_count):
            table_ref[:, BETA + which : BETA + which + 1] = betas[which]
            grad_left = amounts[which] * inner
            grad_right = amounts[which] * met[which]
            mean = shares[which][0] * grad_left + shares[which][1] * grad_right
            place = GATE_GRAD + 2 * which
            table_ref[:, place : place + 1] = shares[which][0] * (grad_left - mean)
            table_ref[:, place + 1 : place + 2] = shares[which][1] * (grad_right - mean)

    @pl.when(step >= token_steps)
    def _():
        tokens = normed_all.shape[0]
        slots = (step - token_steps) * slot_block + iota((slot_block, tokens), 0)
        first = jnp.where(slots == targets_ref[0:1, :], 1.0, 0.0)
        second = jnp.where(slots == targets_ref[1:2, :], 1.0, 0.0)
        rows_ref[...] = dot((first + second).astype(BF16), normed_all[...]).astype(BF16)
        grads_ref[...] = (
            dot(first.astype(BF16), first_all[...]) + dot(second.astype(BF16), second_all[...])
        ).astype(BF16)


def route_tokens(
    hidden, attended, upstream, extra, routes, targets, gain, gathered, experts, constant_count, slots
):
    tokens = hidden.shape[0]
    kinds = extra.shape[1]
    steps = tokens // BLOCK
    slot_block = slots // 4
    token_block = lambda width: pl.BlockSpec(
        (BLOCK, width), lambda step: (jnp.minimum(step, steps - 1), 0)
    )
    slot_rows = pl.BlockSpec((slot_block, D), lambda step: (jnp.maximum(step - steps, 0), 0))
    kernel = functools.partial(
        route_kernel,
        token_steps=steps,
        experts=experts,
        constant_count=constant_count,
        slot_block=slot_block,
    )
    return pl.pallas_call(
        kernel,
        grid=(steps + 4,),
        in_specs=[
            token_block(D),
            token_block(D),
            token_block(D),
            token_block(kinds),
            token_block(2),
            whole((2, tokens)),
            whole((1, D)),
            pl.BlockSpec((D, D), lambda step: (0, 3)),
            pl.BlockSpec((D, LANES), lambda step: (0, 4 * D // LANES)),
        ],
        out_specs=[
            token_block(D),
            token_block(D),
            token_block(LANES),
            slot_rows,
            slot_rows,
        ],
        out_shape=[
            jax.ShapeDtypeStruct((tokens, D), F32),
            jax.ShapeDtypeStruct((tokens, D), BF16),
            jax.ShapeDtypeStruct((tokens, LANES), F32),
            jax.ShapeDtypeStruct((slots, D), BF16),
            jax.ShapeDtypeStruct((slots, D), BF16),
        ],
        scratch_shapes=[pltpu.VMEM((tokens, D), BF16)] * 3,
        compiler_params=params(40),
        cost_estimate=cost(2 * tokens * D * (D + 3 * slots), 20 * tokens * D),
        name="route_tokens",
    )(hidden, attended, upstream, extra, routes, targets, gain, gathered, gathered)


def expert_kernel(
    rows_ref, grads_ref, gate_ref, up_ref, outer_ref, active_ref, grad_gate_ref, grad_up_ref, produced_ref, total
):
    step = pl.program_id(0)
    gate = dot(rows_ref[...], gate_ref[...])
    up = dot(rows_ref[...], up_ref[...])
    sigmoid = 1.0 / (1.0 + jnp.exp(-gate))
    silu = gate * sigmoid
    active = (silu * up).astype(BF16)
    active_ref[...] = active
    part = dot(active, outer_ref[...])
    total[...] = jnp.where(step == 0, part, total[...] + part)
    grad_active = dot(grads_ref[...], outer_ref[...], NT)
    grad_gate_ref[...] = (grad_active * up * sigmoid * (1.0 + gate * (1.0 - sigmoid))).astype(BF16)
    grad_up_ref[...] = (grad_active * silu).astype(BF16)

    @pl.when(step == pl.num_programs(0) - 1)
    def _():
        produced_ref[...] = total[...].astype(BF16)


def expert_forward(rows, grads, inner, outer):
    count = rows.shape[0]
    steps = FF // BLOCK
    hidden_block = pl.BlockSpec((count, BLOCK), lambda step: (0, step))
    return pl.pallas_call(
        expert_kernel,
        grid=(steps,),
        in_specs=[
            whole((count, D)),
            whole((count, D)),
            pl.BlockSpec((D, BLOCK), lambda step: (0, step)),
            pl.BlockSpec((D, BLOCK), lambda step: (0, steps + step)),
            pl.BlockSpec((BLOCK, D), lambda step: (step, 0)),
        ],
        out_specs=[hidden_block, hidden_block, hidden_block, whole((count, D))],
        out_shape=[jax.ShapeDtypeStruct((count, FF), BF16)] * 3
        + [jax.ShapeDtypeStruct((count, D), BF16)],
        scratch_shapes=[pltpu.VMEM((count, D), F32)],
        compiler_params=params(48),
        cost_estimate=cost(8 * count * D * FF, 6 * count * FF + 6 * D * FF, count * FF),
        name="expert_forward",
    )(rows, grads, inner, inner, outer)


def mix_kernel(
    returned_ref,
    targets_ref,
    routes_ref,
    table_ref,
    middle_ref,
    normed_ref,
    upstream_ref,
    small_ref,
    out_ref,
    grads_ref,
    logits_ref,
    work,
    *,
    kinds,
    constant_count,
):
    block = middle_ref.shape[0]
    slots = returned_ref.shape[0]
    wide = upstream_ref[...].astype(F32)
    table = table_ref[...]
    probs = table[:, PROBS : PROBS + kinds]
    places = iota((block, kinds), 1)
    columns = iota((block, slots), 1)
    blended = normed_ref[...].astype(F32) * table[:, COEF : COEF + 1]
    grad_probs = jnp.zeros((block, kinds), F32)
    for route in range(2):
        hot = jnp.where(columns == targets_ref[:, route : route + 1], 1.0, 0.0).astype(BF16)
        paired = dot(hot, returned_ref[...])
        blended = blended + table[:, CHOSEN + route : CHOSEN + route + 1] * paired
        grad_chosen = (
            jnp.sum(wide * paired, axis=1, keepdims=True) + table[:, REST + route : REST + route + 1]
        )
        grad_probs = grad_probs + jnp.where(
            places == routes_ref[:, route : route + 1], grad_chosen, 0.0
        )
    grad_logits = probs * (grad_probs - jnp.sum(probs * grad_probs, axis=1, keepdims=True))
    logits_ref[...] = grad_logits
    gates = 2 * constant_count
    work[...] = jnp.zeros_like(work)
    work[:, :kinds] = grad_logits
    work[:, kinds : kinds + gates] = table[:, GATE_GRAD : GATE_GRAD + gates]
    work[:, kinds + gates : kinds + gates + constant_count] = table[:, BETA : BETA + constant_count]
    values = work[...]
    upper = values.astype(BF16)
    lower = (values - upper.astype(F32)).astype(BF16)
    grads_ref[:, :LANES] = upper
    grads_ref[:, LANES:] = lower
    is_value = iota((block, LANES), 1) >= kinds + gates
    nothing = jnp.zeros((block, LANES), BF16)
    blended = blended + (
        dot(jnp.where(is_value, upper, nothing), small_ref[...], NT)
        + dot(jnp.where(is_value, lower, nothing), small_ref[...], NT)
    )
    out_ref[...] = (middle_ref[...] + blended).astype(BF16)


def mix_branches(
    returned, targets, routes, table, middle, normed, upstream, gathered, kinds, constant_count
):
    tokens = middle.shape[0]
    slots = returned.shape[0]
    token_block = lambda width: pl.BlockSpec((BLOCK, width), lambda step: (step, 0))
    return pl.pallas_call(
        functools.partial(mix_kernel, kinds=kinds, constant_count=constant_count),
        grid=(tokens // BLOCK,),
        in_specs=[
            whole((slots, D)),
            token_block(2),
            token_block(2),
            token_block(LANES),
            token_block(D),
            token_block(D),
            token_block(D),
            pl.BlockSpec((D, LANES), lambda step: (0, 4 * D // LANES)),
        ],
        out_specs=[token_block(D), token_block(2 * LANES), token_block(kinds)],
        out_shape=[
            jax.ShapeDtypeStruct((tokens, D), BF16),
            jax.ShapeDtypeStruct((tokens, 2 * LANES), BF16),
            jax.ShapeDtypeStruct((tokens, kinds), F32),
        ],
        scratch_shapes=[pltpu.VMEM((BLOCK, LANES), F32)],
        compiler_params=params(40),
        cost_estimate=cost(4 * tokens * D * slots, 14 * tokens * D),
        name="mix_branches",
    )(returned, targets, routes, table, middle, normed, upstream, gathered)


def middle_kernel(
    returned_ref,
    targets_ref,
    table_ref,
    grads_ref,
    middle_ref,
    upstream_ref,
    small_ref,
    gain_ref,
    weight_ref,
    grad_middle_ref,
    rounded_ref,
    attended_ref,
    grad_gain_ref,
    *,
    gate_end,
):
    block = middle_ref.shape[0]
    slots = returned_ref.shape[0]
    columns = iota((block, slots), 1)
    hot = jnp.where(columns == targets_ref[:, 0:1], 1.0, 0.0) + jnp.where(
        columns == targets_ref[:, 1:2], 1.0, 0.0
    )
    total = dot(hot.astype(BF16), returned_ref[...])
    wide = upstream_ref[...].astype(F32)
    total = total + wide * table_ref[:, COEF : COEF + 1]
    is_small = iota((block, LANES), 1) < gate_end
    nothing = jnp.zeros((block, LANES), BF16)
    total = total + (
        dot(jnp.where(is_small, grads_ref[:, :LANES], nothing), small_ref[...], NT)
        + dot(jnp.where(is_small, grads_ref[:, LANES:], nothing), small_ref[...], NT)
    )
    scale = table_ref[:, SCALE : SCALE + 1]
    unit = middle_ref[...] * scale
    part = jnp.sum(total * unit, axis=0, keepdims=True)
    grad_gain_ref[...] = jnp.where(pl.program_id(0) == 0, part, grad_gain_ref[...] + part)
    inner = total * gain_ref[...]
    grad_middle = wide + scale * (inner - unit * jnp.mean(inner * unit, axis=1, keepdims=True))
    grad_middle_ref[...] = grad_middle
    rounded = grad_middle.astype(BF16)
    rounded_ref[...] = rounded
    attended_ref[...] = dot(rounded, weight_ref[...], NT).astype(BF16)


def middle_backward(returned, targets, table, grads, middle, upstream, gain, gathered, gate_end):
    tokens = middle.shape[0]
    slots = returned.shape[0]
    token_block = lambda width: pl.BlockSpec((BLOCK, width), lambda step: (step, 0))
    return pl.pallas_call(
        functools.partial(middle_kernel, gate_end=gate_end),
        grid=(tokens // BLOCK,),
        in_specs=[
            whole((slots, D)),
            token_block(2),
            token_block(LANES),
            token_block(2 * LANES),
            token_block(D),
            token_block(D),
            pl.BlockSpec((D, LANES), lambda step: (0, 4 * D // LANES)),
            whole((1, D)),
            pl.BlockSpec((D, D), lambda step: (0, 3)),
        ],
        out_specs=[token_block(D), token_block(D), token_block(D), whole((1, D))],
        out_shape=[
            jax.ShapeDtypeStruct((tokens, D), F32),
            jax.ShapeDtypeStruct((tokens, D), BF16),
            jax.ShapeDtypeStruct((tokens, D), BF16),
            jax.ShapeDtypeStruct((1, D), F32),
        ],
        compiler_params=params(40),
        cost_estimate=cost(2 * tokens * D * (slots + D), 18 * tokens * D),
        name="middle_backward",
    )(returned, targets, table, grads, middle, upstream, gathered, gain, gathered)


def input_kernel(packed_ref, weight_ref, hidden_ref, grad_middle_ref, gain_ref, out_ref, grad_gain_ref):
    total = dot(packed_ref[...], weight_ref[...], NT)
    values = hidden_ref[...].astype(F32)
    scale = row_scale(values)
    unit = values * scale
    part = jnp.sum(total * unit, axis=0, keepdims=True)
    grad_gain_ref[...] = jnp.where(pl.program_id(0) == 0, part, grad_gain_ref[...] + part)
    inner = total * gain_ref[...]
    out_ref[...] = grad_middle_ref[...] + scale * (
        inner - unit * jnp.mean(inner * unit, axis=1, keepdims=True)
    )


def input_backward(grad_packed, gathered, hidden, grad_middle, gain):
    tokens = hidden.shape[0]
    token_block = lambda width: pl.BlockSpec((BLOCK, width), lambda step: (step, 0))
    return pl.pallas_call(
        input_kernel,
        grid=(tokens // BLOCK,),
        in_specs=[
            token_block(3 * D),
            pl.BlockSpec((D, 3 * D), lambda step: (0, 0)),
            token_block(D),
            token_block(D),
            whole((1, D)),
        ],
        out_specs=[token_block(D), whole((1, D))],
        out_shape=[
            jax.ShapeDtypeStruct((tokens, D), F32),
            jax.ShapeDtypeStruct((1, D), F32),
        ],
        compiler_params=params(40),
        cost_estimate=cost(6 * tokens * D * D, 16 * tokens * D),
        name="input_backward",
    )(grad_packed, gathered, hidden, grad_middle, gain)


def pair_targets(routes, priority, experts, total_kinds, capacity):
    kind_ids = jnp.arange(total_kinds, dtype=jnp.int32)
    hot = [(routes[:, k : k + 1] == kind_ids[None, :]).astype(F32) for k in range(2)]
    earlier = (priority[None, :] < priority[:, None]).astype(BF16)
    before = dot(earlier, (hot[0] + hot[1]).astype(BF16))
    slots = jnp.stack([jnp.sum(before * one, axis=1) for one in hot], axis=1).astype(jnp.int32)
    kept_pairs = jnp.logical_and(routes < experts, slots < capacity)
    return jnp.where(kept_pairs, routes * capacity + slots, experts * capacity)


def exchange(blocks, axis):
    return lax.all_to_all(blocks, axis, split_axis=0, concat_axis=0, tiled=True)


def adam_step(master, first, second, grad, factor, step_rate):
    clipped = grad * factor
    first_new = beta_moment * first + (1.0 - beta_moment) * clipped
    second_new = beta_moment * second + (1.0 - beta_moment) * clipped * clipped
    correct = 1.0 - beta_moment**step_number
    update = (
        first_new / correct / (jnp.sqrt(second_new / correct) + adam_epsilon) + decay_rate * master
    )
    master_new = master - step_rate * update
    return (grad, master_new, first_new, second_new, master_new.astype(jnp.bfloat16))


def body(
    hidden_in,
    gate_prior,
    routes,
    priority,
    segments,
    cotangent,
    attend_in,
    first_attend_in,
    second_attend_in,
    attend_out,
    first_attend_out,
    second_attend_out,
    router,
    first_router,
    second_router,
    gate_mix,
    first_gate_mix,
    second_gate_mix,
    constants,
    first_constants,
    second_constants,
    norm_gains,
    first_norm_gains,
    second_norm_gains,
    expert_in,
    first_expert_in,
    second_expert_in,
    expert_out,
    first_expert_out,
    second_expert_out,
):
    groups = lax.axis_size("expert")
    devices = lax.axis_size("dp") * groups
    kinds = gate_prior.shape[1]
    constant_count = constants.shape[1] // 3
    experts = kinds - 2 - constant_count
    token_count = hidden_in.shape[0]
    width_top = routes.shape[1]
    capacity = max(2, width_top * token_count // kinds // 8 * 8)
    slots = experts * capacity
    small_width = kinds + 3 * constant_count
    gate_end = kinds + 2 * constant_count

    mine = jnp.concatenate(
        [
            attend_in,
            attend_out,
            router,
            constants,
            norm_gains.T,
            jnp.zeros((attend_in.shape[0], LANES - small_width - 2), F32),
        ],
        axis=1,
    ).astype(BF16)
    gathered = lax.all_gather(mine, BOTH, axis=0, tiled=True)
    expert_inner = lax.all_gather(expert_in.astype(BF16), "dp", axis=1, tiled=True)[0]
    expert_outer = lax.all_gather(expert_out.astype(BF16), "dp", axis=1, tiled=True)[0]
    gains = gathered[:, 4 * D + small_width : 4 * D + small_width + 2].astype(F32).T
    gain_first, gain_second = gains[0:1], gains[1:2]

    targets = pair_targets(routes, priority[0], experts, kinds, capacity)
    target_rows = targets.T
    extra = jnp.dot(gate_prior, gate_mix.astype(BF16).astype(F32), precision=highest)
    seg_row = segments
    seg_column = segments.reshape(token_count, 1)

    normed_first, packed = project(hidden_in, gain_first, gathered)
    attended, logsum = attend_forward(packed, seg_column, seg_row)
    logsum = jnp.transpose(logsum, (0, 2, 1))
    middle, normed_second, table, rows, row_grads = route_tokens(
        hidden_in,
        attended,
        cotangent,
        extra,
        routes,
        target_rows,
        gain_second,
        gathered,
        experts,
        constant_count,
        slots,
    )
    split = (groups, slots // groups, D)
    arrived = exchange(rows.reshape(split), "expert").reshape(slots, D)
    arrived_grad = exchange(row_grads.reshape(split), "expert").reshape(slots, D)
    active, grad_gate, grad_up, produced = expert_forward(
        arrived, arrived_grad, expert_inner, expert_outer
    )
    returned = exchange(produced.reshape(split), "expert").reshape(slots, D)
    grad_joined = jnp.concatenate([grad_gate, grad_up], axis=1)
    grad_rows = dot(grad_joined, expert_inner, NT).astype(BF16)
    grad_returned = exchange(grad_rows.reshape(split), "expert").reshape(slots, D)
    grad_outer = dot(active, arrived_grad, TN).astype(BF16)
    grad_inner = dot(arrived, grad_joined, TN).astype(BF16)
    grad_outer_own = lax.psum_scatter(grad_outer[None], "dp", scatter_dimension=1, tiled=True)
    grad_inner_own = lax.psum_scatter(grad_inner[None], "dp", scatter_dimension=1, tiled=True)

    activations, token_grads, grad_logits = mix_branches(
        returned,
        targets,
        routes,
        table,
        middle,
        normed_second,
        cotangent,
        gathered,
        kinds,
        constant_count,
    )
    grad_middle, rounded, grad_attended, grad_gain_second = middle_backward(
        grad_returned, targets, table, token_grads, middle, cotangent, gain_second, gathered, gate_end
    )
    from_normed = dot(normed_second, token_grads, TN)
    from_upstream = dot(cotangent, token_grads, TN)
    column = jnp.arange(LANES)[None, :]
    grad_small = jnp.where(
        column < gate_end,
        from_normed[:, :LANES] + from_normed[:, LANES:],
        from_upstream[:, :LANES] + from_upstream[:, LANES:],
    )
    grad_mixer = jnp.einsum("tk,tj->kj", gate_prior, grad_logits, precision=highest)
    grad_out_and_small = jnp.concatenate(
        [dot(attended, rounded, TN).astype(BF16), grad_small.astype(BF16)], axis=1
    )
    out_own = lax.psum_scatter(grad_out_and_small, BOTH, scatter_dimension=0, tiled=True).astype(F32)

    grad_packed = attend_backward(packed, grad_attended, logsum, seg_column, seg_row)
    grad_weight_in = dot(normed_first, grad_packed, TN).astype(BF16)
    in_own = lax.psum_scatter(grad_weight_in, BOTH, scatter_dimension=0, tiled=True).astype(F32)
    input_grad, grad_gain_first = input_backward(
        grad_packed, gathered, hidden_in, grad_middle, gain_first
    )

    width = norm_gains.shape[1]
    grad_gains = jnp.concatenate([grad_gain_first, grad_gain_second], axis=0)
    for_each = grad_gains.reshape(2, devices, width).transpose(1, 0, 2).reshape(devices, 2 * width)
    mixer_flat = jnp.broadcast_to(grad_mixer.reshape(1, kinds * kinds), (devices, kinds * kinds))
    few = jnp.concatenate([for_each, mixer_flat], axis=1)
    few = exchange(few[:, None, :], BOTH).sum(axis=(0, 1))
    gains_own = few[: 2 * width].reshape(2, width)
    mixer_total = few[2 * width :].reshape(kinds, kinds)

    dense_own = (
        in_own,
        out_own[:, :D],
        out_own[:, D : D + kinds],
        out_own[:, D + kinds : D + small_width],
        gains_own,
    )
    owned_grads = dense_own + (grad_inner_own.astype(F32), grad_outer_own.astype(F32))
    partial_square = sum((jnp.sum(member * member) for member in owned_grads))
    squares = exchange(jnp.broadcast_to(partial_square, (devices, 1, LANES)), BOTH)
    square_total = jnp.sum(squares[:, 0, 0])
    grad_norm = jnp.sqrt(square_total + jnp.sum(mixer_total * mixer_total))
    factor = clip_limit / jnp.maximum(grad_norm, clip_limit)
    results = (activations, input_grad, grad_norm)
    states = (
        (attend_in, first_attend_in, second_attend_in, owned_grads[0]),
        (attend_out, first_attend_out, second_attend_out, owned_grads[1]),
        (router, first_router, second_router, owned_grads[2]),
        (gate_mix, first_gate_mix, second_gate_mix, mixer_total),
        (constants, first_constants, second_constants, owned_grads[3]),
        (norm_gains, first_norm_gains, second_norm_gains, owned_grads[4]),
        (expert_in, first_expert_in, second_expert_in, owned_grads[5]),
        (expert_out, first_expert_out, second_expert_out, owned_grads[6]),
    )
    for state, rate in zip(states, learn_rates):
        results = results + adam_step(*state, factor, rate)
    return results


def solution(mesh):
    in_specs = (
        P(("dp", "expert"), None),
        P(("dp", "expert"), None),
        P(("dp", "expert"), None),
        P(("dp", "expert"), None),
        P(("dp", "expert"), None),
        P(("dp", "expert"), None),
        P(("dp", "expert"), None),
        P(("dp", "expert"), None),
        P(("dp", "expert"), None),
        P(("dp", "expert"), None),
        P(("dp", "expert"), None),
        P(("dp", "expert"), None),
        P(("dp", "expert"), None),
        P(("dp", "expert"), None),
        P(("dp", "expert"), None),
        P(),
        P(),
        P(),
        P(("dp", "expert"), None),
        P(("dp", "expert"), None),
        P(("dp", "expert"), None),
        P(None, ("dp", "expert")),
        P(None, ("dp", "expert")),
        P(None, ("dp", "expert")),
        P("expert", "dp", None),
        P("expert", "dp", None),
        P("expert", "dp", None),
        P("expert", "dp", None),
        P("expert", "dp", None),
        P("expert", "dp", None),
    )
    out_specs = (
        P(("dp", "expert"), None),
        P(("dp", "expert"), None),
        P(),
        P(("dp", "expert"), None),
        P(("dp", "expert"), None),
        P(("dp", "expert"), None),
        P(("dp", "expert"), None),
        P(("dp", "expert"), None),
        P(("dp", "expert"), None),
        P(("dp", "expert"), None),
        P(("dp", "expert"), None),
        P(("dp", "expert"), None),
        P(("dp", "expert"), None),
        P(("dp", "expert"), None),
        P(("dp", "expert"), None),
        P(("dp", "expert"), None),
        P(("dp", "expert"), None),
        P(("dp", "expert"), None),
        P(),
        P(),
        P(),
        P(),
        P(),
        P(("dp", "expert"), None),
        P(("dp", "expert"), None),
        P(("dp", "expert"), None),
        P(("dp", "expert"), None),
        P(("dp", "expert"), None),
        P(None, ("dp", "expert")),
        P(None, ("dp", "expert")),
        P(None, ("dp", "expert")),
        P(None, ("dp", "expert")),
        P(None, ("dp", "expert")),
        P("expert", "dp", None),
        P("expert", "dp", None),
        P("expert", "dp", None),
        P("expert", "dp", None),
        P("expert", "dp", None),
        P("expert", "dp", None),
        P("expert", "dp", None),
        P("expert", "dp", None),
        P("expert", "dp", None),
        P("expert", "dp", None),
    )
    return jax.shard_map(body, mesh=mesh, in_specs=in_specs, out_specs=out_specs, check_vma=False)
```

```python
import functools

import jax
import jax.numpy as jnp
from jax import lax
from jax.experimental import pallas as pl
from jax.experimental.pallas import tpu as pltpu
from jax.sharding import PartitionSpec as P

D = 768
FF = 2048
HEAD_DIM = 64
PAIR = 2 * HEAD_DIM
BLOCK = 256
LANES = 128
TOKENS = {'route': 512, 'mix': 512, 'middle': 512, 'input': 512}
BOTH = ("dp", "expert")

norm_epsilon = 1e-05
adam_epsilon = 1e-08
learn_rates = (0.01, 0.04, 0.01, 0.03, 0.01, 0.1, 0.01, 0.01)
decay_rate = 0.1
beta_moment = 0.5
step_number = 4.0
clip_limit = 1.0
score_scale = 0.125
masked_score = -1e30
highest = lax.Precision.HIGHEST
F32 = jnp.float32
BF16 = jnp.bfloat16

NN = (((1,), (0,)), ((), ()))
NT = (((1,), (1,)), ((), ()))
TN = (((0,), (0,)), ((), ()))

CHOSEN, COEF, SCALE, REST, BETA, GATE_GRAD, PROBS = 0, 2, 3, 4, 8, 16, 32


def dot(left, right, form=NN):
    return lax.dot_general(left, right, form, preferred_element_type=F32)


def iota(shape, dim):
    return lax.broadcasted_iota(jnp.int32, shape, dim)


def row_scale(values):
    return lax.rsqrt(jnp.mean(values * values, axis=-1, keepdims=True) + norm_epsilon)


def params():
    return pltpu.CompilerParams(vmem_limit_bytes=56 << 20)


def whole(shape):
    return pl.BlockSpec(shape, lambda *step: (0,) * len(shape))


def cost(flops, moved, transcendentals=0):
    return pl.CostEstimate(flops=flops, bytes_accessed=moved, transcendentals=transcendentals)


def project_kernel(hidden_ref, gain_ref, weight_ref, normed_ref, packed_ref):
    @pl.when(pl.program_id(0) == 0)
    def _():
        values = hidden_ref[...].astype(F32)
        normed_ref[...] = (values * row_scale(values) * gain_ref[...]).astype(BF16)

    packed_ref[...] = dot(normed_ref[...], weight_ref[...]).astype(BF16)


def project(hidden, gain, weights):
    tokens = hidden.shape[0]
    return pl.pallas_call(
        project_kernel,
        grid=(3,),
        in_specs=[
            whole((tokens, D)),
            whole((1, D)),
            pl.BlockSpec((D, D), lambda step: (0, step)),
        ],
        out_specs=[whole((tokens, D)), pl.BlockSpec((tokens, D), lambda step: (0, step))],
        out_shape=[
            jax.ShapeDtypeStruct((tokens, D), BF16),
            jax.ShapeDtypeStruct((tokens, 3 * D), BF16),
        ],
        compiler_params=params(),
        cost_estimate=cost(6 * tokens * D * D, 10 * tokens * D + 6 * D * D),
        name="project",
    )(hidden, gain, weights)


def fill_bias(seg_column_ref, seg_row_ref, bias_ref, block):
    length = bias_ref.shape[0]
    for low in range(0, length, block):
        high = low + block
        columns = low + iota((high, block), 1)
        allowed = jnp.logical_and(
            seg_column_ref[:high, :] == seg_row_ref[:, low:high], iota((high, block), 0) <= columns
        )
        bias_ref[:high, low:high] = jnp.where(allowed, 0.0, masked_score)


def attend_forward_kernel(
    query_ref, key_ref, value_ref, seg_column_ref, seg_row_ref, out_ref, logsum_ref, bias_ref
):
    length, block = query_ref.shape[0], BLOCK

    @pl.when(pl.program_id(0) == 0)
    def _():
        fill_bias(seg_column_ref, seg_row_ref, bias_ref, block)

    for low in range(0, length, block):
        high = low + block
        for head in range(2):
            lanes = slice(head * HEAD_DIM, (head + 1) * HEAD_DIM)
            queries = query_ref[low:high, lanes] * score_scale
            scores = dot(key_ref[:high, lanes], queries, NT) + bias_ref[:high, low:high]
            maximum = jnp.max(scores, axis=0, keepdims=True)
            powers = jnp.exp(scores - maximum)
            totals = jnp.sum(powers, axis=0, keepdims=True)
            weights = (powers * (1.0 / totals)).astype(BF16)
            out_ref[low:high, lanes] = dot(weights, value_ref[:high, lanes], TN).astype(BF16)
            logsum_ref[0, head : head + 1, low:high] = maximum + jnp.log(totals)


def attend_forward(packed, seg_column, seg_row):
    length = packed.shape[0]
    pairs = D // PAIR
    return pl.pallas_call(
        attend_forward_kernel,
        grid=(pairs,),
        in_specs=[
            pl.BlockSpec((length, PAIR), lambda pair: (0, pair)),
            pl.BlockSpec((length, PAIR), lambda pair: (0, pairs + pair)),
            pl.BlockSpec((length, PAIR), lambda pair: (0, 2 * pairs + pair)),
            whole((length, 1)),
            whole((1, length)),
        ],
        out_specs=[
            pl.BlockSpec((length, PAIR), lambda pair: (0, pair)),
            pl.BlockSpec((1, 2, length), lambda pair: (pair, 0, 0)),
        ],
        out_shape=[
            jax.ShapeDtypeStruct((length, D), BF16),
            jax.ShapeDtypeStruct((pairs, 2, length), F32),
        ],
        scratch_shapes=[pltpu.VMEM((length, length), F32)],
        compiler_params=params(),
        cost_estimate=cost(8 * length * length * D, 8 * length * D, length * length * 8),
        name="attend_forward",
    )(packed, packed, packed, seg_column, seg_row)


def attend_backward_kernel(
    query_ref,
    key_ref,
    value_ref,
    grad_ref,
    logsum_ref,
    seg_column_ref,
    seg_row_ref,
    out_ref,
    bias_ref,
    key_sum,
    value_sum,
):
    length, block = query_ref.shape[0], BLOCK

    @pl.when(pl.program_id(0) == 0)
    def _():
        fill_bias(seg_column_ref, seg_row_ref, bias_ref, block)

    for low in reversed(range(0, length, block)):
        high = low + block
        for head in range(2):
            lanes = slice(head * HEAD_DIM, (head + 1) * HEAD_DIM)
            queries = query_ref[low:high, lanes] * score_scale
            grads = grad_ref[low:high, lanes]
            keys = key_ref[:high, lanes]
            scores = dot(keys, queries, NT) + bias_ref[:high, low:high]
            weights = jnp.exp(scores - logsum_ref[0, head : head + 1, low:high])
            grad_weights = dot(value_ref[:high, lanes], grads, NT)
            grad_values = dot(weights.astype(BF16), grads)
            centred = jnp.sum(weights * grad_weights, axis=0, keepdims=True)
            grad_raw = (weights * (grad_weights - centred)).astype(BF16)
            grad_keys = dot(grad_raw, queries)
            if high == length:
                key_sum[:, lanes] = grad_keys
                value_sum[:, lanes] = grad_values
            else:
                key_sum[:high, lanes] += grad_keys
                value_sum[:high, lanes] += grad_values
            out_ref[0, low:high, lanes] = dot(keys * score_scale, grad_raw, TN).T.astype(BF16)
    out_ref[1] = key_sum[...].astype(BF16)
    out_ref[2] = value_sum[...].astype(BF16)


def attend_backward(packed, grad, logsum, seg_column, seg_row):
    length = packed.shape[0]
    pairs = D // PAIR
    return pl.pallas_call(
        attend_backward_kernel,
        grid=(pairs,),
        in_specs=[
            pl.BlockSpec((length, PAIR), lambda pair: (0, pair)),
            pl.BlockSpec((length, PAIR), lambda pair: (0, pairs + pair)),
            pl.BlockSpec((length, PAIR), lambda pair: (0, 2 * pairs + pair)),
            pl.BlockSpec((length, PAIR), lambda pair: (0, pair)),
            pl.BlockSpec((1, 2, length), lambda pair: (pair, 0, 0)),
            whole((length, 1)),
            whole((1, length)),
        ],
        out_specs=pl.BlockSpec((3, length, PAIR), lambda pair: (0, 0, pair)),
        out_shape=jax.ShapeDtypeStruct((3, length, D), BF16),
        scratch_shapes=[
            pltpu.VMEM((length, length), F32),
            pltpu.VMEM((length, PAIR), F32),
            pltpu.VMEM((length, PAIR), F32),
        ],
        compiler_params=params(),
        cost_estimate=cost(20 * length * length * D, 14 * length * D, length * length * 8),
        name="attend_backward",
    )(packed, packed, packed, grad, logsum, seg_column, seg_row)


def route_kernel(
    hidden_ref,
    attended_ref,
    upstream_ref,
    extra_ref,
    routes_ref,
    targets_ref,
    gain_ref,
    weight_ref,
    small_ref,
    middle_ref,
    normed_ref,
    table_ref,
    first_ref,
    second_ref,
    rows_ref,
    normed_all,
    work,
    *,
    token_steps,
    experts,
    constant_count,
    slot_block,
):
    step = pl.program_id(0)
    block = hidden_ref.shape[0]
    kinds = extra_ref.shape[0]
    gate_end = kinds + 2 * constant_count

    @pl.when(step < token_steps)
    def _():
        middle = hidden_ref[...].astype(F32) + dot(attended_ref[...], weight_ref[...])
        scale = row_scale(middle)
        normed = (middle * scale * gain_ref[...]).astype(BF16)
        middle_ref[...] = middle
        normed_ref[...] = normed
        upstream = upstream_ref[...]
        wide = upstream.astype(F32)
        inner = jnp.sum(wide * normed.astype(F32), axis=1, keepdims=True)
        lane = iota((block, LANES), 1)
        small = jnp.where(lane >= gate_end, dot(upstream, small_ref[...]), dot(normed, small_ref[...]))
        small = jnp.where(lane == LANES - 1, inner, jnp.where(lane == LANES - 2, scale, small)).T
        inner = small[LANES - 1 : LANES]
        logits = small[:kinds] + extra_ref[...]
        powers = jnp.exp(logits - jnp.max(logits, axis=0, keepdims=True))
        probs = powers / jnp.sum(powers, axis=0, keepdims=True)
        places = iota((kinds, block), 0)
        work[...] = jnp.zeros_like(work)
        work[PROBS : PROBS + kinds] = probs
        work[SCALE : SCALE + 1] = small[LANES - 2 : LANES - 1]
        shares = []
        for which in range(constant_count):
            left = small[kinds + 2 * which : kinds + 2 * which + 1]
            right = small[kinds + 2 * which + 1 : kinds + 2 * which + 2]
            top = jnp.maximum(left, right)
            left, right = jnp.exp(left - top), jnp.exp(right - top)
            both = left + right
            shares.append((left / both, right / both))
        met = [small[gate_end + which : gate_end + which + 1] for which in range(constant_count)]
        nothing = jnp.zeros((1, block), F32)
        coef = nothing
        betas = [nothing] * constant_count
        amounts = [nothing] * constant_count
        for route in range(2):
            kind = routes_ref[route : route + 1, :]
            chosen = jnp.sum(jnp.where(places == kind, probs, 0.0), axis=0, keepdims=True)
            work[CHOSEN + route : CHOSEN + route + 1] = chosen
            part = jnp.where(kind == experts + 1, 1.0, 0.0)
            rest = nothing
            for which in range(constant_count):
                here = kind == experts + 2 + which
                part = part + jnp.where(here, shares[which][0], 0.0)
                rest = rest + jnp.where(here, shares[which][1] * met[which], 0.0)
                betas[which] = betas[which] + jnp.where(here, chosen * shares[which][1], 0.0)
                amounts[which] = amounts[which] + jnp.where(here, chosen, 0.0)
            coef = coef + chosen * part
            work[REST + route : REST + route + 1] = chosen * (rest + part * inner)
        work[COEF : COEF + 1] = coef
        for which in range(constant_count):
            work[BETA + which : BETA + which + 1] = betas[which]
            grad_left = amounts[which] * inner
            grad_right = amounts[which] * met[which]
            mean = shares[which][0] * grad_left + shares[which][1] * grad_right
            place = GATE_GRAD + 2 * which
            work[place : place + 1] = shares[which][0] * (grad_left - mean)
            work[place + 1 : place + 2] = shares[which][1] * (grad_right - mean)
        table = work[...].T
        table_ref[...] = table
        rows = pl.ds(pl.multiple_of(step * block, block), block)
        normed_all[rows, :] = normed
        first_ref[...] = (table[:, CHOSEN : CHOSEN + 1] * wide).astype(BF16)
        second_ref[...] = (table[:, CHOSEN + 1 : CHOSEN + 2] * wide).astype(BF16)

    @pl.when(step >= token_steps)
    def _():
        tokens = normed_all.shape[0]
        slots = (step - token_steps) * slot_block + iota((slot_block, tokens), 0)
        hot = jnp.where(slots == targets_ref[0:1, :], 1.0, 0.0) + jnp.where(
            slots == targets_ref[1:2, :], 1.0, 0.0
        )
        rows_ref[...] = dot(hot.astype(BF16), normed_all[...]).astype(BF16)


def grad_rows_kernel(first_ref, second_ref, targets_ref, out_ref):
    slot_block, tokens = out_ref.shape[0], first_ref.shape[0]
    slots = pl.program_id(0) * slot_block + iota((slot_block, tokens), 0)
    first = jnp.where(slots == targets_ref[0:1, :], 1.0, 0.0).astype(BF16)
    second = jnp.where(slots == targets_ref[1:2, :], 1.0, 0.0).astype(BF16)
    out_ref[...] = (dot(first, first_ref[...]) + dot(second, second_ref[...])).astype(BF16)


def place_grads(first, second, targets, slots):
    tokens = first.shape[0]
    return pl.pallas_call(
        grad_rows_kernel,
        grid=(4,),
        in_specs=[whole((tokens, D)), whole((tokens, D)), whole((2, tokens))],
        out_specs=pl.BlockSpec((slots // 4, D), lambda step: (step, 0)),
        out_shape=jax.ShapeDtypeStruct((slots, D), BF16),
        compiler_params=params(),
        cost_estimate=cost(4 * tokens * D * slots, 6 * tokens * D),
        name="place_grads",
    )(first, second, targets)


def route_tokens(
    hidden, attended, upstream, extra, routes, targets, gain, gathered, experts, constant_count, slots
):
    tokens = hidden.shape[0]
    kinds = extra.shape[0]
    block = TOKENS['route']
    steps = tokens // block
    slot_block = slots // 4
    token_block = lambda width: pl.BlockSpec(
        (block, width), lambda step: (jnp.minimum(step, steps - 1), 0)
    )
    token_lanes = lambda height: pl.BlockSpec(
        (height, block), lambda step: (0, jnp.minimum(step, steps - 1))
    )
    slot_rows = pl.BlockSpec((slot_block, D), lambda step: (jnp.maximum(step - steps, 0), 0))
    kernel = functools.partial(
        route_kernel,
        token_steps=steps,
        experts=experts,
        constant_count=constant_count,
        slot_block=slot_block,
    )
    return pl.pallas_call(
        kernel,
        grid=(steps + 4,),
        in_specs=[
            token_block(D),
            token_block(D),
            token_block(D),
            token_lanes(kinds),
            token_lanes(2),
            whole((2, tokens)),
            whole((1, D)),
            pl.BlockSpec((D, D), lambda step: (0, 3)),
            pl.BlockSpec((D, LANES), lambda step: (0, 4 * D // LANES)),
        ],
        out_specs=[
            token_block(D),
            token_block(D),
            token_block(LANES),
            token_block(D),
            token_block(D),
            slot_rows,
        ],
        out_shape=[
            jax.ShapeDtypeStruct((tokens, D), F32),
            jax.ShapeDtypeStruct((tokens, D), BF16),
            jax.ShapeDtypeStruct((tokens, LANES), F32),
            jax.ShapeDtypeStruct((tokens, D), BF16),
            jax.ShapeDtypeStruct((tokens, D), BF16),
            jax.ShapeDtypeStruct((slots, D), BF16),
        ],
        scratch_shapes=[pltpu.VMEM((tokens, D), BF16), pltpu.VMEM((LANES, block), F32)],
        compiler_params=params(),
        cost_estimate=cost(2 * tokens * D * (D + slots), 20 * tokens * D),
        name="route_tokens",
    )(hidden, attended, upstream, extra, routes, targets, gain, gathered, gathered)


def inner_spec(weights, pieces, column):
    if weights.ndim == 2:
        return pl.BlockSpec((D, pieces * BLOCK), lambda step: (0, column(step)))
    shards = weights.shape[0]
    return pl.BlockSpec((shards, pieces * D // shards, BLOCK), lambda step: (0, column(step), 0))


def read_inner(ref):
    if len(ref.shape) == 2:
        return ref[...]
    rows = D // ref.shape[0]
    pieces = [ref[:, low : low + rows, :].reshape(D, BLOCK) for low in range(0, ref.shape[1], rows)]
    return jnp.concatenate(pieces, axis=1)


def outer_specs(weights, pieces):
    if weights.ndim == 2:
        return [pl.BlockSpec((pieces * BLOCK, D), lambda step: (step, 0))]
    first = weights.shape[1] // BLOCK - D // BLOCK
    piece = lambda c: pl.BlockSpec((pieces, BLOCK, BLOCK), lambda step: (step, first + c, 0))
    return [piece(c) for c in range(D // BLOCK)]


def read_outer(refs):
    if len(refs) == 1:
        return refs[0][...]
    return jnp.concatenate([ref[...].reshape(-1, BLOCK) for ref in refs], axis=1)


def expert_kernel(rows_ref, grads_ref, gate_ref, up_ref, *refs, outers, merged):
    outer_refs, refs = refs[:outers], refs[outers:]
    joined_ref, produced_ref, met_ref = refs[:3]
    weights, (total, turned) = refs[3 : 4 if merged else 5], refs[4 if merged else 5 :][:2]
    step = pl.program_id(0)
    steps = pl.num_programs(0)

    @pl.when(step == 0)
    def _():
        turned[...] = rows_ref[...].T

    outer = read_outer(outer_refs)
    gate = dot(rows_ref[...], read_inner(gate_ref))
    up = dot(rows_ref[...], read_inner(up_ref))
    grad_active = dot(grads_ref[...], outer, NT)
    sigmoid = 1.0 / (1.0 + jnp.exp(-gate))
    silu = gate * sigmoid
    active = (silu * up).astype(BF16)
    slope = sigmoid * (1.0 + gate * (1.0 - sigmoid))
    joined = ((grad_active * up * slope).astype(BF16), (grad_active * silu).astype(BF16))
    joined_ref[0], joined_ref[1] = joined
    part = dot(active, outer)
    total[...] = jnp.where(step == 0, part, total[...] + part)
    width = part.shape[1]
    grad_inner = [dot(turned[...], one) for one in joined]
    grad_outer = dot(active, grads_ref[...], TN)
    width = grad_outer.shape[0]
    if merged:
        inner_stage, outer_stage, semaphores = refs[6:]
        shards, rows = inner_stage.shape[1], inner_stage.shape[2] // 2
        owners, low = outer_stage.shape[1], outer_stage.shape[2] // (D // BLOCK)
        slot = step % 2

        def copies(step, slot):
            lanes = pl.ds(pl.multiple_of(step * width, LANES), width)
            return (
                pltpu.make_async_copy(
                    inner_stage.at[slot], weights[0].at[:, 0 : 2 * rows, lanes], semaphores.at[0, slot]
                ),
                pltpu.make_async_copy(
                    outer_stage.at[slot],
                    weights[0].at[pl.ds(step * owners, owners), 2 * rows : 3 * rows, :],
                    semaphores.at[1, slot],
                ),
            )

        @pl.when(step >= 2)
        def _():
            for copy in copies(step - 2, slot):
                copy.wait()

        for half in range(2):
            block = grad_inner[half].reshape(shards, rows, width).astype(BF16)
            inner_stage[slot, :, half * rows : (half + 1) * rows, :] = block
        grad_outer = grad_outer.astype(BF16)
        groups = FF // BLOCK
        for owner in range(owners):
            for piece in range(D // BLOCK):
                for group in range(groups):
                    start = (owner * groups + group) * low
                    outer_stage[
                        slot,
                        owner,
                        piece * low : (piece + 1) * low,
                        group * BLOCK : (group + 1) * BLOCK,
                    ] = grad_outer[start : start + low, piece * BLOCK : (piece + 1) * BLOCK]
        for copy in copies(step, slot):
            copy.start()

        @pl.when(step == steps - 1)
        def _():
            for copy in copies(step - 1, 1 - slot) + copies(step, slot):
                copy.wait()
    else:
        shards = weights[0].shape[0]
        for half in range(2):
            weights[0][:, half] = grad_inner[half].reshape(shards, -1, width).astype(BF16)
        weights[1][...] = grad_outer.astype(BF16)

    @pl.when(step == steps - 1)
    def _():
        produced = total[...].astype(BF16)
        produced_ref[...] = produced
        met = grads_ref[...].astype(F32) * produced.astype(F32)
        met = sum(met[:, low : low + LANES] for low in range(0, D, LANES))
        met_ref[...] = jnp.sum(met.T, axis=0, keepdims=True)


def expert_forward(rows, grads, inner, outer, shards):
    count = rows.shape[0]
    pieces = 2
    width = pieces * BLOCK
    steps = FF // width
    outers = outer_specs(outer, pieces)
    share = D // shards
    merged = inner.ndim == 3
    out_specs = [
        pl.BlockSpec((2, count, width), lambda step: (0, 0, step)),
        whole((count, D)),
        whole((1, count)),
    ]
    out_shape = [
        jax.ShapeDtypeStruct((2, count, FF), BF16),
        jax.ShapeDtypeStruct((count, D), BF16),
        jax.ShapeDtypeStruct((1, count), F32),
    ]
    scratch = [pltpu.VMEM((count, D), F32), pltpu.VMEM((D, count), BF16)]
    if merged:
        out_specs += [pl.BlockSpec(memory_space=pl.ANY)]
        out_shape += [jax.ShapeDtypeStruct((shards, 3 * share, FF), BF16)]
        scratch += [
            pltpu.VMEM((2, shards, 2 * share, width), BF16),
            pltpu.VMEM((2, shards // steps, share, FF), BF16),
            pltpu.SemaphoreType.DMA((2, 2)),
        ]
    else:
        out_specs += [
            pl.BlockSpec((shards, 2, share, width), lambda step: (0, 0, 0, step)),
            pl.BlockSpec((width, D), lambda step: (step, 0)),
        ]
        out_shape += [
            jax.ShapeDtypeStruct((shards, 2, share, FF), BF16),
            jax.ShapeDtypeStruct((FF, D), BF16),
        ]
    return pl.pallas_call(
        functools.partial(expert_kernel, outers=len(outers), merged=merged),
        grid=(steps,),
        in_specs=[
            whole((count, D)),
            whole((count, D)),
            inner_spec(inner, pieces, lambda step: step),
            inner_spec(inner, pieces, lambda step: steps + step),
            *outers,
        ],
        out_specs=out_specs,
        out_shape=out_shape,
        scratch_shapes=scratch,
        compiler_params=params(),
        cost_estimate=cost(14 * count * D * FF, 6 * count * FF + 10 * D * FF, count * FF),
        name="expert_forward",
    )(rows, grads, inner, inner, *[outer] * len(outers))


def scatter_experts(grads):
    sums = [lax.psum_scatter(grad, "dp", scatter_dimension=0, tiled=True) for grad in grads]
    if len(sums) == 1:
        return sums[0][0]
    inner, outer = sums[0][0], sums[1]
    groups = FF // BLOCK
    outer = outer.reshape(groups, -1, D // BLOCK, BLOCK).transpose(2, 1, 0, 3)
    return jnp.concatenate([inner.reshape(-1, FF), outer.reshape(-1, FF)], axis=0).astype(F32)


def expert_backward_kernel(joined_ref, inner_ref, grads_ref, total):
    step = pl.program_id(0)
    part = dot(joined_ref[0], read_inner(inner_ref), NT)
    total[...] = jnp.where(step == 0, part, total[...] + part)

    @pl.when(step == pl.num_programs(0) - 1)
    def _():
        grads_ref[...] = total[...].astype(BF16)


def expert_backward(joined, inner):
    count = joined.shape[1]
    pieces = 4
    width = pieces * BLOCK
    half = FF // width
    return pl.pallas_call(
        expert_backward_kernel,
        grid=(2 * half,),
        in_specs=[
            pl.BlockSpec((1, count, width), lambda step: (step // half, 0, step % half)),
            inner_spec(inner, pieces, lambda step: step),
        ],
        out_specs=whole((count, D)),
        out_shape=jax.ShapeDtypeStruct((count, D), BF16),
        scratch_shapes=[pltpu.VMEM((count, D), F32)],
        compiler_params=params(),
        cost_estimate=cost(4 * count * D * FF, 4 * count * FF + 4 * D * FF),
        name="expert_backward",
    )(joined, inner)


def mix_kernel(
    returned_ref,
    targets_ref,
    table_ref,
    middle_ref,
    normed_ref,
    small_ref,
    out_ref,
    *,
    value_place,
    constant_count,
):
    block = middle_ref.shape[0]
    slots = returned_ref.shape[0]
    table = table_ref[...]
    columns = iota((block, slots), 1)
    lane = iota((block, LANES), 1)
    blended = normed_ref[...].astype(F32) * table[:, COEF : COEF + 1]
    for route in range(2):
        hot = jnp.where(columns == targets_ref[:, route : route + 1], 1.0, 0.0).astype(BF16)
        paired = dot(hot, returned_ref[...])
        blended = blended + table[:, CHOSEN + route : CHOSEN + route + 1] * paired
    values = jnp.zeros((block, LANES), F32)
    for which in range(constant_count):
        place = BETA + which
        values = jnp.where(lane == value_place + which, table[:, place : place + 1], values)
    upper = values.astype(BF16)
    lower = (values - upper.astype(F32)).astype(BF16)
    blended = blended + (dot(upper, small_ref[...], NT) + dot(lower, small_ref[...], NT))
    out_ref[...] = (middle_ref[...] + blended).astype(BF16)


def mix_branches(returned, targets, table, middle, normed, gathered, value_place, constant_count):
    block = TOKENS["mix"]
    tokens = middle.shape[0]
    slots = returned.shape[0]
    token_block = lambda width: pl.BlockSpec((block, width), lambda step: (step, 0))
    return pl.pallas_call(
        functools.partial(mix_kernel, value_place=value_place, constant_count=constant_count),
        grid=(tokens // block,),
        in_specs=[
            whole((slots, D)),
            token_block(2),
            token_block(LANES),
            token_block(D),
            token_block(D),
            pl.BlockSpec((D, LANES), lambda step: (0, 4 * D // LANES)),
        ],
        out_specs=token_block(D),
        out_shape=jax.ShapeDtypeStruct((tokens, D), BF16),
        compiler_params=params(),
        cost_estimate=cost(4 * tokens * D * slots, 12 * tokens * D),
        name="mix_branches",
    )(returned, targets, table, middle, normed, gathered)


def middle_kernel(
    returned_ref,
    met_ref,
    targets_ref,
    routes_ref,
    prior_ref,
    table_ref,
    middle_ref,
    normed_ref,
    upstream_ref,
    attended_ref,
    small_ref,
    gain_ref,
    weight_ref,
    grad_middle_ref,
    grad_attended_ref,
    grad_weight_ref,
    mixer_ref,
    work,
    grad_gain,
    grad_small,
    grad_weight,
    *,
    experts,
    constant_count,
):
    block = middle_ref.shape[0]
    slots = returned_ref.shape[0]
    kinds = prior_ref.shape[0]
    gates = 2 * constant_count
    first = pl.program_id(0) == 0
    table = table_ref[...]
    wide = upstream_ref[...].astype(F32)
    columns = iota((block, slots), 1)
    hot = jnp.where(columns == targets_ref[:, 0:1], 1.0, 0.0) + jnp.where(
        columns == targets_ref[:, 1:2], 1.0, 0.0
    )
    hot = hot.astype(BF16)
    total = dot(hot, returned_ref[...]) + wide * table[:, COEF : COEF + 1]
    met = met_ref[...]
    upper = met.astype(BF16).astype(F32)
    here = iota((LANES, slots), 1) // (slots // experts) == iota((LANES, slots), 0) % experts
    halves = jnp.where(iota((LANES, slots), 0) < experts, upper, met - upper)
    met = jnp.where(jnp.logical_and(here, iota((LANES, slots), 0) < 2 * experts), halves, 0.0)
    met = dot(hot, met.astype(BF16), NT)
    met = met.T
    turned = table.T
    probs = turned[PROBS : PROBS + kinds]
    places = iota((kinds, block), 0)
    met = met[:experts] + met[experts : 2 * experts]
    work[...] = jnp.zeros_like(work)
    work[:experts] = met
    weighed = work[:kinds]
    for route in range(2):
        rest = turned[REST + route : REST + route + 1]
        weighed = weighed + jnp.where(places == routes_ref[route : route + 1, :], rest, 0.0)
    grad_logits = weighed - probs * jnp.sum(weighed, axis=0, keepdims=True)
    part = lax.dot_general(
        prior_ref[...], grad_logits, NT, precision=highest, preferred_element_type=F32
    )
    mixer_ref[...] = jnp.where(first, part, mixer_ref[...] + part)
    work[:kinds] = grad_logits
    work[kinds : kinds + gates] = turned[GATE_GRAD : GATE_GRAD + gates]
    work[kinds + gates : kinds + gates + constant_count] = turned[BETA : BETA + constant_count]
    values = work[...].T
    upper = values.astype(BF16)
    lower = (values - upper.astype(F32)).astype(BF16)
    is_small = iota((block, LANES), 1) < kinds + gates
    nothing = jnp.zeros((block, LANES), BF16)
    total = total + (
        dot(jnp.where(is_small, upper, nothing), small_ref[...], NT)
        + dot(jnp.where(is_small, lower, nothing), small_ref[...], NT)
    )
    both = jnp.concatenate([upper, lower], axis=1)
    part = jnp.where(
        iota((1, 2 * LANES), 1) % LANES < kinds + gates,
        dot(normed_ref[...], both, TN),
        dot(upstream_ref[...], both, TN),
    )
    part = part[:, :LANES] + part[:, LANES:]
    grad_small[...] = jnp.where(first, part, grad_small[...] + part)

    scale = table[:, SCALE : SCALE + 1]
    unit = middle_ref[...] * scale
    part = jnp.sum(total * unit, axis=0, keepdims=True)
    grad_gain[...] = jnp.where(first, part, grad_gain[...] + part)
    inner = total * gain_ref[...]
    grad_middle = wide + scale * (inner - unit * jnp.mean(inner * unit, axis=1, keepdims=True))
    grad_middle_ref[...] = grad_middle
    rounded = grad_middle.astype(BF16)
    grad_attended_ref[...] = dot(rounded, weight_ref[...], NT).astype(BF16)
    part = dot(attended_ref[...], rounded, TN)
    grad_weight[...] = jnp.where(first, part, grad_weight[...] + part)

    @pl.when(pl.program_id(0) == pl.num_programs(0) - 1)
    def _():
        grad_weight_ref[:, :D] = grad_weight[...].astype(BF16)
        column = jnp.broadcast_to(grad_gain[...], (LANES, D)).T
        place = kinds + gates + constant_count
        grad_weight_ref[:, D:] = jnp.where(
            iota((D, LANES), 1) == place, column, grad_small[...]
        ).astype(BF16)


def middle_backward(
    returned,
    met,
    targets,
    routes,
    prior,
    table,
    middle,
    normed,
    upstream,
    attended,
    gain,
    gathered,
    experts,
    constant_count,
):
    block = TOKENS["middle"]
    tokens = middle.shape[0]
    slots = returned.shape[0]
    kinds = prior.shape[0]
    token_block = lambda width: pl.BlockSpec((block, width), lambda step: (step, 0))
    token_lanes = lambda height: pl.BlockSpec((height, block), lambda step: (0, step))
    return pl.pallas_call(
        functools.partial(middle_kernel, experts=experts, constant_count=constant_count),
        grid=(tokens // block,),
        in_specs=[
            whole((slots, D)),
            whole((1, slots)),
            token_block(2),
            token_lanes(2),
            token_lanes(kinds),
            token_block(LANES),
            token_block(D),
            token_block(D),
            token_block(D),
            token_block(D),
            pl.BlockSpec((D, LANES), lambda step: (0, 4 * D // LANES)),
            whole((1, D)),
            pl.BlockSpec((D, D), lambda step: (0, 3)),
        ],
        out_specs=[token_block(D), token_block(D), whole((D, D + LANES)), whole((kinds, kinds))],
        out_shape=[
            jax.ShapeDtypeStruct((tokens, D), F32),
            jax.ShapeDtypeStruct((tokens, D), BF16),
            jax.ShapeDtypeStruct((D, D + LANES), BF16),
            jax.ShapeDtypeStruct((kinds, kinds), F32),
        ],
        scratch_shapes=[
            pltpu.VMEM((LANES, block), F32),
            pltpu.VMEM((1, D), F32),
            pltpu.VMEM((D, LANES), F32),
            pltpu.VMEM((D, D), F32),
        ],
        compiler_params=params(),
        cost_estimate=cost(2 * tokens * D * (slots + 2 * D), 18 * tokens * D),
        name="middle_backward",
    )(
        returned,
        met,
        targets,
        routes,
        prior,
        table,
        middle,
        normed,
        upstream,
        attended,
        gathered,
        gain,
        gathered,
    )


def project_backward_kernel(normed_ref, packed_ref, out_ref, turned):
    @pl.when(pl.program_id(0) == 0)
    def _():
        turned[...] = normed_ref[...].T

    out_ref[...] = dot(turned[...], packed_ref[0]).astype(BF16)


def project_backward(normed, grad_packed):
    tokens = normed.shape[0]
    return pl.pallas_call(
        project_backward_kernel,
        grid=(3,),
        in_specs=[whole((tokens, D)), pl.BlockSpec((1, tokens, D), lambda step: (step, 0, 0))],
        out_specs=pl.BlockSpec((D, D), lambda step: (0, step)),
        out_shape=jax.ShapeDtypeStruct((D, 3 * D), BF16),
        scratch_shapes=[pltpu.VMEM((D, tokens), BF16)],
        compiler_params=params(),
        cost_estimate=cost(6 * tokens * D * D, 8 * tokens * D + 6 * D * D),
        name="project_backward",
    )(normed, grad_packed)


def input_kernel(packed_ref, weight_ref, hidden_ref, grad_middle_ref, gain_ref, out_ref, grad_gain_ref):
    total = sum(dot(packed_ref[c], weight_ref[:, c * D : (c + 1) * D], NT) for c in range(3))
    values = hidden_ref[...].astype(F32)
    scale = row_scale(values)
    unit = values * scale
    part = jnp.sum(total * unit, axis=0, keepdims=True)
    grad_gain_ref[...] = jnp.where(pl.program_id(0) == 0, part, grad_gain_ref[...] + part)
    inner = total * gain_ref[...]
    out_ref[...] = grad_middle_ref[...] + scale * (
        inner - unit * jnp.mean(inner * unit, axis=1, keepdims=True)
    )


def input_backward(grad_packed, gathered, hidden, grad_middle, gain):
    block = TOKENS['input']
    tokens = hidden.shape[0]
    token_block = lambda width: pl.BlockSpec((block, width), lambda step: (step, 0))
    return pl.pallas_call(
        input_kernel,
        grid=(tokens // block,),
        in_specs=[
            pl.BlockSpec((3, block, D), lambda step: (0, step, 0)),
            pl.BlockSpec((D, 3 * D), lambda step: (0, 0)),
            token_block(D),
            token_block(D),
            whole((1, D)),
        ],
        out_specs=[token_block(D), whole((1, D))],
        out_shape=[
            jax.ShapeDtypeStruct((tokens, D), F32),
            jax.ShapeDtypeStruct((1, D), F32),
        ],
        compiler_params=params(),
        cost_estimate=cost(6 * tokens * D * D, 16 * tokens * D),
        name="input_backward",
    )(grad_packed, gathered, hidden, grad_middle, gain)


def pair_targets(routes, priority, experts, total_kinds, capacity):
    kind_ids = jnp.arange(total_kinds, dtype=jnp.int32)
    hot = [(routes[:, k : k + 1] == kind_ids[None, :]).astype(F32) for k in range(2)]
    earlier = (priority[None, :] < priority[:, None]).astype(BF16)
    before = dot(earlier, (hot[0] + hot[1]).astype(BF16))
    slots = jnp.stack([jnp.sum(before * one, axis=1) for one in hot], axis=1).astype(jnp.int32)
    kept_pairs = jnp.logical_and(routes < experts, slots < capacity)
    return jnp.where(kept_pairs, routes * capacity + slots, experts * capacity)


def exchange(blocks, axis):
    return lax.all_to_all(blocks, axis, split_axis=0, concat_axis=0, tiled=True)


def flip(axis):
    return [(i, i ^ 1) for i in range(lax.axis_size(axis))]


def shift(axis, step):
    count = lax.axis_size(axis)
    return [(i, (i + 2 * step) % count) for i in range(count)]


def gather_all(mine):
    rows, width = mine.shape
    far, wide = lax.axis_size("dp") // 2, lax.axis_size("expert") // 2
    depth, side = lax.axis_index("dp") // 2, lax.axis_index("dp") % 2
    place, core = lax.axis_index("expert") // 2, lax.axis_index("expert") % 2
    column = jnp.zeros((far, rows, width), mine.dtype)
    for step in range(far):
        came = mine if step == 0 else lax.ppermute(mine, "dp", shift("dp", step))
        column = lax.dynamic_update_slice(column, came[None], ((depth - step) % far, 0, 0))
    near = [column, lax.ppermute(column, "dp", flip("dp"))]
    total = jnp.zeros((far, 2, wide, 2, rows, width), mine.dtype)
    for step in range(wide):
        for other in range(2):
            piece = near[other]
            if step:
                piece = lax.ppermute(piece, "expert", shift("expert", step))
            twin = lax.ppermute(piece, "expert", flip("expert"))
            spot = (0, side ^ other, (place - step) % wide)
            shaped = (far, 1, 1, 1, rows, width)
            total = lax.dynamic_update_slice(total, piece.reshape(shaped), (*spot, core, 0, 0))
            total = lax.dynamic_update_slice(total, twin.reshape(shaped), (*spot, 1 - core, 0, 0))
    return total.reshape(-1, width)


def scatter_side(terms):
    width = terms.shape[1]
    count, wide = lax.axis_size("dp"), lax.axis_size("expert") // 2
    rows = terms.shape[0] // (2 * count * wide)
    place, core = lax.axis_index("expert") // 2, lax.axis_index("expert") % 2
    terms = terms.reshape(count, wide, 2, rows, width)
    pick = lambda array, index, axis: lax.dynamic_index_in_dim(array, index, axis, keepdims=False)
    came = lax.ppermute(pick(terms, 1 - core, 2), "expert", flip("expert"))
    pair = (pick(terms, core, 2).astype(F32) + came.astype(F32)).astype(BF16)
    total = pick(pair, place, 1).astype(F32)
    for step in range(1, wide):
        came = lax.ppermute(pick(pair, (place + step) % wide, 1), "expert", shift("expert", step))
        total = total + came.astype(F32)
    return total.astype(BF16)


def gather_experts(expert_in, expert_out):
    inner, outer = expert_in[0].astype(BF16), expert_out[0].astype(BF16)
    if inner.shape[0] % 16 or outer.shape[0] != BLOCK:
        return (
            lax.all_gather(inner, "dp", axis=0, tiled=True),
            lax.all_gather(outer, "dp", axis=0, tiled=True),
        )
    pieces = [
        array.reshape(array.shape[0], -1, BLOCK).transpose(1, 0, 2).reshape(-1, BLOCK)
        for array in (inner, outer)
    ]
    both = lax.all_gather(jnp.concatenate(pieces, axis=0), "dp", axis=0)
    return both, both


def own_kernel(shares_ref, expert_ref, out_ref, gain_ref, mixer_ref, own_ref, few_ref, *, kinds):
    total = jnp.sum(shares_ref[...].astype(F32), axis=0)
    own_ref[...] = total
    expert = expert_ref[...].astype(F32)
    width = few_ref.shape[1]
    square = jnp.sum(total * total, axis=(0, 1), keepdims=True)
    square = square + jnp.sum(expert * expert, axis=(0, 1), keepdims=True)
    square = square + jnp.sum(out_ref[...] * out_ref[...], axis=(0, 1), keepdims=True)
    few_ref[...] = jnp.zeros_like(few_ref)
    few_ref[0:1, :D] = gain_ref[...]
    for row in range(kinds):
        place = D + row * kinds
        few_ref[0:1, place : place + kinds] = mixer_ref[row : row + 1, :]
    few_ref[0:1, width - LANES :] = jnp.broadcast_to(square, (1, LANES))


def own_sums(shares, expert, out, grad_gain, grad_mixer):
    kinds = grad_mixer.shape[0]
    width = D + (-(-kinds * kinds // LANES) + 1) * LANES
    return pl.pallas_call(
        functools.partial(own_kernel, kinds=kinds),
        out_shape=[
            jax.ShapeDtypeStruct(shares.shape[1:], F32),
            jax.ShapeDtypeStruct((1, width), F32),
        ],
        compiler_params=params(),
        cost_estimate=cost(4 * shares.size + 4 * expert.size, 2 * shares.size + 2 * expert.size),
        name="own_sums",
    )(shares, expert, out, grad_gain, grad_mixer)


def adam(master, first, second, grad, factor, step_rate):
    clipped = grad * factor
    first_new = beta_moment * first + (1.0 - beta_moment) * clipped
    second_new = beta_moment * second + (1.0 - beta_moment) * clipped * clipped
    correct = 1.0 - beta_moment**step_number
    update = (
        first_new / correct / (jnp.sqrt(second_new / correct) + adam_epsilon) + decay_rate * master
    )
    return (master - step_rate * update, first_new, second_new)


def update_kernel(*refs, kinds, constant_count):
    index_ref, few_ref, in_ref, out_ref, inner_ref, outer_ref = refs[:6]
    states = [refs[6 + 3 * which : 9 + 3 * which] for which in range(8)]
    norm_ref, results = refs[30], refs[31:]
    width = out_ref.shape[1]
    few = jnp.sum(few_ref[...], axis=0)
    gain_total = few[:, :D]
    mixer_total = few[:, D : D + kinds * kinds]
    square = (
        few[:, few.shape[1] - 1 :]
        + jnp.sum(gain_total * gain_total, axis=1, keepdims=True)
        + jnp.sum(mixer_total * mixer_total, axis=1, keepdims=True)
    )
    norm = jnp.sqrt(square)
    factor = clip_limit / jnp.maximum(norm, clip_limit)
    places = iter(results)
    slots = [[next(places) for _ in range(4 if which == 0 else 5)] for which in range(8)]

    def step(which, grad):
        master, first, second = states[which]
        outs = slots[which]
        if len(outs) == 5:
            outs[0][...] = grad.reshape(outs[0].shape)
            outs = outs[1:]
        shape = outs[0].shape
        lay = lambda value: value.reshape(grad.shape)
        new = adam(lay(master[...]), lay(first[...]), lay(second[...]), grad, factor, learn_rates[which])
        for ref, value in zip(outs, new + (new[0],)):
            ref[...] = value.reshape(shape).astype(ref.dtype)

    step(6, inner_ref[...].astype(F32))
    folded = outer_ref[...].astype(F32)
    low = folded.shape[0] // (D // BLOCK)
    step(
        7,
        jnp.concatenate(
            [
                jnp.concatenate(
                    [folded[c * low : (c + 1) * low, g : g + BLOCK] for c in range(D // BLOCK)], axis=1
                )
                for g in range(0, folded.shape[1], BLOCK)
            ],
            axis=0,
        ),
    )

    @pl.when(pl.program_id(0) == 0)
    def _():
        norm_ref[...] = norm
        step(0, in_ref[...])
        step(1, out_ref[:, :D])
        rows = out_ref.shape[0]
        narrow = jnp.pad(out_ref[:, D:], ((0, LANES - rows), (0, 0))).T
        step(2, narrow[:kinds, :rows])
        step(3, jnp.concatenate([mixer_total[:, k * kinds : (k + 1) * kinds] for k in range(kinds)], axis=0))
        small = kinds + 3 * constant_count
        step(4, narrow[kinds:small, :rows])
        start = index_ref[0] * rows
        picked = (iota((D, LANES), 0) == start + iota((D, LANES), 1)).astype(F32)
        own = lax.dot_general(
            jnp.broadcast_to(gain_total, (8, D)), picked, NN, precision=highest, preferred_element_type=F32
        )
        step(5, jnp.concatenate([own[0:1, :rows], narrow[small : small + 1, :rows]], axis=0))


def update(index, few, in_own, out_own, expert_own, states, kinds, constant_count):
    steps = 4
    turn = lambda which, array: array.T if which in (2, 4) else array
    states = [[turn(which, array) for array in state] for which, state in enumerate(states)]
    share = expert_own.shape[0] // 3
    half = steps // 2
    flat = [array for state in states for array in state]

    def spec(shape):
        if len(shape) == 3 and shape[2] == 2 * FF:
            return pl.BlockSpec((1, shape[1], shape[2] // steps), lambda step, index: (0, 0, step))
        if len(shape) == 3:
            return pl.BlockSpec((1, shape[1] // steps, shape[2]), lambda step, index: (0, step, 0))
        return pl.BlockSpec(shape, lambda step, index: (0, 0))

    out_shape = [jax.ShapeDtypeStruct((1, 1), F32)]
    for which in range(8):
        shape = states[which][0].shape
        kept = 3 if which == 0 else 4
        out_shape += [jax.ShapeDtypeStruct(shape, F32)] * kept + [jax.ShapeDtypeStruct(shape, BF16)]
    results = pl.pallas_call(
        functools.partial(update_kernel, kinds=kinds, constant_count=constant_count),
        grid_spec=pltpu.PrefetchScalarGridSpec(
            num_scalar_prefetch=1,
            grid=(steps,),
            in_specs=[
                pl.BlockSpec(few.shape, lambda step, index: (0, 0, 0)),
                spec(in_own.shape),
                spec(out_own.shape),
                pl.BlockSpec((share, FF // half), lambda step, index: (step // half, step % half)),
                pl.BlockSpec((share, FF // steps), lambda step, index: (2, step)),
            ]
            + [spec(array.shape) for array in flat],
            out_specs=[spec(leaf.shape) for leaf in out_shape],
        ),
        out_shape=out_shape,
        compiler_params=params(),
        cost_estimate=cost(40 * D * FF, 60 * D * FF // 2),
        name="update",
    )(index, few, in_own, out_own, expert_own, expert_own, *flat)
    norm, rest = results[0].reshape(()), list(results[1:])
    ordered = [in_own]
    for which in range(8):
        taken = 4 if which == 0 else 5
        ordered += [turn(which, array) for array in rest[:taken]]
        rest = rest[taken:]
    return norm, ordered


def body(
    hidden_in,
    gate_prior,
    routes,
    priority,
    segments,
    cotangent,
    attend_in,
    first_attend_in,
    second_attend_in,
    attend_out,
    first_attend_out,
    second_attend_out,
    router,
    first_router,
    second_router,
    gate_mix,
    first_gate_mix,
    second_gate_mix,
    constants,
    first_constants,
    second_constants,
    norm_gains,
    first_norm_gains,
    second_norm_gains,
    expert_in,
    first_expert_in,
    second_expert_in,
    expert_out,
    first_expert_out,
    second_expert_out,
):
    groups = lax.axis_size("expert")
    devices = lax.axis_size("dp") * groups
    kinds = gate_prior.shape[1]
    constant_count = constants.shape[1] // 3
    experts = kinds - 2 - constant_count
    token_count = hidden_in.shape[0]
    width_top = routes.shape[1]
    capacity = max(2, width_top * token_count // kinds // 8 * 8)
    slots = experts * capacity
    small_width = kinds + 3 * constant_count
    gate_end = kinds + 2 * constant_count

    mine = jnp.concatenate(
        [
            attend_in,
            attend_out,
            router,
            constants,
            norm_gains.T,
            jnp.zeros((attend_in.shape[0], LANES - small_width - 2), F32),
        ],
        axis=1,
    ).astype(BF16)
    gathered = gather_all(mine)
    expert_inner, expert_outer = gather_experts(expert_in, expert_out)
    gains = gathered[:, 4 * D + small_width : 4 * D + small_width + 2].astype(F32).T
    gain_first, gain_second = gains[0:1], gains[1:2]

    targets = pair_targets(routes, priority[0], experts, kinds, capacity)
    target_rows = targets.T
    route_rows = routes.T
    prior_rows = gate_prior.T
    extra = jnp.dot(gate_mix.astype(BF16).astype(F32).T, prior_rows, precision=highest)
    seg_row = segments
    seg_column = segments.reshape(token_count, 1)

    normed_first, packed = project(hidden_in, gain_first, gathered)
    attended, logsum = attend_forward(packed, seg_column, seg_row)
    middle, normed_second, table, first_grads, second_grads, rows = route_tokens(
        hidden_in,
        attended,
        cotangent,
        extra,
        route_rows,
        target_rows,
        gain_second,
        gathered,
        experts,
        constant_count,
        slots,
    )
    split = (groups, slots // groups, D)
    arrived = exchange(rows.reshape(split), "expert").reshape(slots, D)
    row_grads = place_grads(first_grads, second_grads, target_rows, slots)
    arrived, row_grads = lax.optimization_barrier((arrived, row_grads))
    arrived_grad = exchange(row_grads.reshape(split), "expert").reshape(slots, D)
    grad_joined, produced, met, *grad_expert = expert_forward(
        arrived, arrived_grad, expert_inner, expert_outer, lax.axis_size("dp")
    )
    expert_own = scatter_experts(grad_expert)
    met = exchange(met.reshape(groups, 1, slots // groups), "expert").reshape(1, slots)
    grad_rows = expert_backward(grad_joined, expert_inner)
    met, grad_rows = lax.optimization_barrier((met, grad_rows))
    grad_returned = exchange(grad_rows.reshape(split), "expert").reshape(slots, D)
    grad_returned, produced = lax.optimization_barrier((grad_returned, produced))
    returned = exchange(produced.reshape(split), "expert").reshape(slots, D)
    grad_middle, grad_attended, grad_out_and_small, grad_mixer = middle_backward(
        grad_returned,
        met,
        targets,
        route_rows,
        prior_rows,
        table,
        middle,
        normed_second,
        cotangent,
        attended,
        gain_second,
        gathered,
        experts,
        constant_count,
    )
    out_shares = exchange(grad_out_and_small.reshape(devices, -1, D + LANES), BOTH)

    grad_packed = attend_backward(packed, grad_attended, logsum, seg_column, seg_row)
    grad_packed, returned = lax.optimization_barrier((grad_packed, returned))
    grad_weight_in = project_backward(normed_first, grad_packed)
    grad_weight_in, out_shares = lax.optimization_barrier((grad_weight_in, out_shares))
    in_sum = scatter_side(grad_weight_in)
    in_shares = exchange(in_sum, "dp")
    out_own = jnp.sum(out_shares.astype(F32), axis=0)
    input_grad, grad_gain_first = input_backward(
        grad_packed, gathered, hidden_in, grad_middle, gain_first
    )
    activations = mix_branches(
        returned, targets, table, middle, normed_second, gathered, gate_end, constant_count
    )

    in_own, few = own_sums(in_shares, expert_own, out_own, grad_gain_first, grad_mixer)
    few = exchange(jnp.broadcast_to(few[None], (devices, 1, few.shape[1])), BOTH)
    index = lax.axis_index("dp") * groups + lax.axis_index("expert")
    states = (
        (attend_in, first_attend_in, second_attend_in),
        (attend_out, first_attend_out, second_attend_out),
        (router, first_router, second_router),
        (gate_mix, first_gate_mix, second_gate_mix),
        (constants, first_constants, second_constants),
        (norm_gains, first_norm_gains, second_norm_gains),
        (expert_in, first_expert_in, second_expert_in),
        (expert_out, first_expert_out, second_expert_out),
    )
    grad_norm, updated = update(
        index.reshape(1).astype(jnp.int32),
        few,
        in_own,
        out_own,
        expert_own,
        states,
        kinds,
        constant_count,
    )
    return (activations, input_grad, grad_norm, *updated)


def solution(mesh):
    in_specs = (
        P(("dp", "expert"), None),
        P(("dp", "expert"), None),
        P(("dp", "expert"), None),
        P(("dp", "expert"), None),
        P(("dp", "expert"), None),
        P(("dp", "expert"), None),
        P(("dp", "expert"), None),
        P(("dp", "expert"), None),
        P(("dp", "expert"), None),
        P(("dp", "expert"), None),
        P(("dp", "expert"), None),
        P(("dp", "expert"), None),
        P(("dp", "expert"), None),
        P(("dp", "expert"), None),
        P(("dp", "expert"), None),
        P(),
        P(),
        P(),
        P(("dp", "expert"), None),
        P(("dp", "expert"), None),
        P(("dp", "expert"), None),
        P(None, ("dp", "expert")),
        P(None, ("dp", "expert")),
        P(None, ("dp", "expert")),
        P("expert", "dp", None),
        P("expert", "dp", None),
        P("expert", "dp", None),
        P("expert", "dp", None),
        P("expert", "dp", None),
        P("expert", "dp", None),
    )
    out_specs = (
        P(("dp", "expert"), None),
        P(("dp", "expert"), None),
        P(),
        P(("dp", "expert"), None),
        P(("dp", "expert"), None),
        P(("dp", "expert"), None),
        P(("dp", "expert"), None),
        P(("dp", "expert"), None),
        P(("dp", "expert"), None),
        P(("dp", "expert"), None),
        P(("dp", "expert"), None),
        P(("dp", "expert"), None),
        P(("dp", "expert"), None),
        P(("dp", "expert"), None),
        P(("dp", "expert"), None),
        P(("dp", "expert"), None),
        P(("dp", "expert"), None),
        P(("dp", "expert"), None),
        P(),
        P(),
        P(),
        P(),
        P(),
        P(("dp", "expert"), None),
        P(("dp", "expert"), None),
        P(("dp", "expert"), None),
        P(("dp", "expert"), None),
        P(("dp", "expert"), None),
        P(None, ("dp", "expert")),
        P(None, ("dp", "expert")),
        P(None, ("dp", "expert")),
        P(None, ("dp", "expert")),
        P(None, ("dp", "expert")),
        P("expert", "dp", None),
        P("expert", "dp", None),
        P("expert", "dp", None),
        P("expert", "dp", None),
        P("expert", "dp", None),
        P("expert", "dp", None),
        P("expert", "dp", None),
        P("expert", "dp", None),
        P("expert", "dp", None),
        P("expert", "dp", None),
    )
    return jax.shard_map(body, mesh=mesh, in_specs=in_specs, out_specs=out_specs, check_vma=False)
```

```python
import functools

import jax
import jax.numpy as jnp
from jax import lax
from jax.experimental import pallas as pl
from jax.experimental.pallas import tpu as pltpu
from jax.sharding import PartitionSpec as P

D = 768
FF = 2048
HEAD_DIM = 64
PAIR = 2 * HEAD_DIM
BLOCK = 256
LANES = 128
TOKENS = {'route': 512, 'mix': 512, 'middle': 512, 'input': 512}
BOTH = ("dp", "expert")

norm_epsilon = 1e-05
adam_epsilon = 1e-08
learn_rates = (0.01, 0.04, 0.01, 0.03, 0.01, 0.1, 0.01, 0.01)
decay_rate = 0.1
beta_moment = 0.5
step_number = 4.0
clip_limit = 1.0
score_scale = 0.125
masked_score = -1e30
highest = lax.Precision.HIGHEST
F32 = jnp.float32
BF16 = jnp.bfloat16

NN = (((1,), (0,)), ((), ()))
NT = (((1,), (1,)), ((), ()))
TN = (((0,), (0,)), ((), ()))

CHOSEN, COEF, SCALE, REST, BETA, GATE_GRAD, PROBS = 0, 2, 3, 4, 8, 16, 32
PIECES = 3
HINT = 64


def dot(left, right, form=NN):
    return lax.dot_general(left, right, form, preferred_element_type=F32)


def iota(shape, dim):
    return lax.broadcasted_iota(jnp.int32, shape, dim)


def row_scale(values):
    return lax.rsqrt(jnp.mean(values * values, axis=-1, keepdims=True) + norm_epsilon)


def params(mebibytes=56):
    return pltpu.CompilerParams(vmem_limit_bytes=mebibytes << 20)


def whole(shape):
    return pl.BlockSpec(shape, lambda *step: (0,) * len(shape))


def cost(flops, moved, transcendentals=0):
    share = HINT
    return pl.CostEstimate(
        flops=flops // share, bytes_accessed=moved // share, transcendentals=transcendentals // share
    )


def project_kernel(hidden_ref, gain_ref, weight_ref, normed_ref, packed_ref):
    @pl.when(pl.program_id(0) == 0)
    def _():
        values = hidden_ref[...].astype(F32)
        normed_ref[...] = (values * row_scale(values) * gain_ref[...]).astype(BF16)

    packed_ref[...] = dot(normed_ref[...], weight_ref[...]).astype(BF16)


def project(hidden, gain, weights):
    tokens = hidden.shape[0]
    return pl.pallas_call(
        project_kernel,
        grid=(3,),
        in_specs=[
            whole((tokens, D)),
            whole((1, D)),
            pl.BlockSpec((D, D), lambda step: (0, step)),
        ],
        out_specs=[whole((tokens, D)), pl.BlockSpec((tokens, D), lambda step: (0, step))],
        out_shape=[
            jax.ShapeDtypeStruct((tokens, D), BF16),
            jax.ShapeDtypeStruct((tokens, 3 * D), BF16),
        ],
        compiler_params=params(),
        cost_estimate=cost(6 * tokens * D * D, 10 * tokens * D + 6 * D * D),
        name="project",
    )(hidden, gain, weights)


def fill_bias(seg_column_ref, seg_row_ref, bias_ref, block):
    length = bias_ref.shape[0]
    for low in range(0, length, block):
        high = low + block
        columns = low + iota((high, block), 1)
        allowed = jnp.logical_and(
            seg_column_ref[:high, :] == seg_row_ref[:, low:high], iota((high, block), 0) <= columns
        )
        bias_ref[:high, low:high] = jnp.where(allowed, 0.0, masked_score)


def attend_forward_kernel(
    query_ref, key_ref, value_ref, seg_column_ref, seg_row_ref, out_ref, logsum_ref, bias_ref
):
    length, block = query_ref.shape[0], BLOCK

    @pl.when(pl.program_id(0) == 0)
    def _():
        fill_bias(seg_column_ref, seg_row_ref, bias_ref, block)

    for low in range(0, length, block):
        high = low + block
        for head in range(2):
            lanes = slice(head * HEAD_DIM, (head + 1) * HEAD_DIM)
            queries = query_ref[low:high, lanes] * score_scale
            scores = dot(key_ref[:high, lanes], queries, NT) + bias_ref[:high, low:high]
            maximum = jnp.max(scores, axis=0, keepdims=True)
            powers = jnp.exp(scores - maximum)
            totals = jnp.sum(powers, axis=0, keepdims=True)
            weights = (powers * (1.0 / totals)).astype(BF16)
            out_ref[low:high, lanes] = dot(weights, value_ref[:high, lanes], TN).astype(BF16)
            logsum_ref[0, head : head + 1, low:high] = maximum + jnp.log(totals)


def attend_forward(packed, seg_column, seg_row):
    length = packed.shape[0]
    pairs = D // PAIR
    return pl.pallas_call(
        attend_forward_kernel,
        grid=(pairs,),
        in_specs=[
            pl.BlockSpec((length, PAIR), lambda pair: (0, pair)),
            pl.BlockSpec((length, PAIR), lambda pair: (0, pairs + pair)),
            pl.BlockSpec((length, PAIR), lambda pair: (0, 2 * pairs + pair)),
            whole((length, 1)),
            whole((1, length)),
        ],
        out_specs=[
            pl.BlockSpec((length, PAIR), lambda pair: (0, pair)),
            pl.BlockSpec((1, 2, length), lambda pair: (pair, 0, 0)),
        ],
        out_shape=[
            jax.ShapeDtypeStruct((length, D), BF16),
            jax.ShapeDtypeStruct((pairs, 2, length), F32),
        ],
        scratch_shapes=[pltpu.VMEM((length, length), F32)],
        compiler_params=params(),
        cost_estimate=cost(8 * length * length * D, 8 * length * D, length * length * 8),
        name="attend_forward",
    )(packed, packed, packed, seg_column, seg_row)


def attend_backward_kernel(
    query_ref,
    key_ref,
    value_ref,
    grad_ref,
    logsum_ref,
    seg_column_ref,
    seg_row_ref,
    out_ref,
    bias_ref,
    key_sum,
    value_sum,
):
    length, block = query_ref.shape[0], BLOCK

    @pl.when(pl.program_id(0) == 0)
    def _():
        fill_bias(seg_column_ref, seg_row_ref, bias_ref, block)

    for low in reversed(range(0, length, block)):
        high = low + block
        for head in range(2):
            lanes = slice(head * HEAD_DIM, (head + 1) * HEAD_DIM)
            queries = query_ref[low:high, lanes] * score_scale
            grads = grad_ref[low:high, lanes]
            keys = key_ref[:high, lanes]
            scores = dot(keys, queries, NT) + bias_ref[:high, low:high]
            weights = jnp.exp(scores - logsum_ref[0, head : head + 1, low:high])
            grad_weights = dot(value_ref[:high, lanes], grads, NT)
            grad_values = dot(weights.astype(BF16), grads)
            centred = jnp.sum(weights * grad_weights, axis=0, keepdims=True)
            grad_raw = (weights * (grad_weights - centred)).astype(BF16)
            grad_keys = dot(grad_raw, queries)
            if high == length:
                key_sum[:, lanes] = grad_keys
                value_sum[:, lanes] = grad_values
            else:
                key_sum[:high, lanes] += grad_keys
                value_sum[:high, lanes] += grad_values
            out_ref[0, low:high, lanes] = dot(keys * score_scale, grad_raw, TN).T.astype(BF16)
    out_ref[1] = key_sum[...].astype(BF16)
    out_ref[2] = value_sum[...].astype(BF16)


def attend_backward(packed, grad, logsum, seg_column, seg_row):
    length = packed.shape[0]
    pairs = D // PAIR
    return pl.pallas_call(
        attend_backward_kernel,
        grid=(pairs,),
        in_specs=[
            pl.BlockSpec((length, PAIR), lambda pair: (0, pair)),
            pl.BlockSpec((length, PAIR), lambda pair: (0, pairs + pair)),
            pl.BlockSpec((length, PAIR), lambda pair: (0, 2 * pairs + pair)),
            pl.BlockSpec((length, PAIR), lambda pair: (0, pair)),
            pl.BlockSpec((1, 2, length), lambda pair: (pair, 0, 0)),
            whole((length, 1)),
            whole((1, length)),
        ],
        out_specs=pl.BlockSpec((3, length, PAIR), lambda pair: (0, 0, pair)),
        out_shape=jax.ShapeDtypeStruct((3, length, D), BF16),
        scratch_shapes=[
            pltpu.VMEM((length, length), F32),
            pltpu.VMEM((length, PAIR), F32),
            pltpu.VMEM((length, PAIR), F32),
        ],
        compiler_params=params(),
        cost_estimate=cost(20 * length * length * D, 14 * length * D, length * length * 8),
        name="attend_backward",
    )(packed, packed, packed, grad, logsum, seg_column, seg_row)


def route_kernel(
    hidden_ref,
    attended_ref,
    upstream_ref,
    extra_ref,
    routes_ref,
    targets_ref,
    gain_ref,
    weight_ref,
    small_ref,
    middle_ref,
    normed_ref,
    table_ref,
    rows_ref,
    normed_all,
    first_all,
    second_all,
    work,
    *,
    token_steps,
    experts,
    constant_count,
    slot_block,
):
    step = pl.program_id(0)
    block = hidden_ref.shape[0]
    kinds = extra_ref.shape[0]
    gate_end = kinds + 2 * constant_count

    @pl.when(step < token_steps)
    def _():
        middle = hidden_ref[...].astype(F32) + dot(attended_ref[...], weight_ref[...])
        scale = row_scale(middle)
        normed = (middle * scale * gain_ref[...]).astype(BF16)
        middle_ref[...] = middle
        normed_ref[...] = normed
        upstream = upstream_ref[...]
        wide = upstream.astype(F32)
        inner = jnp.sum(wide * normed.astype(F32), axis=1, keepdims=True)
        lane = iota((block, LANES), 1)
        small = jnp.where(lane >= gate_end, dot(upstream, small_ref[...]), dot(normed, small_ref[...]))
        small = jnp.where(lane == LANES - 1, inner, jnp.where(lane == LANES - 2, scale, small)).T
        inner = small[LANES - 1 : LANES]
        logits = small[:kinds] + extra_ref[...]
        powers = jnp.exp(logits - jnp.max(logits, axis=0, keepdims=True))
        probs = powers / jnp.sum(powers, axis=0, keepdims=True)
        places = iota((kinds, block), 0)
        work[...] = jnp.zeros_like(work)
        work[PROBS : PROBS + kinds] = probs
        work[SCALE : SCALE + 1] = small[LANES - 2 : LANES - 1]
        shares = []
        for which in range(constant_count):
            left = small[kinds + 2 * which : kinds + 2 * which + 1]
            right = small[kinds + 2 * which + 1 : kinds + 2 * which + 2]
            top = jnp.maximum(left, right)
            left, right = jnp.exp(left - top), jnp.exp(right - top)
            both = left + right
            shares.append((left / both, right / both))
        met = [small[gate_end + which : gate_end + which + 1] for which in range(constant_count)]
        nothing = jnp.zeros((1, block), F32)
        coef = nothing
        betas = [nothing] * constant_count
        amounts = [nothing] * constant_count
        for route in range(2):
            kind = routes_ref[route : route + 1, :]
            chosen = jnp.sum(jnp.where(places == kind, probs, 0.0), axis=0, keepdims=True)
            work[CHOSEN + route : CHOSEN + route + 1] = chosen
            part = jnp.where(kind == experts + 1, 1.0, 0.0)
            rest = nothing
            for which in range(constant_count):
                here = kind == experts + 2 + which
                part = part + jnp.where(here, shares[which][0], 0.0)
                rest = rest + jnp.where(here, shares[which][1] * met[which], 0.0)
                betas[which] = betas[which] + jnp.where(here, chosen * shares[which][1], 0.0)
                amounts[which] = amounts[which] + jnp.where(here, chosen, 0.0)
            coef = coef + chosen * part
            work[REST + route : REST + route + 1] = chosen * (rest + part * inner)
        work[COEF : COEF + 1] = coef
        for which in range(constant_count):
            work[BETA + which : BETA + which + 1] = betas[which]
            grad_left = amounts[which] * inner
            grad_right = amounts[which] * met[which]
            mean = shares[which][0] * grad_left + shares[which][1] * grad_right
            place = GATE_GRAD + 2 * which
            work[place : place + 1] = shares[which][0] * (grad_left - mean)
            work[place + 1 : place + 2] = shares[which][1] * (grad_right - mean)
        table = work[...].T
        table_ref[...] = table
        rows = pl.ds(pl.multiple_of(step * block, block), block)
        normed_all[rows, :] = normed
        for route, kept in enumerate((first_all, second_all)):
            rest = jnp.broadcast_to(table[:, CHOSEN + route : CHOSEN + route + 1], (block, LANES))
            pieces = jnp.zeros((block, LANES), F32)
            for piece in range(PIECES):
                upper = rest.astype(BF16).astype(F32)
                pieces = jnp.where(lane == piece, upper, pieces)
                rest = rest - upper
            kept[rows, :] = pieces.astype(BF16)

    @pl.when(step >= token_steps)
    def _():
        tokens = normed_all.shape[0]
        slots = (step - token_steps) * slot_block + iota((slot_block, tokens), 0)
        first = jnp.where(slots == targets_ref[0:1, :], 1.0, 0.0)
        second = jnp.where(slots == targets_ref[1:2, :], 1.0, 0.0)
        rows_ref[:, :D] = dot((first + second).astype(BF16), normed_all[...]).astype(BF16)
        rows_ref[:, D:] = (
            dot(first.astype(BF16), first_all[...]) + dot(second.astype(BF16), second_all[...])
        ).astype(BF16)


def place_kernel(rows_ref, targets_ref, out_ref):
    slot_block, tokens = out_ref.shape[0], rows_ref.shape[0]
    slots = pl.program_id(0) * slot_block + iota((slot_block, tokens), 0)
    hot = jnp.where(slots == targets_ref[0:1, :], 1.0, 0.0) + jnp.where(
        slots == targets_ref[1:2, :], 1.0, 0.0
    )
    out_ref[...] = dot(hot.astype(BF16), rows_ref[...]).astype(BF16)


def place_rows(rows, targets, slots):
    tokens = rows.shape[0]
    return pl.pallas_call(
        place_kernel,
        grid=(4,),
        in_specs=[whole((tokens, D)), whole((2, tokens))],
        out_specs=pl.BlockSpec((slots // 4, D), lambda step: (step, 0)),
        out_shape=jax.ShapeDtypeStruct((slots, D), BF16),
        compiler_params=params(),
        cost_estimate=cost(2 * tokens * D * slots, 4 * tokens * D),
        name="place_rows",
    )(rows, targets)


def route_tokens(
    hidden, attended, upstream, extra, routes, targets, gain, gathered, experts, constant_count, slots
):
    tokens = hidden.shape[0]
    kinds = extra.shape[0]
    block = TOKENS['route']
    steps = tokens // block
    slot_block = slots // 4
    token_block = lambda width: pl.BlockSpec(
        (block, width), lambda step: (jnp.minimum(step, steps - 1), 0)
    )
    token_lanes = lambda height: pl.BlockSpec(
        (height, block), lambda step: (0, jnp.minimum(step, steps - 1))
    )
    slot_rows = pl.BlockSpec((slot_block, D + LANES), lambda step: (jnp.maximum(step - steps, 0), 0))
    kernel = functools.partial(
        route_kernel,
        token_steps=steps,
        experts=experts,
        constant_count=constant_count,
        slot_block=slot_block,
    )
    return pl.pallas_call(
        kernel,
        grid=(steps + 4,),
        in_specs=[
            token_block(D),
            token_block(D),
            token_block(D),
            token_lanes(kinds),
            token_lanes(2),
            whole((2, tokens)),
            whole((1, D)),
            pl.BlockSpec((D, D), lambda step: (0, 3)),
            pl.BlockSpec((D, LANES), lambda step: (0, 4 * D // LANES)),
        ],
        out_specs=[
            token_block(D),
            token_block(D),
            token_block(LANES),
            slot_rows,
        ],
        out_shape=[
            jax.ShapeDtypeStruct((tokens, D), F32),
            jax.ShapeDtypeStruct((tokens, D), BF16),
            jax.ShapeDtypeStruct((tokens, LANES), F32),
            jax.ShapeDtypeStruct((slots, D + LANES), BF16),
        ],
        scratch_shapes=[
            pltpu.VMEM((tokens, D), BF16),
            pltpu.VMEM((tokens, LANES), BF16),
            pltpu.VMEM((tokens, LANES), BF16),
            pltpu.VMEM((LANES, block), F32),
        ],
        compiler_params=params(),
        cost_estimate=cost(2 * tokens * D * (D + slots), 20 * tokens * D),
        name="route_tokens",
    )(hidden, attended, upstream, extra, routes, targets, gain, gathered, gathered)


def inner_spec(weights, pieces, column):
    if weights.ndim == 2:
        return pl.BlockSpec((D, pieces * BLOCK), lambda step: (0, column(step)))
    shards = weights.shape[0]
    return pl.BlockSpec((shards, pieces * D // shards, BLOCK), lambda step: (0, column(step), 0))


def read_inner(ref):
    if len(ref.shape) == 2:
        return ref[...]
    shards = ref.shape[0]
    rows = D // shards
    pieces = [
        jnp.concatenate([ref[position(shards, k), low : low + rows, :] for k in range(shards)], axis=0)
        for low in range(0, ref.shape[1], rows)
    ]
    return jnp.concatenate(pieces, axis=1)


def outer_specs(weights, pieces):
    if weights.ndim == 2:
        return [pl.BlockSpec((pieces * BLOCK, D), lambda step: (step, 0))]
    shards = weights.shape[0]
    first = weights.shape[1] // BLOCK - D // BLOCK
    even = lambda c: pl.BlockSpec((1, BLOCK, BLOCK), lambda step: (step, first + c, 0))
    odd = lambda c: pl.BlockSpec((1, BLOCK, BLOCK), lambda step: (shards - 1 - step, first + c, 0))
    return [even(c) for c in range(D // BLOCK)] + [odd(c) for c in range(D // BLOCK)]


def read_outer(refs):
    if len(refs) == 1:
        return refs[0][...]
    half = len(refs) // 2
    return jnp.concatenate(
        [jnp.concatenate([ref[0] for ref in some], axis=1) for some in (refs[:half], refs[half:])], axis=0
    )


def expert_kernel(rows_ref, grads_ref, gate_ref, up_ref, *refs, outers):
    outer_refs, refs = refs[:outers], refs[outers:]
    joined_ref, active_ref, produced_ref, met_ref, weighed_ref, total = refs
    step = pl.program_id(0)

    @pl.when(step == 0)
    def _():
        chosen = jnp.sum(rows_ref[:, D:].astype(F32), axis=1, keepdims=True)
        weighed_ref[...] = (chosen * grads_ref[...].astype(F32)).astype(BF16)

    outer = read_outer(outer_refs)
    gates, ups = read_inner(gate_ref), read_inner(up_ref)
    parts = [slice(low, low + BLOCK) for low in range(0, outer.shape[0], BLOCK)]

    def enter(part):
        return (
            dot(rows_ref[:, :D], gates[:, part]),
            dot(rows_ref[:, :D], ups[:, part]),
            dot(weighed_ref[...], outer[part], NT),
        )

    part_total = 0.0
    entered = enter(parts[0])
    for index, part in enumerate(parts):
        gate, up, grad_active = entered
        if index + 1 < len(parts):
            entered = enter(parts[index + 1])
        sigmoid = 1.0 / (1.0 + jnp.exp(-gate))
        silu = gate * sigmoid
        active = (silu * up).astype(BF16)
        active_ref[:, part] = active
        slope = sigmoid * (1.0 + gate * (1.0 - sigmoid))
        joined_ref[0, :, part] = (grad_active * up * slope).astype(BF16)
        joined_ref[1, :, part] = (grad_active * silu).astype(BF16)
        part_total = part_total + dot(active, outer[part])
    total[...] = jnp.where(step == 0, part_total, total[...] + part_total)

    @pl.when(step == pl.num_programs(0) - 1)
    def _():
        produced = total[...].astype(BF16)
        produced_ref[...] = produced
        met = weighed_ref[...].astype(F32) * produced.astype(F32)
        met = sum(met[:, low : low + LANES] for low in range(0, D, LANES))
        met_ref[...] = jnp.sum(met.T, axis=0, keepdims=True)


def expert_forward(rows, grads, inner, outer):
    count = rows.shape[0]
    pieces = 2
    width = pieces * BLOCK
    steps = FF // width
    outers = outer_specs(outer, pieces)
    return pl.pallas_call(
        functools.partial(expert_kernel, outers=len(outers)),
        grid=(steps,),
        in_specs=[
            whole((count, D + LANES)),
            whole((count, D)),
            inner_spec(inner, pieces, lambda step: step),
            inner_spec(inner, pieces, lambda step: steps + step),
            *outers,
        ],
        out_specs=[
            pl.BlockSpec((2, count, width), lambda step: (0, 0, step)),
            pl.BlockSpec((count, width), lambda step: (0, step)),
            whole((count, D)),
            whole((1, count)),
            whole((count, D)),
        ],
        out_shape=[
            jax.ShapeDtypeStruct((2, count, FF), BF16),
            jax.ShapeDtypeStruct((count, FF), BF16),
            jax.ShapeDtypeStruct((count, D), BF16),
            jax.ShapeDtypeStruct((1, count), F32),
            jax.ShapeDtypeStruct((count, D), BF16),
        ],
        scratch_shapes=[pltpu.VMEM((count, D), F32)],
        compiler_params=params(),
        cost_estimate=cost(8 * count * D * FF, 6 * count * FF + 6 * D * FF, count * FF),
        name="expert_forward",
    )(rows, grads, inner, inner, *[outer] * len(outers))


def expert_weights_kernel(rows_ref, weighed_ref, joined_ref, active_ref, inner_ref, outer_ref, turned):
    @pl.when(pl.program_id(0) == 0)
    def _():
        turned[...] = rows_ref[:, :D].T

    shards, _, share, width = inner_ref.shape
    for half in range(2):
        grads = dot(turned[...], joined_ref[half]).astype(BF16)
        for k in range(shards):
            inner_ref[position(shards, k), half] = grads[k * share : (k + 1) * share]
    grads = dot(active_ref[...], weighed_ref[...], TN).astype(BF16)
    outer_ref[...] = grads.reshape(outer_ref.shape)


def expert_weights(rows, weighed, joined, active, shards):
    count = rows.shape[0]
    width = FF // shards
    share = D // shards
    place = lambda step: jnp.where(step < shards // 2, 2 * step, 2 * (shards - 1 - step) + 1)
    lanes = max(width, LANES)
    if lanes != width:
        place = lambda step: step
    steps = FF // lanes
    outer_block = (lanes // width, width, D)
    results = pl.pallas_call(
        expert_weights_kernel,
        grid=(steps,),
        in_specs=[
            whole((count, D + LANES)),
            whole((count, D)),
            pl.BlockSpec((2, count, lanes), lambda step: (0, 0, step)),
            pl.BlockSpec((count, lanes), lambda step: (0, place(step))),
        ],
        out_specs=[
            pl.BlockSpec((shards, 2, share, lanes), lambda step: (0, 0, 0, step)),
            pl.BlockSpec(outer_block, lambda step: (step, 0, 0)),
        ],
        out_shape=[
            jax.ShapeDtypeStruct((shards, 2, share, FF), BF16),
            jax.ShapeDtypeStruct((shards, width, D), BF16),
        ],
        scratch_shapes=[pltpu.VMEM((D, count), BF16)],
        compiler_params=params(),
        cost_estimate=cost(6 * count * D * FF, 6 * count * FF + 6 * D * FF),
        name="expert_weights",
    )(rows, weighed, joined, active)
    inner, outer = results
    if lanes != width:
        outer = jnp.concatenate([outer[k : k + 1] for k in around(shards)], axis=0)
    return inner, outer


def expert_backward_kernel(joined_ref, inner_ref, grads_ref, total):
    step = pl.program_id(0)
    part = dot(joined_ref[0], read_inner(inner_ref), NT)
    total[...] = jnp.where(step == 0, part, total[...] + part)

    @pl.when(step == pl.num_programs(0) - 1)
    def _():
        grads_ref[...] = total[...].astype(BF16)


def expert_backward(joined, inner):
    count = joined.shape[1]
    pieces = 4
    width = pieces * BLOCK
    half = FF // width
    return pl.pallas_call(
        expert_backward_kernel,
        grid=(2 * half,),
        in_specs=[
            pl.BlockSpec((1, count, width), lambda step: (step // half, 0, step % half)),
            inner_spec(inner, pieces, lambda step: step),
        ],
        out_specs=whole((count, D)),
        out_shape=jax.ShapeDtypeStruct((count, D), BF16),
        scratch_shapes=[pltpu.VMEM((count, D), F32)],
        compiler_params=params(),
        cost_estimate=cost(4 * count * D * FF, 4 * count * FF + 4 * D * FF),
        name="expert_backward",
    )(joined, inner)


def mix_kernel(
    returned_ref,
    targets_ref,
    table_ref,
    middle_ref,
    normed_ref,
    small_ref,
    out_ref,
    *,
    value_place,
    constant_count,
):
    block = middle_ref.shape[0]
    slots = returned_ref.shape[0]
    table = table_ref[...]
    columns = iota((block, slots), 1)
    lane = iota((block, LANES), 1)
    blended = normed_ref[...].astype(F32) * table[:, COEF : COEF + 1]
    for route in range(2):
        hot = jnp.where(columns == targets_ref[:, route : route + 1], 1.0, 0.0).astype(BF16)
        paired = dot(hot, returned_ref[...])
        blended = blended + table[:, CHOSEN + route : CHOSEN + route + 1] * paired
    values = jnp.zeros((block, LANES), F32)
    for which in range(constant_count):
        place = BETA + which
        values = jnp.where(lane == value_place + which, table[:, place : place + 1], values)
    upper = values.astype(BF16)
    lower = (values - upper.astype(F32)).astype(BF16)
    blended = blended + (dot(upper, small_ref[...], NT) + dot(lower, small_ref[...], NT))
    out_ref[...] = (middle_ref[...] + blended).astype(BF16)


def mix_branches(returned, targets, table, middle, normed, gathered, value_place, constant_count):
    block = TOKENS["mix"]
    tokens = middle.shape[0]
    slots = returned.shape[0]
    token_block = lambda width: pl.BlockSpec((block, width), lambda step: (step, 0))
    return pl.pallas_call(
        functools.partial(mix_kernel, value_place=value_place, constant_count=constant_count),
        grid=(tokens // block,),
        in_specs=[
            whole((slots, D)),
            token_block(2),
            token_block(LANES),
            token_block(D),
            token_block(D),
            pl.BlockSpec((D, LANES), lambda step: (0, 4 * D // LANES)),
        ],
        out_specs=token_block(D),
        out_shape=jax.ShapeDtypeStruct((tokens, D), BF16),
        compiler_params=params(),
        cost_estimate=cost(4 * tokens * D * slots, 12 * tokens * D),
        name="mix_branches",
    )(returned, targets, table, middle, normed, gathered)


def middle_kernel(
    returned_ref,
    met_ref,
    targets_ref,
    routes_ref,
    prior_ref,
    table_ref,
    middle_ref,
    normed_ref,
    upstream_ref,
    attended_ref,
    small_ref,
    gain_ref,
    weight_ref,
    grad_middle_ref,
    grad_attended_ref,
    grad_weight_ref,
    mixer_ref,
    work,
    grad_gain,
    grad_small,
    grad_weight,
    *,
    experts,
    constant_count,
):
    block = middle_ref.shape[0]
    slots = returned_ref.shape[0]
    kinds = prior_ref.shape[0]
    gates = 2 * constant_count
    first = pl.program_id(0) == 0
    table = table_ref[...]
    wide = upstream_ref[...].astype(F32)
    columns = iota((block, slots), 1)
    hot = jnp.where(columns == targets_ref[:, 0:1], 1.0, 0.0) + jnp.where(
        columns == targets_ref[:, 1:2], 1.0, 0.0
    )
    hot = hot.astype(BF16)
    total = dot(hot, returned_ref[...]) + wide * table[:, COEF : COEF + 1]
    met = met_ref[...]
    upper = met.astype(BF16).astype(F32)
    here = iota((LANES, slots), 1) // (slots // experts) == iota((LANES, slots), 0) % experts
    halves = jnp.where(iota((LANES, slots), 0) < experts, upper, met - upper)
    met = jnp.where(jnp.logical_and(here, iota((LANES, slots), 0) < 2 * experts), halves, 0.0)
    met = dot(hot, met.astype(BF16), NT)
    met = met.T
    turned = table.T
    probs = turned[PROBS : PROBS + kinds]
    places = iota((kinds, block), 0)
    met = met[:experts] + met[experts : 2 * experts]
    work[...] = jnp.zeros_like(work)
    work[:experts] = met
    weighed = work[:kinds]
    for route in range(2):
        rest = turned[REST + route : REST + route + 1]
        weighed = weighed + jnp.where(places == routes_ref[route : route + 1, :], rest, 0.0)
    grad_logits = weighed - probs * jnp.sum(weighed, axis=0, keepdims=True)
    part = lax.dot_general(
        prior_ref[...], grad_logits, NT, precision=highest, preferred_element_type=F32
    )
    mixer_ref[...] = jnp.where(first, part, mixer_ref[...] + part)
    work[:kinds] = grad_logits
    work[kinds : kinds + gates] = turned[GATE_GRAD : GATE_GRAD + gates]
    work[kinds + gates : kinds + gates + constant_count] = turned[BETA : BETA + constant_count]
    values = work[...].T
    upper = values.astype(BF16)
    lower = (values - upper.astype(F32)).astype(BF16)
    is_small = iota((block, LANES), 1) < kinds + gates
    nothing = jnp.zeros((block, LANES), BF16)
    total = total + (
        dot(jnp.where(is_small, upper, nothing), small_ref[...], NT)
        + dot(jnp.where(is_small, lower, nothing), small_ref[...], NT)
    )
    both = jnp.concatenate([upper, lower], axis=1)
    part = jnp.where(
        iota((1, 2 * LANES), 1) % LANES < kinds + gates,
        dot(normed_ref[...], both, TN),
        dot(upstream_ref[...], both, TN),
    )
    part = part[:, :LANES] + part[:, LANES:]
    grad_small[...] = jnp.where(first, part, grad_small[...] + part)

    scale = table[:, SCALE : SCALE + 1]
    unit = middle_ref[...] * scale
    part = jnp.sum(total * unit, axis=0, keepdims=True)
    grad_gain[...] = jnp.where(first, part, grad_gain[...] + part)
    inner = total * gain_ref[...]
    grad_middle = wide + scale * (inner - unit * jnp.mean(inner * unit, axis=1, keepdims=True))
    grad_middle_ref[...] = grad_middle
    rounded = grad_middle.astype(BF16)
    grad_attended_ref[...] = dot(rounded, weight_ref[...], NT).astype(BF16)
    part = dot(attended_ref[...], rounded, TN)
    grad_weight[...] = jnp.where(first, part, grad_weight[...] + part)

    @pl.when(pl.program_id(0) == pl.num_programs(0) - 1)
    def _():
        grad_weight_ref[:, :D] = grad_weight[...].astype(BF16)
        column = jnp.broadcast_to(grad_gain[...], (LANES, D)).T
        place = kinds + gates + constant_count
        grad_weight_ref[:, D:] = jnp.where(
            iota((D, LANES), 1) == place, column, grad_small[...]
        ).astype(BF16)


def middle_backward(
    returned,
    met,
    targets,
    routes,
    prior,
    table,
    middle,
    normed,
    upstream,
    attended,
    gain,
    gathered,
    experts,
    constant_count,
):
    block = TOKENS["middle"]
    tokens = middle.shape[0]
    slots = returned.shape[0]
    kinds = prior.shape[0]
    token_block = lambda width: pl.BlockSpec((block, width), lambda step: (step, 0))
    token_lanes = lambda height: pl.BlockSpec((height, block), lambda step: (0, step))
    return pl.pallas_call(
        functools.partial(middle_kernel, experts=experts, constant_count=constant_count),
        grid=(tokens // block,),
        in_specs=[
            whole((slots, D)),
            whole((1, slots)),
            token_block(2),
            token_lanes(2),
            token_lanes(kinds),
            token_block(LANES),
            token_block(D),
            token_block(D),
            token_block(D),
            token_block(D),
            pl.BlockSpec((D, LANES), lambda step: (0, 4 * D // LANES)),
            whole((1, D)),
            pl.BlockSpec((D, D), lambda step: (0, 3)),
        ],
        out_specs=[token_block(D), token_block(D), whole((D, D + LANES)), whole((kinds, kinds))],
        out_shape=[
            jax.ShapeDtypeStruct((tokens, D), F32),
            jax.ShapeDtypeStruct((tokens, D), BF16),
            jax.ShapeDtypeStruct((D, D + LANES), BF16),
            jax.ShapeDtypeStruct((kinds, kinds), F32),
        ],
        scratch_shapes=[
            pltpu.VMEM((LANES, block), F32),
            pltpu.VMEM((1, D), F32),
            pltpu.VMEM((D, LANES), F32),
            pltpu.VMEM((D, D), F32),
        ],
        compiler_params=params(),
        cost_estimate=cost(2 * tokens * D * (slots + 2 * D), 18 * tokens * D),
        name="middle_backward",
    )(
        returned,
        met,
        targets,
        routes,
        prior,
        table,
        middle,
        normed,
        upstream,
        attended,
        gathered,
        gain,
        gathered,
    )


def project_backward_kernel(normed_ref, packed_ref, out_ref, turned):
    @pl.when(pl.program_id(0) == 0)
    def _():
        turned[...] = normed_ref[...].T

    out_ref[...] = dot(turned[...], packed_ref[0]).astype(BF16)


def project_backward(normed, grad_packed):
    tokens = normed.shape[0]
    return pl.pallas_call(
        project_backward_kernel,
        grid=(3,),
        in_specs=[whole((tokens, D)), pl.BlockSpec((1, tokens, D), lambda step: (step, 0, 0))],
        out_specs=pl.BlockSpec((D, D), lambda step: (0, step)),
        out_shape=jax.ShapeDtypeStruct((D, 3 * D), BF16),
        scratch_shapes=[pltpu.VMEM((D, tokens), BF16)],
        compiler_params=params(),
        cost_estimate=cost(6 * tokens * D * D, 8 * tokens * D + 6 * D * D),
        name="project_backward",
    )(normed, grad_packed)


def input_kernel(packed_ref, weight_ref, hidden_ref, grad_middle_ref, gain_ref, out_ref, grad_gain_ref):
    total = sum(dot(packed_ref[c], weight_ref[:, c * D : (c + 1) * D], NT) for c in range(3))
    values = hidden_ref[...].astype(F32)
    scale = row_scale(values)
    unit = values * scale
    part = jnp.sum(total * unit, axis=0, keepdims=True)
    grad_gain_ref[...] = jnp.where(pl.program_id(0) == 0, part, grad_gain_ref[...] + part)
    inner = total * gain_ref[...]
    out_ref[...] = grad_middle_ref[...] + scale * (
        inner - unit * jnp.mean(inner * unit, axis=1, keepdims=True)
    )


def input_backward(grad_packed, gathered, hidden, grad_middle, gain):
    block = TOKENS['input']
    tokens = hidden.shape[0]
    token_block = lambda width: pl.BlockSpec((block, width), lambda step: (step, 0))
    return pl.pallas_call(
        input_kernel,
        grid=(tokens // block,),
        in_specs=[
            pl.BlockSpec((3, block, D), lambda step: (0, step, 0)),
            pl.BlockSpec((D, 3 * D), lambda step: (0, 0)),
            token_block(D),
            token_block(D),
            whole((1, D)),
        ],
        out_specs=[token_block(D), whole((1, D))],
        out_shape=[
            jax.ShapeDtypeStruct((tokens, D), F32),
            jax.ShapeDtypeStruct((1, D), F32),
        ],
        compiler_params=params(),
        cost_estimate=cost(6 * tokens * D * D, 16 * tokens * D),
        name="input_backward",
    )(grad_packed, gathered, hidden, grad_middle, gain)


def pair_targets(routes, priority, experts, total_kinds, capacity):
    kind_ids = jnp.arange(total_kinds, dtype=jnp.int32)
    hot = [(routes[:, k : k + 1] == kind_ids[None, :]).astype(F32) for k in range(2)]
    earlier = (priority[None, :] < priority[:, None]).astype(BF16)
    before = dot(earlier, (hot[0] + hot[1]).astype(BF16))
    slots = jnp.stack([jnp.sum(before * one, axis=1) for one in hot], axis=1).astype(jnp.int32)
    kept_pairs = jnp.logical_and(routes < experts, slots < capacity)
    return jnp.where(kept_pairs, routes * capacity + slots, experts * capacity)


def exchange(blocks, axis):
    return lax.all_to_all(blocks, axis, split_axis=0, concat_axis=0, tiled=True)


def flip(axis):
    return [(i, i ^ 1) for i in range(lax.axis_size(axis))]


def shift(axis, step):
    count = lax.axis_size(axis)
    return [(i, (i + 2 * step) % count) for i in range(count)]


def gather_far(mine):
    far, depth = lax.axis_size("dp") // 2, lax.axis_index("dp") // 2
    column = jnp.zeros((far, *mine.shape), mine.dtype)
    for step in range(far):
        came = mine if step == 0 else lax.ppermute(mine, "dp", shift("dp", step))
        column = lax.dynamic_update_slice(column, came[None], ((depth - step) % far, 0, 0))
    return column


def gather_all(column):
    far, rows, width = column.shape
    wide, side = lax.axis_size("expert") // 2, lax.axis_index("dp") % 2
    place, core = lax.axis_index("expert") // 2, lax.axis_index("expert") % 2
    near = [column, lax.ppermute(column, "dp", flip("dp"))]
    total = jnp.zeros((far, 2, wide, 2, rows, width), column.dtype)
    for step in range(wide):
        for other in range(2):
            piece = near[other]
            if step:
                piece = lax.ppermute(piece, "expert", shift("expert", step))
            twin = lax.ppermute(piece, "expert", flip("expert"))
            spot = (0, side ^ other, (place - step) % wide)
            shaped = (far, 1, 1, 1, rows, width)
            total = lax.dynamic_update_slice(total, piece.reshape(shaped), (*spot, core, 0, 0))
            total = lax.dynamic_update_slice(total, twin.reshape(shaped), (*spot, 1 - core, 0, 0))
    return total.reshape(-1, width)


def scatter_side(terms):
    width = terms.shape[1]
    count, wide = lax.axis_size("dp"), lax.axis_size("expert") // 2
    rows = terms.shape[0] // (2 * count * wide)
    place, core = lax.axis_index("expert") // 2, lax.axis_index("expert") % 2
    terms = terms.reshape(count, wide, 2, rows, width)
    pick = lambda array, index, axis: lax.dynamic_index_in_dim(array, index, axis, keepdims=False)
    came = lax.ppermute(pick(terms, 1 - core, 2), "expert", flip("expert"))
    pair = (pick(terms, core, 2).astype(F32) + came.astype(F32)).astype(BF16)
    total = pick(pair, place, 1).astype(F32)
    for step in range(1, wide):
        came = lax.ppermute(pick(pair, (place + step) % wide, 1), "expert", shift("expert", step))
        total = total + came.astype(F32)
    return total.astype(BF16)


def around(count):
    return list(range(0, count, 2)) + list(range(count - 1, 0, -2))


def position(count, place):
    return place // 2 if place % 2 == 0 else count - 1 - place // 2


def split_experts(expert_in, expert_out):
    inner, outer = expert_in[0].astype(BF16), expert_out[0].astype(BF16)
    if inner.shape[0] % 16 or outer.shape[0] != BLOCK:
        return [inner, outer]
    pieces = [
        array.reshape(array.shape[0], -1, BLOCK).transpose(1, 0, 2).reshape(-1, BLOCK)
        for array in (inner, outer)
    ]
    return [jnp.concatenate(pieces, axis=0)]


def gather_experts(pieces):
    ring = [around(lax.axis_size("dp"))]
    if len(pieces) == 1:
        both = lax.all_gather(pieces[0], "dp", axis=0, axis_index_groups=ring)
        return both, both
    return [lax.all_gather(piece, "dp", axis=0, tiled=True) for piece in pieces]


def scatter_expert(grads):
    ring = [around(lax.axis_size("dp"))]
    return lax.psum_scatter(grads, "dp", scatter_dimension=0, tiled=True, axis_index_groups=ring)[0]


def own_kernel(
    shares_ref, inner_ref, outer_ref, gain_ref, mixer_ref, own_ref, out_ref, own_outer_ref, few_ref, *, kinds
):
    total = jnp.sum(shares_ref[...].astype(F32), axis=0)
    own_ref[...] = total[:, : 3 * D]
    out_ref[...] = total[:, 3 * D :]
    inner, outer = inner_ref[...].astype(F32), outer_ref[...].astype(F32)
    own_outer_ref[...] = outer
    width = few_ref.shape[2]
    square = jnp.sum(jnp.sum(inner * inner, axis=0), axis=(0, 1), keepdims=True)
    for member in (total, outer):
        square = square + jnp.sum(member * member, axis=(0, 1), keepdims=True)
    few = few_ref.at[0]
    few[...] = jnp.zeros_like(few)
    few[0:1, :D] = gain_ref[...]
    for row in range(kinds):
        place = D + row * kinds
        few[0:1, place : place + kinds] = mixer_ref[row : row + 1, :]
    few[0:1, width - LANES :] = jnp.broadcast_to(square, (1, LANES))
    row = few[...]
    for device in range(1, few_ref.shape[0]):
        few_ref[device] = row


def own_sums(shares, inner, outer, grad_gain, grad_mixer, devices):
    kinds = grad_mixer.shape[0]
    width = D + (-(-kinds * kinds // LANES) + 1) * LANES
    rows = shares.shape[1]
    return pl.pallas_call(
        functools.partial(own_kernel, kinds=kinds),
        out_shape=[
            jax.ShapeDtypeStruct((rows, 3 * D), F32),
            jax.ShapeDtypeStruct((rows, D + LANES), F32),
            jax.ShapeDtypeStruct(outer.shape, F32),
            jax.ShapeDtypeStruct((devices, 1, width), F32),
        ],
        compiler_params=params(),
        cost_estimate=cost(6 * D * FF, 3 * D * FF),
        name="own_sums",
    )(shares, inner, outer, grad_gain, grad_mixer)


def adam(master, first, second, grad, factor, step_rate):
    clipped = grad * factor
    first_new = beta_moment * first + (1.0 - beta_moment) * clipped
    second_new = beta_moment * second + (1.0 - beta_moment) * clipped * clipped
    correct = 1.0 - beta_moment**step_number
    update = (
        first_new / correct / (jnp.sqrt(second_new / correct) + adam_epsilon) + decay_rate * master
    )
    return (master - step_rate * update, first_new, second_new)


def update_kernel(*refs, kinds, constant_count):
    index_ref, few_ref, in_ref, out_ref, inner_ref, outer_ref = refs[:6]
    states = [refs[6 + 3 * which : 9 + 3 * which] for which in range(8)]
    norm_ref, results = refs[30], refs[31:]
    width = out_ref.shape[1]
    few = jnp.sum(few_ref[...], axis=0)
    gain_total = few[:, :D]
    mixer_total = few[:, D : D + kinds * kinds]
    square = (
        few[:, few.shape[1] - 1 :]
        + jnp.sum(gain_total * gain_total, axis=1, keepdims=True)
        + jnp.sum(mixer_total * mixer_total, axis=1, keepdims=True)
    )
    norm = jnp.sqrt(square)
    factor = clip_limit / jnp.maximum(norm, clip_limit)
    places = iter(results)
    slots = [[next(places) for _ in range(4 if which in (0, 7) else 5)] for which in range(8)]

    def step(which, grad):
        master, first, second = states[which]
        outs = slots[which]
        if len(outs) == 5:
            outs[0][...] = grad.reshape(outs[0].shape)
            outs = outs[1:]
        shape = outs[0].shape
        lay = lambda value: value.reshape(grad.shape)
        new = adam(lay(master[...]), lay(first[...]), lay(second[...]), grad, factor, learn_rates[which])
        for ref, value in zip(outs, new + (new[0],)):
            ref[...] = value.reshape(shape).astype(ref.dtype)

    step(6, inner_ref[0].astype(F32))
    step(7, outer_ref[...])

    @pl.when(pl.program_id(0) == 0)
    def _():
        norm_ref[...] = norm
        step(0, in_ref[...])
        step(1, out_ref[:, :D])
        rows = out_ref.shape[0]
        narrow = jnp.pad(out_ref[:, D:], ((0, LANES - rows), (0, 0))).T
        step(2, narrow[:kinds, :rows])
        step(3, jnp.concatenate([mixer_total[:, k * kinds : (k + 1) * kinds] for k in range(kinds)], axis=0))
        small = kinds + 3 * constant_count
        step(4, narrow[kinds:small, :rows])
        start = index_ref[0] * rows
        picked = (iota((D, LANES), 0) == start + iota((D, LANES), 1)).astype(F32)
        own = lax.dot_general(
            jnp.broadcast_to(gain_total, (8, D)), picked, NN, precision=highest, preferred_element_type=F32
        )
        step(5, jnp.concatenate([own[0:1, :rows], narrow[small : small + 1, :rows]], axis=0))


def update(index, few, in_own, out_own, inner_own, outer_own, states, kinds, constant_count):
    steps = 4
    turn = lambda which, array: array.T if which in (2, 4) else array
    states = [[turn(which, array) for array in state] for which, state in enumerate(states)]
    half = steps // 2
    flat = [array for state in states for array in state]

    def spec(shape):
        if len(shape) == 3 and shape[2] == 2 * FF:
            return pl.BlockSpec((1, shape[1], shape[2] // steps), lambda step, index: (0, 0, step))
        if len(shape) == 3:
            return pl.BlockSpec((1, shape[1] // steps, shape[2]), lambda step, index: (0, step, 0))
        return pl.BlockSpec(shape, lambda step, index: (0, 0))

    out_shape = [jax.ShapeDtypeStruct((1, 1), F32)]
    for which in range(8):
        shape = states[which][0].shape
        kept = 3 if which in (0, 7) else 4
        out_shape += [jax.ShapeDtypeStruct(shape, F32)] * kept + [jax.ShapeDtypeStruct(shape, BF16)]
    results = pl.pallas_call(
        functools.partial(update_kernel, kinds=kinds, constant_count=constant_count),
        grid_spec=pltpu.PrefetchScalarGridSpec(
            num_scalar_prefetch=1,
            grid=(steps,),
            in_specs=[
                pl.BlockSpec(few.shape, lambda step, index: (0, 0, 0)),
                spec(in_own.shape),
                spec(out_own.shape),
                pl.BlockSpec(
                    (1, inner_own.shape[1], FF // half), lambda step, index: (step // half, 0, step % half)
                ),
                pl.BlockSpec((outer_own.shape[0] // steps, D), lambda step, index: (step, 0)),
            ]
            + [spec(array.shape) for array in flat],
            out_specs=[spec(leaf.shape) for leaf in out_shape],
        ),
        out_shape=out_shape,
        compiler_params=params(),
        cost_estimate=cost(40 * D * FF, 60 * D * FF // 2),
        name="update",
    )(index, few, in_own, out_own, inner_own, outer_own, *flat)
    norm, rest = results[0].reshape(()), list(results[1:])
    grads = {0: in_own, 7: outer_own[None]}
    ordered = []
    for which in range(8):
        taken = 4 if which in grads else 5
        ordered += [grads[which]] if which in grads else []
        ordered += [turn(which, array) for array in rest[:taken]]
        rest = rest[taken:]
    return norm, ordered


def body(
    hidden_in,
    gate_prior,
    routes,
    priority,
    segments,
    cotangent,
    attend_in,
    first_attend_in,
    second_attend_in,
    attend_out,
    first_attend_out,
    second_attend_out,
    router,
    first_router,
    second_router,
    gate_mix,
    first_gate_mix,
    second_gate_mix,
    constants,
    first_constants,
    second_constants,
    norm_gains,
    first_norm_gains,
    second_norm_gains,
    expert_in,
    first_expert_in,
    second_expert_in,
    expert_out,
    first_expert_out,
    second_expert_out,
):
    groups = lax.axis_size("expert")
    devices = lax.axis_size("dp") * groups
    kinds = gate_prior.shape[1]
    constant_count = constants.shape[1] // 3
    experts = kinds - 2 - constant_count
    token_count = hidden_in.shape[0]
    width_top = routes.shape[1]
    capacity = max(2, width_top * token_count // kinds // 8 * 8)
    slots = experts * capacity
    small_width = kinds + 3 * constant_count
    gate_end = kinds + 2 * constant_count

    expert_pieces = split_experts(expert_in, expert_out)
    mine = jnp.concatenate(
        [
            attend_in,
            attend_out,
            router,
            constants,
            norm_gains.T,
            jnp.zeros((attend_in.shape[0], LANES - small_width - 2), F32),
        ],
        axis=1,
    ).astype(BF16)
    mine, expert_pieces = lax.optimization_barrier((mine, expert_pieces))
    gathered = gather_all(gather_far(mine))
    expert_inner, expert_outer = gather_experts(expert_pieces)
    gains = gathered[:, 4 * D + small_width : 4 * D + small_width + 2].astype(F32).T
    gain_first, gain_second = gains[0:1], gains[1:2]

    targets = pair_targets(routes, priority[0], experts, kinds, capacity)
    target_rows = targets.T
    split = (groups, slots // groups, -1)
    arrived_grad = exchange(place_rows(cotangent, target_rows, slots).reshape(split), "expert")
    arrived_grad = arrived_grad.reshape(slots, D)
    route_rows = routes.T
    prior_rows = gate_prior.T
    extra = jnp.dot(gate_mix.astype(BF16).astype(F32).T, prior_rows, precision=highest)
    seg_row = segments
    seg_column = segments.reshape(token_count, 1)

    normed_first, packed = project(hidden_in, gain_first, gathered)
    attended, logsum = attend_forward(packed, seg_column, seg_row)
    middle, normed_second, table, rows = route_tokens(
        hidden_in,
        attended,
        cotangent,
        extra,
        route_rows,
        target_rows,
        gain_second,
        gathered,
        experts,
        constant_count,
        slots,
    )
    arrived = exchange(rows.reshape(split), "expert").reshape(slots, D + LANES)
    grad_joined, active, produced, met, weighed = expert_forward(
        arrived, arrived_grad, expert_inner, expert_outer
    )
    met = exchange(met.reshape(groups, 1, slots // groups), "expert").reshape(1, slots)
    grad_rows = expert_backward(grad_joined, expert_inner)
    met, grad_rows = lax.optimization_barrier((met, grad_rows))
    grad_returned = exchange(grad_rows.reshape(split), "expert").reshape(slots, D)
    grad_inner, grad_outer = expert_weights(
        arrived, weighed, grad_joined, active, lax.axis_size("dp")
    )
    grad_returned, produced, grad_inner, grad_outer = lax.optimization_barrier(
        (grad_returned, produced, grad_inner, grad_outer)
    )
    inner_own = scatter_expert(grad_inner)
    outer_own = scatter_expert(grad_outer)
    returned = exchange(produced.reshape(split), "expert").reshape(slots, D)
    grad_middle, grad_attended, grad_out_and_small, grad_mixer = middle_backward(
        grad_returned,
        met,
        targets,
        route_rows,
        prior_rows,
        table,
        middle,
        normed_second,
        cotangent,
        attended,
        gain_second,
        gathered,
        experts,
        constant_count,
    )
    out_sum = scatter_side(grad_out_and_small)

    grad_packed = attend_backward(packed, grad_attended, logsum, seg_column, seg_row)
    grad_packed, returned, out_sum = lax.optimization_barrier((grad_packed, returned, out_sum))
    in_sum = scatter_side(project_backward(normed_first, grad_packed))
    shares = exchange(jnp.concatenate([in_sum, out_sum], axis=2), "dp")
    input_grad, grad_gain_first = input_backward(
        grad_packed, gathered, hidden_in, grad_middle, gain_first
    )
    activations = mix_branches(
        returned, targets, table, middle, normed_second, gathered, gate_end, constant_count
    )

    in_own, out_own, outer_own, few = own_sums(
        shares, inner_own, outer_own, grad_gain_first, grad_mixer, devices
    )
    few = exchange(few, BOTH)
    index = lax.axis_index("dp") * groups + lax.axis_index("expert")
    states = (
        (attend_in, first_attend_in, second_attend_in),
        (attend_out, first_attend_out, second_attend_out),
        (router, first_router, second_router),
        (gate_mix, first_gate_mix, second_gate_mix),
        (constants, first_constants, second_constants),
        (norm_gains, first_norm_gains, second_norm_gains),
        (expert_in, first_expert_in, second_expert_in),
        (expert_out, first_expert_out, second_expert_out),
    )
    grad_norm, updated = update(
        index.reshape(1).astype(jnp.int32),
        few,
        in_own,
        out_own,
        inner_own,
        outer_own,
        states,
        kinds,
        constant_count,
    )
    return (activations, input_grad, grad_norm, *updated)


def solution(mesh):
    in_specs = (
        P(("dp", "expert"), None),
        P(("dp", "expert"), None),
        P(("dp", "expert"), None),
        P(("dp", "expert"), None),
        P(("dp", "expert"), None),
        P(("dp", "expert"), None),
        P(("dp", "expert"), None),
        P(("dp", "expert"), None),
        P(("dp", "expert"), None),
        P(("dp", "expert"), None),
        P(("dp", "expert"), None),
        P(("dp", "expert"), None),
        P(("dp", "expert"), None),
        P(("dp", "expert"), None),
        P(("dp", "expert"), None),
        P(),
        P(),
        P(),
        P(("dp", "expert"), None),
        P(("dp", "expert"), None),
        P(("dp", "expert"), None),
        P(None, ("dp", "expert")),
        P(None, ("dp", "expert")),
        P(None, ("dp", "expert")),
        P("expert", "dp", None),
        P("expert", "dp", None),
        P("expert", "dp", None),
        P("expert", "dp", None),
        P("expert", "dp", None),
        P("expert", "dp", None),
    )
    out_specs = (
        P(("dp", "expert"), None),
        P(("dp", "expert"), None),
        P(),
        P(("dp", "expert"), None),
        P(("dp", "expert"), None),
        P(("dp", "expert"), None),
        P(("dp", "expert"), None),
        P(("dp", "expert"), None),
        P(("dp", "expert"), None),
        P(("dp", "expert"), None),
        P(("dp", "expert"), None),
        P(("dp", "expert"), None),
        P(("dp", "expert"), None),
        P(("dp", "expert"), None),
        P(("dp", "expert"), None),
        P(("dp", "expert"), None),
        P(("dp", "expert"), None),
        P(("dp", "expert"), None),
        P(),
        P(),
        P(),
        P(),
        P(),
        P(("dp", "expert"), None),
        P(("dp", "expert"), None),
        P(("dp", "expert"), None),
        P(("dp", "expert"), None),
        P(("dp", "expert"), None),
        P(None, ("dp", "expert")),
        P(None, ("dp", "expert")),
        P(None, ("dp", "expert")),
        P(None, ("dp", "expert")),
        P(None, ("dp", "expert")),
        P("expert", "dp", None),
        P("expert", "dp", None),
        P("expert", "dp", None),
        P("expert", "dp", None),
        P("expert", "dp", None),
        P("expert", "dp", None),
        P("expert", "dp", None),
        P("expert", "dp", None),
        P("expert", "dp", None),
        P("expert", "dp", None),
    )
    return jax.shard_map(body, mesh=mesh, in_specs=in_specs, out_specs=out_specs, check_vma=False)
```

```python
import functools

import jax
import jax.numpy as jnp
from jax import lax
from jax.experimental import pallas as pl
from jax.experimental.pallas import tpu as pltpu
from jax.sharding import PartitionSpec as P

D = 768
FF = 2048
HEAD_DIM = 64
PAIR = 2 * HEAD_DIM
BLOCK = 256
LANES = 128
TOKENS = {'route': 512, 'mix': 512, 'middle': 512, 'input': 512}
BOTH = ("dp", "expert")

norm_epsilon = 1e-05
adam_epsilon = 1e-08
learn_rates = (0.01, 0.04, 0.01, 0.03, 0.01, 0.1, 0.01, 0.01)
decay_rate = 0.1
beta_moment = 0.5
step_number = 4.0
clip_limit = 1.0
score_scale = 0.125
masked_score = -1e30
highest = lax.Precision.HIGHEST
F32 = jnp.float32
BF16 = jnp.bfloat16

NN = (((1,), (0,)), ((), ()))
NT = (((1,), (1,)), ((), ()))
TN = (((0,), (0,)), ((), ()))

CHOSEN, COEF, SCALE, REST, BETA, GATE_GRAD, PROBS = 0, 2, 3, 4, 8, 16, 32
PIECES = 3
HINT = 64
UPDATE_STEPS = 4


def dot(left, right, form=NN):
    return lax.dot_general(left, right, form, preferred_element_type=F32)


def iota(shape, dim):
    return lax.broadcasted_iota(jnp.int32, shape, dim)


def row_scale(values):
    return lax.rsqrt(jnp.mean(values * values, axis=-1, keepdims=True) + norm_epsilon)


def params(mebibytes=56):
    return pltpu.CompilerParams(vmem_limit_bytes=mebibytes << 20)


def whole(shape):
    return pl.BlockSpec(shape, lambda *step: (0,) * len(shape))


def cost(flops, moved, transcendentals=0):
    share = HINT
    return pl.CostEstimate(
        flops=flops // share, bytes_accessed=moved // share, transcendentals=transcendentals // share
    )


def fill_bias(seg_column_ref, seg_row_ref, bias_ref, block):
    length = bias_ref.shape[0]
    for low in range(0, length, block):
        high = low + block
        columns = low + iota((high, block), 1)
        allowed = jnp.logical_and(
            seg_column_ref[:high, :] == seg_row_ref[:, low:high], iota((high, block), 0) <= columns
        )
        bias_ref[:high, low:high] = jnp.where(allowed, 0.0, masked_score)


def attend_forward_kernel(
    hidden_ref,
    gain_ref,
    query_weight_ref,
    key_weight_ref,
    value_weight_ref,
    seg_column_ref,
    seg_row_ref,
    normed_ref,
    packed_ref,
    out_ref,
    logsum_ref,
    bias_ref,
):
    length, block = hidden_ref.shape[0], BLOCK

    @pl.when(pl.program_id(0) == 0)
    def _():
        fill_bias(seg_column_ref, seg_row_ref, bias_ref, block)
        values = hidden_ref[...].astype(F32)
        normed_ref[...] = (values * row_scale(values) * gain_ref[...]).astype(BF16)

    weights = jnp.concatenate([query_weight_ref[...], key_weight_ref[...], value_weight_ref[...]], axis=1)
    packed = dot(normed_ref[...], weights).astype(BF16)
    for part in range(3):
        packed_ref[part] = packed[:, part * PAIR : (part + 1) * PAIR]
    for low in range(0, length, block):
        high = low + block
        for head in range(2):
            lanes = slice(head * HEAD_DIM, (head + 1) * HEAD_DIM)
            queries = packed_ref[0, low:high, lanes] * score_scale
            scores = dot(packed_ref[1, :high, lanes], queries, NT) + bias_ref[:high, low:high]
            maximum = jnp.max(scores, axis=0, keepdims=True)
            powers = jnp.exp(scores - maximum)
            totals = jnp.sum(powers, axis=0, keepdims=True)
            chances = (powers * (1.0 / totals)).astype(BF16)
            out_ref[low:high, lanes] = dot(chances, packed_ref[2, :high, lanes], TN).astype(BF16)
            logsum_ref[0, head : head + 1, low:high] = maximum + jnp.log(totals)


def attend_forward(hidden, gain, gathered, seg_column, seg_row):
    length = hidden.shape[0]
    pairs = D // PAIR
    return pl.pallas_call(
        attend_forward_kernel,
        grid=(pairs,),
        in_specs=[
            whole((length, D)),
            whole((1, D)),
            pl.BlockSpec((D, PAIR), lambda pair: (0, pair)),
            pl.BlockSpec((D, PAIR), lambda pair: (0, pairs + pair)),
            pl.BlockSpec((D, PAIR), lambda pair: (0, 2 * pairs + pair)),
            whole((length, 1)),
            whole((1, length)),
        ],
        out_specs=[
            whole((length, D)),
            pl.BlockSpec((3, length, PAIR), lambda pair: (0, 0, pair)),
            pl.BlockSpec((length, PAIR), lambda pair: (0, pair)),
            pl.BlockSpec((1, 2, length), lambda pair: (pair, 0, 0)),
        ],
        out_shape=[
            jax.ShapeDtypeStruct((length, D), BF16),
            jax.ShapeDtypeStruct((3, length, D), BF16),
            jax.ShapeDtypeStruct((length, D), BF16),
            jax.ShapeDtypeStruct((pairs, 2, length), F32),
        ],
        scratch_shapes=[pltpu.VMEM((length, length), F32)],
        compiler_params=params(),
        cost_estimate=cost(8 * length * length * D, 8 * length * D, length * length * 8),
        name="attend_forward",
    )(hidden, gain, gathered, gathered, gathered, seg_column, seg_row)


def part_rows(total, core, send_ref, keep_ref):
    rows = send_ref.shape[1]
    for k in range(send_ref.shape[0]):
        for ref, which in ((keep_ref, core), (send_ref, 1 - core)):
            start = pl.multiple_of((2 * k + which) * rows, 8)
            ref[k] = total[pl.ds(start, rows), :].astype(BF16)


def attend_backward_kernel(
    core_ref,
    query_ref,
    key_ref,
    value_ref,
    grad_ref,
    logsum_ref,
    seg_column_ref,
    seg_row_ref,
    normed_ref,
    out_ref,
    *refs,
):
    weight_refs, (bias_ref, key_sum, value_sum, turned, total) = refs[:-5], refs[-5:]
    length, block = seg_row_ref.shape[1], BLOCK

    @pl.when(pl.program_id(0) == 0)
    def _():
        fill_bias(seg_column_ref, seg_row_ref, bias_ref, block)
        turned[...] = normed_ref[...].T

    def lanes(head):
        return slice(head * HEAD_DIM, (head + 1) * HEAD_DIM)

    def scores(low, head):
        high, here = low + block, lanes(head)
        queries = query_ref[0, low:high, here] * score_scale
        return (
            dot(key_ref[0, :high, here], queries, NT),
            dot(value_ref[0, :high, here], grad_ref[low:high, here], NT),
        )

    def chances(low, head, raw, grad_weights):
        high = low + block
        weights = jnp.exp(raw + bias_ref[:high, low:high] - logsum_ref[0, head : head + 1, low:high])
        centred = jnp.sum(weights * grad_weights, axis=0, keepdims=True)
        return weights.astype(BF16), (weights * (grad_weights - centred)).astype(BF16)

    def gradients(low, head, weights, grad_raw):
        high, here = low + block, lanes(head)
        grad_values = dot(weights, grad_ref[low:high, here])
        grad_keys = dot(grad_raw, query_ref[0, low:high, here] * score_scale)
        if high == length:
            key_sum[:, here] = grad_keys
            value_sum[:, here] = grad_values
        else:
            key_sum[:high, here] += grad_keys
            value_sum[:high, here] += grad_values
        keys = key_ref[0, :high, here] * score_scale
        out_ref[0, low:high, here] = dot(keys, grad_raw, TN).T.astype(BF16)

    blocks = [(low, head) for low in reversed(range(0, length, block)) for head in range(2)]
    ready, before = scores(*blocks[0]), None
    for index, place in enumerate(blocks):
        after = scores(*blocks[index + 1]) if index + 1 < len(blocks) else None
        now = chances(*place, *ready)
        if before is not None:
            gradients(*before)
        before, ready = (*place, *now), after
    gradients(*before)
    out_ref[1] = key_sum[...].astype(BF16)
    out_ref[2] = value_sum[...].astype(BF16)
    weights = dot(turned[...], jnp.concatenate([out_ref[part] for part in range(3)], axis=1))
    if len(weight_refs) == 1:
        weight_refs[0][...] = weights.astype(BF16)
    else:
        total[...] = weights
        part_rows(total, core_ref[0], *weight_refs)


def attend_backward(core, packed, grad, logsum, seg_column, seg_row, normed, shards):
    length = packed.shape[1]
    pairs = D // PAIR
    rows = D // shards
    spec = lambda shape, place: pl.BlockSpec(shape, lambda pair, core: place(pair))
    always = lambda shape: spec(shape, lambda pair: (0,) * len(shape))
    if rows % 8:
        weight_specs = [spec((D, 3 * PAIR), lambda pair: (0, pair))]
        weight_shapes = [jax.ShapeDtypeStruct((D, 3 * D), BF16)]
    else:
        weight_specs = [spec((shards // 2, rows, 3 * PAIR), lambda pair: (0, 0, pair))] * 2
        weight_shapes = [jax.ShapeDtypeStruct((shards // 2, rows, 3 * D), BF16)] * 2
    results = pl.pallas_call(
        attend_backward_kernel,
        grid_spec=pltpu.PrefetchScalarGridSpec(
            num_scalar_prefetch=1,
            grid=(pairs,),
            in_specs=[
                spec((1, length, PAIR), lambda pair: (0, 0, pair)),
                spec((1, length, PAIR), lambda pair: (1, 0, pair)),
                spec((1, length, PAIR), lambda pair: (2, 0, pair)),
                spec((length, PAIR), lambda pair: (0, pair)),
                spec((1, 2, length), lambda pair: (pair, 0, 0)),
                always((length, 1)),
                always((1, length)),
                always((length, D)),
            ],
            out_specs=[spec((3, length, PAIR), lambda pair: (0, 0, pair)), *weight_specs],
            scratch_shapes=[
                pltpu.VMEM((length, length), F32),
                pltpu.VMEM((length, PAIR), F32),
                pltpu.VMEM((length, PAIR), F32),
                pltpu.VMEM((D, length), BF16),
                pltpu.VMEM((D, 3 * PAIR), F32),
            ],
        ),
        out_shape=[jax.ShapeDtypeStruct((3, length, D), BF16), *weight_shapes],
        compiler_params=params(),
        cost_estimate=cost(20 * length * length * D, 14 * length * D, length * length * 8),
        name="attend_backward",
    )(core, packed, packed, packed, grad, logsum, seg_column, seg_row, normed)
    return results[0], results[1:]


def route_kernel(
    hidden_ref,
    attended_ref,
    upstream_ref,
    extra_ref,
    routes_ref,
    targets_ref,
    gain_ref,
    weight_ref,
    small_ref,
    middle_ref,
    normed_ref,
    table_ref,
    rows_ref,
    normed_all,
    first_all,
    second_all,
    work,
    *,
    token_steps,
    experts,
    constant_count,
    slot_block,
):
    step = pl.program_id(0)
    block = hidden_ref.shape[0]
    kinds = extra_ref.shape[0]
    gate_end = kinds + 2 * constant_count

    @pl.when(step < token_steps)
    def _():
        middle = hidden_ref[...].astype(F32) + dot(attended_ref[...], weight_ref[...])
        scale = row_scale(middle)
        normed = (middle * scale * gain_ref[...]).astype(BF16)
        middle_ref[...] = middle
        normed_ref[...] = normed
        upstream = upstream_ref[...]
        wide = upstream.astype(F32)
        inner = jnp.sum(wide * normed.astype(F32), axis=1, keepdims=True)
        lane = iota((block, LANES), 1)
        small = jnp.where(lane >= gate_end, dot(upstream, small_ref[...]), dot(normed, small_ref[...]))
        small = jnp.where(lane == LANES - 1, inner, jnp.where(lane == LANES - 2, scale, small)).T
        inner = small[LANES - 1 : LANES]
        logits = small[:kinds] + extra_ref[...]
        powers = jnp.exp(logits - jnp.max(logits, axis=0, keepdims=True))
        probs = powers / jnp.sum(powers, axis=0, keepdims=True)
        places = iota((kinds, block), 0)
        work[...] = jnp.zeros_like(work)
        work[PROBS : PROBS + kinds] = probs
        work[SCALE : SCALE + 1] = small[LANES - 2 : LANES - 1]
        shares = []
        for which in range(constant_count):
            left = small[kinds + 2 * which : kinds + 2 * which + 1]
            right = small[kinds + 2 * which + 1 : kinds + 2 * which + 2]
            top = jnp.maximum(left, right)
            left, right = jnp.exp(left - top), jnp.exp(right - top)
            both = left + right
            shares.append((left / both, right / both))
        met = [small[gate_end + which : gate_end + which + 1] for which in range(constant_count)]
        nothing = jnp.zeros((1, block), F32)
        coef = nothing
        betas = [nothing] * constant_count
        amounts = [nothing] * constant_count
        for route in range(2):
            kind = routes_ref[route : route + 1, :]
            chosen = jnp.sum(jnp.where(places == kind, probs, 0.0), axis=0, keepdims=True)
            work[CHOSEN + route : CHOSEN + route + 1] = chosen
            part = jnp.where(kind == experts + 1, 1.0, 0.0)
            rest = nothing
            for which in range(constant_count):
                here = kind == experts + 2 + which
                part = part + jnp.where(here, shares[which][0], 0.0)
                rest = rest + jnp.where(here, shares[which][1] * met[which], 0.0)
                betas[which] = betas[which] + jnp.where(here, chosen * shares[which][1], 0.0)
                amounts[which] = amounts[which] + jnp.where(here, chosen, 0.0)
            coef = coef + chosen * part
            work[REST + route : REST + route + 1] = chosen * (rest + part * inner)
        work[COEF : COEF + 1] = coef
        for which in range(constant_count):
            work[BETA + which : BETA + which + 1] = betas[which]
            grad_left = amounts[which] * inner
            grad_right = amounts[which] * met[which]
            mean = shares[which][0] * grad_left + shares[which][1] * grad_right
            place = GATE_GRAD + 2 * which
            work[place : place + 1] = shares[which][0] * (grad_left - mean)
            work[place + 1 : place + 2] = shares[which][1] * (grad_right - mean)
        table = work[...].T
        table_ref[...] = table
        rows = pl.ds(pl.multiple_of(step * block, block), block)
        normed_all[rows, :] = normed
        for route, kept in enumerate((first_all, second_all)):
            rest = jnp.broadcast_to(table[:, CHOSEN + route : CHOSEN + route + 1], (block, LANES))
            pieces = jnp.zeros((block, LANES), F32)
            for piece in range(PIECES):
                upper = rest.astype(BF16).astype(F32)
                pieces = jnp.where(lane == piece, upper, pieces)
                rest = rest - upper
            kept[rows, :] = pieces.astype(BF16)

    @pl.when(step >= token_steps)
    def _():
        tokens = normed_all.shape[0]
        slots = (step - token_steps) * slot_block + iota((slot_block, tokens), 0)
        first = jnp.where(slots == targets_ref[0:1, :], 1.0, 0.0)
        second = jnp.where(slots == targets_ref[1:2, :], 1.0, 0.0)
        rows_ref[:, :D] = dot((first + second).astype(BF16), normed_all[...]).astype(BF16)
        rows_ref[:, D:] = (
            dot(first.astype(BF16), first_all[...]) + dot(second.astype(BF16), second_all[...])
        ).astype(BF16)


def place_kernel(rows_ref, targets_ref, out_ref):
    slot_block, tokens = out_ref.shape[0], rows_ref.shape[0]
    slots = pl.program_id(0) * slot_block + iota((slot_block, tokens), 0)
    hot = jnp.where(slots == targets_ref[0:1, :], 1.0, 0.0) + jnp.where(
        slots == targets_ref[1:2, :], 1.0, 0.0
    )
    out_ref[...] = dot(hot.astype(BF16), rows_ref[...]).astype(BF16)


def place_rows(rows, targets, slots):
    tokens = rows.shape[0]
    return pl.pallas_call(
        place_kernel,
        grid=(4,),
        in_specs=[whole((tokens, D)), whole((2, tokens))],
        out_specs=pl.BlockSpec((slots // 4, D), lambda step: (step, 0)),
        out_shape=jax.ShapeDtypeStruct((slots, D), BF16),
        compiler_params=params(),
        cost_estimate=cost(2 * tokens * D * slots, 4 * tokens * D),
        name="place_rows",
    )(rows, targets)


def route_tokens(
    hidden, attended, upstream, extra, routes, targets, gain, gathered, experts, constant_count, slots
):
    tokens = hidden.shape[0]
    kinds = extra.shape[0]
    block = TOKENS['route']
    steps = tokens // block
    slot_block = slots // 4
    token_block = lambda width: pl.BlockSpec(
        (block, width), lambda step: (jnp.minimum(step, steps - 1), 0)
    )
    token_lanes = lambda height: pl.BlockSpec(
        (height, block), lambda step: (0, jnp.minimum(step, steps - 1))
    )
    slot_rows = pl.BlockSpec((slot_block, D + LANES), lambda step: (jnp.maximum(step - steps, 0), 0))
    kernel = functools.partial(
        route_kernel,
        token_steps=steps,
        experts=experts,
        constant_count=constant_count,
        slot_block=slot_block,
    )
    return pl.pallas_call(
        kernel,
        grid=(steps + 4,),
        in_specs=[
            token_block(D),
            token_block(D),
            token_block(D),
            token_lanes(kinds),
            token_lanes(2),
            whole((2, tokens)),
            whole((1, D)),
            pl.BlockSpec((D, D), lambda step: (0, 3)),
            pl.BlockSpec((D, LANES), lambda step: (0, 4 * D // LANES)),
        ],
        out_specs=[
            token_block(D),
            token_block(D),
            token_block(LANES),
            slot_rows,
        ],
        out_shape=[
            jax.ShapeDtypeStruct((tokens, D), F32),
            jax.ShapeDtypeStruct((tokens, D), BF16),
            jax.ShapeDtypeStruct((tokens, LANES), F32),
            jax.ShapeDtypeStruct((slots, D + LANES), BF16),
        ],
        scratch_shapes=[
            pltpu.VMEM((tokens, D), BF16),
            pltpu.VMEM((tokens, LANES), BF16),
            pltpu.VMEM((tokens, LANES), BF16),
            pltpu.VMEM((LANES, block), F32),
        ],
        compiler_params=params(),
        cost_estimate=cost(2 * tokens * D * (D + slots), 20 * tokens * D),
        name="route_tokens",
    )(hidden, attended, upstream, extra, routes, targets, gain, gathered, gathered)


def inner_spec(weights, pieces, column):
    if weights.ndim == 2:
        return pl.BlockSpec((D, pieces * BLOCK), lambda step: (0, column(step)))
    shards = weights.shape[0]
    return pl.BlockSpec((shards, pieces * D // shards, BLOCK), lambda step: (0, column(step), 0))


def read_inner(ref):
    if len(ref.shape) == 2:
        return ref[...]
    shards = ref.shape[0]
    rows = D // shards
    pieces = [
        jnp.concatenate([ref[position(shards, k), low : low + rows, :] for k in range(shards)], axis=0)
        for low in range(0, ref.shape[1], rows)
    ]
    return jnp.concatenate(pieces, axis=1)


def outer_specs(weights, pieces):
    if weights.ndim == 2:
        return [pl.BlockSpec((pieces * BLOCK, D), lambda step: (step, 0))]
    shards = weights.shape[0]
    first = weights.shape[1] // BLOCK - D // BLOCK
    even = lambda c: pl.BlockSpec((1, BLOCK, BLOCK), lambda step: (step, first + c, 0))
    odd = lambda c: pl.BlockSpec((1, BLOCK, BLOCK), lambda step: (shards - 1 - step, first + c, 0))
    return [even(c) for c in range(D // BLOCK)] + [odd(c) for c in range(D // BLOCK)]


def read_outer(refs):
    if len(refs) == 1:
        return refs[0][...]
    half = len(refs) // 2
    return jnp.concatenate(
        [jnp.concatenate([ref[0] for ref in some], axis=1) for some in (refs[:half], refs[half:])], axis=0
    )


def expert_kernel(rows_ref, grads_ref, gate_ref, up_ref, *refs, outers):
    outer_refs, refs = refs[:outers], refs[outers:]
    joined_ref, active_ref, produced_ref, met_ref, weighed_ref, total = refs
    step = pl.program_id(0)

    @pl.when(step == 0)
    def _():
        chosen = jnp.sum(rows_ref[:, D:].astype(F32), axis=1, keepdims=True)
        weighed_ref[...] = (chosen * grads_ref[...].astype(F32)).astype(BF16)

    outer = read_outer(outer_refs)
    gates, ups = read_inner(gate_ref), read_inner(up_ref)
    parts = [slice(low, low + BLOCK) for low in range(0, outer.shape[0], BLOCK)]

    def enter(part):
        return (
            dot(rows_ref[:, :D], gates[:, part]),
            dot(rows_ref[:, :D], ups[:, part]),
            dot(weighed_ref[...], outer[part], NT),
        )

    part_total = 0.0
    entered = enter(parts[0])
    for index, part in enumerate(parts):
        gate, up, grad_active = entered
        if index + 1 < len(parts):
            entered = enter(parts[index + 1])
        sigmoid = 1.0 / (1.0 + jnp.exp(-gate))
        silu = gate * sigmoid
        active = (silu * up).astype(BF16)
        active_ref[:, part] = active
        slope = sigmoid * (1.0 + gate * (1.0 - sigmoid))
        joined_ref[0, :, part] = (grad_active * up * slope).astype(BF16)
        joined_ref[1, :, part] = (grad_active * silu).astype(BF16)
        part_total = part_total + dot(active, outer[part])
    total[...] = jnp.where(step == 0, part_total, total[...] + part_total)

    @pl.when(step == pl.num_programs(0) - 1)
    def _():
        produced = total[...].astype(BF16)
        produced_ref[...] = produced
        met = weighed_ref[...].astype(F32) * produced.astype(F32)
        met = sum(met[:, low : low + LANES] for low in range(0, D, LANES))
        met_ref[...] = jnp.sum(met.T, axis=0, keepdims=True)


def expert_forward(rows, grads, inner, outer):
    count = rows.shape[0]
    pieces = 2
    width = pieces * BLOCK
    steps = FF // width
    outers = outer_specs(outer, pieces)
    return pl.pallas_call(
        functools.partial(expert_kernel, outers=len(outers)),
        grid=(steps,),
        in_specs=[
            whole((count, D + LANES)),
            whole((count, D)),
            inner_spec(inner, pieces, lambda step: step),
            inner_spec(inner, pieces, lambda step: steps + step),
            *outers,
        ],
        out_specs=[
            pl.BlockSpec((2, count, width), lambda step: (0, 0, step)),
            pl.BlockSpec((count, width), lambda step: (0, step)),
            whole((count, D)),
            whole((1, count)),
            whole((count, D)),
        ],
        out_shape=[
            jax.ShapeDtypeStruct((2, count, FF), BF16),
            jax.ShapeDtypeStruct((count, FF), BF16),
            jax.ShapeDtypeStruct((count, D), BF16),
            jax.ShapeDtypeStruct((1, count), F32),
            jax.ShapeDtypeStruct((count, D), BF16),
        ],
        scratch_shapes=[pltpu.VMEM((count, D), F32)],
        compiler_params=params(),
        cost_estimate=cost(8 * count * D * FF, 6 * count * FF + 6 * D * FF, count * FF),
        name="expert_forward",
    )(rows, grads, inner, inner, *[outer] * len(outers))


def outer_weights_kernel(*refs):
    *active_refs, weighed_ref, out_ref = refs
    active = jnp.concatenate([ref[...] for ref in active_refs], axis=1)
    out_ref[...] = dot(active, weighed_ref[...], TN).astype(BF16).reshape(out_ref.shape)


def outer_weights(active, weighed, shards):
    count = active.shape[0]
    width = FF // shards
    if width % LANES:
        lanes, taken, places = LANES, LANES // width, [lambda step: step]
    else:
        lanes, taken = width, 4
        place = lambda at: jnp.where(at < shards // 2, 2 * at, 2 * (shards - 1 - at) + 1)
        places = [lambda step, k=k: place(4 * step + k) for k in range(4)]
    out = pl.pallas_call(
        outer_weights_kernel,
        grid=(shards // taken,),
        in_specs=[
            pl.BlockSpec((count, lanes), lambda step, place=place: (0, place(step))) for place in places
        ]
        + [whole((count, D))],
        out_specs=pl.BlockSpec((taken, width, D), lambda step: (step, 0, 0)),
        out_shape=jax.ShapeDtypeStruct((shards, width, D), BF16),
        compiler_params=params(),
        cost_estimate=cost(2 * count * D * FF, 2 * count * FF + 2 * D * FF),
        name="outer_weights",
    )(*[active] * len(places), weighed)
    if width % LANES:
        out = jnp.concatenate([out[k : k + 1] for k in around(shards)], axis=0)
    return out


def inner_weights_kernel(rows_ref, joined_ref, out_ref, turned):
    @pl.when(pl.program_id(0) == 0)
    def _():
        turned[...] = rows_ref[...].T

    shards, _, share, _ = out_ref.shape
    for half in range(2):
        grads = dot(turned[...], joined_ref[half]).astype(BF16)
        for k in range(shards):
            out_ref[position(shards, k), half] = grads[k * share : (k + 1) * share]


def inner_weights(rows, joined, shards):
    count = rows.shape[0]
    width = 2 * BLOCK
    share = D // shards
    return pl.pallas_call(
        inner_weights_kernel,
        grid=(FF // width,),
        in_specs=[
            pl.BlockSpec((count, D), lambda step: (0, 0)),
            pl.BlockSpec((2, count, width), lambda step: (0, 0, step)),
        ],
        out_specs=pl.BlockSpec((shards, 2, share, width), lambda step: (0, 0, 0, step)),
        out_shape=jax.ShapeDtypeStruct((shards, 2, share, FF), BF16),
        scratch_shapes=[pltpu.VMEM((D, count), BF16)],
        compiler_params=params(),
        cost_estimate=cost(4 * count * D * FF, 4 * count * FF + 4 * D * FF),
        name="inner_weights",
    )(rows, joined)


def expert_backward_kernel(joined_ref, inner_ref, grads_ref, total):
    step = pl.program_id(0)
    part = dot(joined_ref[0], read_inner(inner_ref), NT)
    total[...] = jnp.where(step == 0, part, total[...] + part)

    @pl.when(step == pl.num_programs(0) - 1)
    def _():
        grads_ref[...] = total[...].astype(BF16)


def expert_backward(joined, inner):
    count = joined.shape[1]
    pieces = 4
    width = pieces * BLOCK
    half = FF // width
    return pl.pallas_call(
        expert_backward_kernel,
        grid=(2 * half,),
        in_specs=[
            pl.BlockSpec((1, count, width), lambda step: (step // half, 0, step % half)),
            inner_spec(inner, pieces, lambda step: step),
        ],
        out_specs=whole((count, D)),
        out_shape=jax.ShapeDtypeStruct((count, D), BF16),
        scratch_shapes=[pltpu.VMEM((count, D), F32)],
        compiler_params=params(),
        cost_estimate=cost(4 * count * D * FF, 4 * count * FF + 4 * D * FF),
        name="expert_backward",
    )(joined, inner)


def mix_kernel(
    returned_ref,
    targets_ref,
    table_ref,
    middle_ref,
    normed_ref,
    small_ref,
    out_ref,
    *,
    value_place,
    constant_count,
):
    block = middle_ref.shape[0]
    slots = returned_ref.shape[0]
    table = table_ref[...]
    columns = iota((block, slots), 1)
    lane = iota((block, LANES), 1)
    blended = normed_ref[...].astype(F32) * table[:, COEF : COEF + 1]
    for route in range(2):
        hot = jnp.where(columns == targets_ref[:, route : route + 1], 1.0, 0.0).astype(BF16)
        paired = dot(hot, returned_ref[...])
        blended = blended + table[:, CHOSEN + route : CHOSEN + route + 1] * paired
    values = jnp.zeros((block, LANES), F32)
    for which in range(constant_count):
        place = BETA + which
        values = jnp.where(lane == value_place + which, table[:, place : place + 1], values)
    upper = values.astype(BF16)
    lower = (values - upper.astype(F32)).astype(BF16)
    blended = blended + (dot(upper, small_ref[...], NT) + dot(lower, small_ref[...], NT))
    out_ref[...] = (middle_ref[...] + blended).astype(BF16)


def mix_branches(returned, targets, table, middle, normed, gathered, value_place, constant_count):
    block = TOKENS["mix"]
    tokens = middle.shape[0]
    slots = returned.shape[0]
    token_block = lambda width: pl.BlockSpec((block, width), lambda step: (step, 0))
    return pl.pallas_call(
        functools.partial(mix_kernel, value_place=value_place, constant_count=constant_count),
        grid=(tokens // block,),
        in_specs=[
            whole((slots, D)),
            token_block(2),
            token_block(LANES),
            token_block(D),
            token_block(D),
            pl.BlockSpec((D, LANES), lambda step: (0, 4 * D // LANES)),
        ],
        out_specs=token_block(D),
        out_shape=jax.ShapeDtypeStruct((tokens, D), BF16),
        compiler_params=params(),
        cost_estimate=cost(4 * tokens * D * slots, 12 * tokens * D),
        name="mix_branches",
    )(returned, targets, table, middle, normed, gathered)


def middle_kernel(
    core_ref,
    returned_ref,
    met_ref,
    targets_ref,
    routes_ref,
    prior_ref,
    table_ref,
    middle_ref,
    normed_ref,
    upstream_ref,
    attended_ref,
    small_ref,
    gain_ref,
    weight_ref,
    grad_middle_ref,
    grad_attended_ref,
    mixer_ref,
    *refs,
    experts,
    constant_count,
):
    weight_refs, (work, grad_gain, grad_small, grad_weight) = refs[:-4], refs[-4:]
    block = middle_ref.shape[0]
    slots = returned_ref.shape[0]
    kinds = prior_ref.shape[0]
    gates = 2 * constant_count
    first = pl.program_id(0) == 0
    table = table_ref[...]
    wide = upstream_ref[...].astype(F32)
    columns = iota((block, slots), 1)
    hot = jnp.where(columns == targets_ref[:, 0:1], 1.0, 0.0) + jnp.where(
        columns == targets_ref[:, 1:2], 1.0, 0.0
    )
    hot = hot.astype(BF16)
    total = dot(hot, returned_ref[...]) + wide * table[:, COEF : COEF + 1]
    met = met_ref[...]
    upper = met.astype(BF16).astype(F32)
    here = iota((LANES, slots), 1) // (slots // experts) == iota((LANES, slots), 0) % experts
    halves = jnp.where(iota((LANES, slots), 0) < experts, upper, met - upper)
    met = jnp.where(jnp.logical_and(here, iota((LANES, slots), 0) < 2 * experts), halves, 0.0)
    met = dot(hot, met.astype(BF16), NT)
    met = met.T
    turned = table.T
    probs = turned[PROBS : PROBS + kinds]
    places = iota((kinds, block), 0)
    met = met[:experts] + met[experts : 2 * experts]
    work[...] = jnp.zeros_like(work)
    work[:experts] = met
    weighed = work[:kinds]
    for route in range(2):
        rest = turned[REST + route : REST + route + 1]
        weighed = weighed + jnp.where(places == routes_ref[route : route + 1, :], rest, 0.0)
    grad_logits = weighed - probs * jnp.sum(weighed, axis=0, keepdims=True)
    part = lax.dot_general(
        prior_ref[...], grad_logits, NT, precision=highest, preferred_element_type=F32
    )
    mixer_ref[...] = jnp.where(first, part, mixer_ref[...] + part)
    work[:kinds] = grad_logits
    work[kinds : kinds + gates] = turned[GATE_GRAD : GATE_GRAD + gates]
    work[kinds + gates : kinds + gates + constant_count] = turned[BETA : BETA + constant_count]
    values = work[...].T
    upper = values.astype(BF16)
    lower = (values - upper.astype(F32)).astype(BF16)
    is_small = iota((block, LANES), 1) < kinds + gates
    nothing = jnp.zeros((block, LANES), BF16)
    total = total + (
        dot(jnp.where(is_small, upper, nothing), small_ref[...], NT)
        + dot(jnp.where(is_small, lower, nothing), small_ref[...], NT)
    )
    both = jnp.concatenate([upper, lower], axis=1)
    part = jnp.where(
        iota((1, 2 * LANES), 1) % LANES < kinds + gates,
        dot(normed_ref[...], both, TN),
        dot(upstream_ref[...], both, TN),
    )
    part = part[:, :LANES] + part[:, LANES:]
    grad_small[...] = jnp.where(first, part, grad_small[...] + part)

    scale = table[:, SCALE : SCALE + 1]
    unit = middle_ref[...] * scale
    part = jnp.sum(total * unit, axis=0, keepdims=True)
    grad_gain[...] = jnp.where(first, part, grad_gain[...] + part)
    inner = total * gain_ref[...]
    grad_middle = wide + scale * (inner - unit * jnp.mean(inner * unit, axis=1, keepdims=True))
    grad_middle_ref[...] = grad_middle
    rounded = grad_middle.astype(BF16)
    grad_attended_ref[...] = dot(rounded, weight_ref[...], NT).astype(BF16)
    part = dot(attended_ref[...], rounded, TN)
    grad_weight[:, :D] = jnp.where(first, part, grad_weight[:, :D] + part)

    @pl.when(pl.program_id(0) == pl.num_programs(0) - 1)
    def _():
        column = jnp.broadcast_to(grad_gain[...], (LANES, D)).T
        place = kinds + gates + constant_count
        grad_weight[:, D:] = jnp.where(iota((D, LANES), 1) == place, column, grad_small[...])
        if len(weight_refs) == 1:
            weight_refs[0][...] = grad_weight[...].astype(BF16)
        else:
            part_rows(grad_weight, core_ref[0], *weight_refs)


def middle_backward(
    core,
    returned,
    met,
    targets,
    routes,
    prior,
    table,
    middle,
    normed,
    upstream,
    attended,
    gain,
    gathered,
    experts,
    constant_count,
    shards,
):
    block = TOKENS["middle"]
    tokens = middle.shape[0]
    slots = returned.shape[0]
    kinds = prior.shape[0]
    rows = D // shards
    spec = lambda shape, place: pl.BlockSpec(shape, lambda step, core: place(step))
    always = lambda shape: spec(shape, lambda step: (0,) * len(shape))
    token_block = lambda width: spec((block, width), lambda step: (step, 0))
    token_lanes = lambda height: spec((height, block), lambda step: (0, step))
    if rows % 8:
        weights = [(D, D + LANES)]
    else:
        weights = [(shards // 2, rows, D + LANES)] * 2
    results = pl.pallas_call(
        functools.partial(middle_kernel, experts=experts, constant_count=constant_count),
        grid_spec=pltpu.PrefetchScalarGridSpec(
            num_scalar_prefetch=1,
            grid=(tokens // block,),
            in_specs=[
                always((slots, D)),
                always((1, slots)),
                token_block(2),
                token_lanes(2),
                token_lanes(kinds),
                token_block(LANES),
                token_block(D),
                token_block(D),
                token_block(D),
                token_block(D),
                spec((D, LANES), lambda step: (0, 4 * D // LANES)),
                always((1, D)),
                spec((D, D), lambda step: (0, 3)),
            ],
            out_specs=[token_block(D), token_block(D), always((kinds, kinds))]
            + [always(shape) for shape in weights],
            scratch_shapes=[
                pltpu.VMEM((LANES, block), F32),
                pltpu.VMEM((1, D), F32),
                pltpu.VMEM((D, LANES), F32),
                pltpu.VMEM((D, D + LANES), F32),
            ],
        ),
        out_shape=[
            jax.ShapeDtypeStruct((tokens, D), F32),
            jax.ShapeDtypeStruct((tokens, D), BF16),
            jax.ShapeDtypeStruct((kinds, kinds), F32),
        ]
        + [jax.ShapeDtypeStruct(shape, BF16) for shape in weights],
        compiler_params=params(),
        cost_estimate=cost(2 * tokens * D * (slots + 2 * D), 18 * tokens * D),
        name="middle_backward",
    )(
        core,
        returned,
        met,
        targets,
        routes,
        prior,
        table,
        middle,
        normed,
        upstream,
        attended,
        gathered,
        gain,
        gathered,
    )
    return *results[:3], results[3:]


def input_kernel(packed_ref, weight_ref, hidden_ref, grad_middle_ref, gain_ref, out_ref, grad_gain_ref):
    total = sum(dot(packed_ref[c], weight_ref[:, c * D : (c + 1) * D], NT) for c in range(3))
    values = hidden_ref[...].astype(F32)
    scale = row_scale(values)
    unit = values * scale
    part = jnp.sum(total * unit, axis=0, keepdims=True)
    grad_gain_ref[...] = jnp.where(pl.program_id(0) == 0, part, grad_gain_ref[...] + part)
    inner = total * gain_ref[...]
    out_ref[...] = grad_middle_ref[...] + scale * (
        inner - unit * jnp.mean(inner * unit, axis=1, keepdims=True)
    )


def input_backward(grad_packed, gathered, hidden, grad_middle, gain):
    block = TOKENS['input']
    tokens = hidden.shape[0]
    token_block = lambda width: pl.BlockSpec((block, width), lambda step: (step, 0))
    return pl.pallas_call(
        input_kernel,
        grid=(tokens // block,),
        in_specs=[
            pl.BlockSpec((3, block, D), lambda step: (0, step, 0)),
            pl.BlockSpec((D, 3 * D), lambda step: (0, 0)),
            token_block(D),
            token_block(D),
            whole((1, D)),
        ],
        out_specs=[token_block(D), whole((1, D))],
        out_shape=[
            jax.ShapeDtypeStruct((tokens, D), F32),
            jax.ShapeDtypeStruct((1, D), F32),
        ],
        compiler_params=params(),
        cost_estimate=cost(6 * tokens * D * D, 16 * tokens * D),
        name="input_backward",
    )(grad_packed, gathered, hidden, grad_middle, gain)


def pair_targets(routes, priority, experts, total_kinds, capacity):
    kind_ids = jnp.arange(total_kinds, dtype=jnp.int32)
    hot = [(routes[:, k : k + 1] == kind_ids[None, :]).astype(F32) for k in range(2)]
    earlier = (priority[None, :] < priority[:, None]).astype(BF16)
    before = dot(earlier, (hot[0] + hot[1]).astype(BF16))
    slots = jnp.stack([jnp.sum(before * one, axis=1) for one in hot], axis=1).astype(jnp.int32)
    kept_pairs = jnp.logical_and(routes < experts, slots < capacity)
    return jnp.where(kept_pairs, routes * capacity + slots, experts * capacity)


def exchange(blocks, axis):
    return lax.all_to_all(blocks, axis, split_axis=0, concat_axis=0, tiled=True)


def exchange_apart(blocks, axis):
    count, me = lax.axis_size(axis), lax.axis_index(axis)
    out = jnp.zeros_like(blocks)
    for step in range(count):
        block = pick(blocks, (me + step) % count, 0)
        if step:
            block = lax.ppermute(block, axis, [(i, (i + step) % count) for i in range(count)])
        out = lax.dynamic_update_slice(out, block[None], ((me - step) % count,) + (0,) * block.ndim)
    return out


def flip(axis):
    return [(i, i ^ 1) for i in range(lax.axis_size(axis))]


def shift(axis, step):
    count = lax.axis_size(axis)
    return [(i, (i + 2 * step) % count) for i in range(count)]


def gather_far(mine):
    far, depth = lax.axis_size("dp") // 2, lax.axis_index("dp") // 2
    column = jnp.zeros((far, *mine.shape), mine.dtype)
    for step in range(far):
        came = mine if step == 0 else lax.ppermute(mine, "dp", shift("dp", step))
        column = lax.dynamic_update_slice(column, came[None], ((depth - step) % far, 0, 0))
    return column


def gather_all(column):
    far, rows, width = column.shape
    wide, side = lax.axis_size("expert") // 2, lax.axis_index("dp") % 2
    place, core = lax.axis_index("expert") // 2, lax.axis_index("expert") % 2
    near = [column, lax.ppermute(column, "dp", flip("dp"))]
    total = jnp.zeros((far, 2, wide, 2, rows, width), column.dtype)
    for step in range(wide):
        for other in range(2):
            piece = near[other]
            if step:
                piece = lax.ppermute(piece, "expert", shift("expert", step))
            twin = lax.ppermute(piece, "expert", flip("expert"))
            spot = (0, side ^ other, (place - step) % wide)
            shaped = (far, 1, 1, 1, rows, width)
            total = lax.dynamic_update_slice(total, piece.reshape(shaped), (*spot, core, 0, 0))
            total = lax.dynamic_update_slice(total, twin.reshape(shaped), (*spot, 1 - core, 0, 0))
    return total.reshape(-1, width)


def pick(array, index, axis):
    return lax.dynamic_index_in_dim(array, index, axis, keepdims=False)


def scatter_side(parted):
    wide = lax.axis_size("expert") // 2
    place, core = lax.axis_index("expert") // 2, lax.axis_index("expert") % 2
    if len(parted) == 1:
        terms = parted[0].reshape(lax.axis_size("dp") * wide, 2, -1, parted[0].shape[1])
        parted = (pick(terms, 1 - core, 1), pick(terms, core, 1))
    send, keep = parted
    came = lax.ppermute(send, "expert", flip("expert"))
    pair = (keep.astype(F32) + came.astype(F32)).astype(BF16)
    pair = pair.reshape(lax.axis_size("dp"), wide, *pair.shape[1:])
    total = pick(pair, place, 1).astype(F32)
    for step in range(1, wide):
        came = lax.ppermute(pick(pair, (place + step) % wide, 1), "expert", shift("expert", step))
        total = total + came.astype(F32)
    return total.astype(BF16)


def around(count):
    return list(range(0, count, 2)) + list(range(count - 1, 0, -2))


def position(count, place):
    return place // 2 if place % 2 == 0 else count - 1 - place // 2


def split_experts(expert_in, expert_out):
    inner, outer = expert_in[0].astype(BF16), expert_out[0].astype(BF16)
    if inner.shape[0] % 16 or outer.shape[0] != BLOCK:
        return [inner, outer]
    pieces = [
        array.reshape(array.shape[0], -1, BLOCK).transpose(1, 0, 2).reshape(-1, BLOCK)
        for array in (inner, outer)
    ]
    return [jnp.concatenate(pieces, axis=0)]


def gather_experts(pieces):
    ring = [around(lax.axis_size("dp"))]
    if len(pieces) == 1:
        both = lax.all_gather(pieces[0], "dp", axis=0, axis_index_groups=ring)
        return both, both
    return [lax.all_gather(piece, "dp", axis=0, tiled=True) for piece in pieces]


def scatter_expert(grads):
    ring = [around(lax.axis_size("dp"))]
    return lax.psum_scatter(grads, "dp", scatter_dimension=0, tiled=True, axis_index_groups=ring)[0]


def own_kernel(
    in_ref, shares_ref, inner_ref, outer_ref, gain_ref, mixer_ref, own_ref, out_ref, own_outer_ref, few_ref, *, kinds
):
    total = jnp.sum(in_ref[...].astype(F32), axis=0)
    out = jnp.sum(shares_ref[...].astype(F32), axis=0)
    for pair in range(D // PAIR):
        for part in range(3):
            low, place = (3 * pair + part) * PAIR, part * D + pair * PAIR
            own_ref[:, place : place + PAIR] = total[:, low : low + PAIR]
    out_ref[...] = out
    inner, outer = inner_ref[...].astype(F32), outer_ref[...].astype(F32)
    own_outer_ref[...] = outer
    width = few_ref.shape[2]
    square = jnp.sum(jnp.sum(inner * inner, axis=0), axis=(0, 1), keepdims=True)
    for member in (total, out, outer):
        square = square + jnp.sum(member * member, axis=(0, 1), keepdims=True)
    few = few_ref.at[0]
    few[...] = jnp.zeros_like(few)
    few[0:1, :D] = gain_ref[...]
    for row in range(kinds):
        place = D + row * kinds
        few[0:1, place : place + kinds] = mixer_ref[row : row + 1, :]
    few[0:1, width - LANES :] = jnp.broadcast_to(square, (1, LANES))
    row = few[...]
    for device in range(1, few_ref.shape[0]):
        few_ref[device] = row


def own_sums(in_shares, out_shares, inner, outer, grad_gain, grad_mixer, devices):
    kinds = grad_mixer.shape[0]
    width = D + (-(-kinds * kinds // LANES) + 1) * LANES
    rows = in_shares.shape[1]
    return pl.pallas_call(
        functools.partial(own_kernel, kinds=kinds),
        out_shape=[
            jax.ShapeDtypeStruct((rows, 3 * D), F32),
            jax.ShapeDtypeStruct((rows, D + LANES), F32),
            jax.ShapeDtypeStruct(outer.shape, F32),
            jax.ShapeDtypeStruct((devices, 1, width), F32),
        ],
        compiler_params=params(),
        cost_estimate=cost(6 * D * FF, 3 * D * FF),
        name="own_sums",
    )(in_shares, out_shares, inner, outer, grad_gain, grad_mixer)


def adam(master, first, second, grad, factor, step_rate):
    clipped = grad * factor
    first_new = beta_moment * first + (1.0 - beta_moment) * clipped
    second_new = beta_moment * second + (1.0 - beta_moment) * clipped * clipped
    correct = 1.0 - beta_moment**step_number
    update = (
        first_new / correct / (jnp.sqrt(second_new / correct) + adam_epsilon) + decay_rate * master
    )
    return (master - step_rate * update, first_new, second_new)


def update_kernel(*refs, kinds, constant_count):
    index_ref, few_ref, in_ref, out_ref, inner_ref, outer_ref = refs[:6]
    states = [refs[6 + 3 * which : 9 + 3 * which] for which in range(8)]
    norm_ref, results = refs[30], refs[31:]
    width = out_ref.shape[1]
    few = jnp.sum(few_ref[...], axis=0)
    gain_total = few[:, :D]
    mixer_total = few[:, D : D + kinds * kinds]
    square = (
        few[:, few.shape[1] - 1 :]
        + jnp.sum(gain_total * gain_total, axis=1, keepdims=True)
        + jnp.sum(mixer_total * mixer_total, axis=1, keepdims=True)
    )
    norm = jnp.sqrt(square)
    factor = clip_limit / jnp.maximum(norm, clip_limit)
    places = iter(results)
    slots = [[next(places) for _ in range(4 if which in (0, 7) else 5)] for which in range(8)]

    def step(which, grad):
        master, first, second = states[which]
        outs = slots[which]
        if len(outs) == 5:
            outs[0][...] = grad.reshape(outs[0].shape)
            outs = outs[1:]
        shape = outs[0].shape
        lay = lambda value: value.reshape(grad.shape)
        new = adam(lay(master[...]), lay(first[...]), lay(second[...]), grad, factor, learn_rates[which])
        for ref, value in zip(outs, new + (new[0],)):
            ref[...] = value.reshape(shape).astype(ref.dtype)

    step(6, inner_ref[0].astype(F32))
    step(7, outer_ref[...])

    @pl.when(pl.program_id(0) == 0)
    def _():
        norm_ref[...] = norm
        step(0, in_ref[...])
        step(1, out_ref[:, :D])
        rows = out_ref.shape[0]
        narrow = jnp.pad(out_ref[:, D:], ((0, LANES - rows), (0, 0))).T
        step(2, narrow[:kinds, :rows])
        step(3, jnp.concatenate([mixer_total[:, k * kinds : (k + 1) * kinds] for k in range(kinds)], axis=0))
        small = kinds + 3 * constant_count
        step(4, narrow[kinds:small, :rows])
        start = index_ref[0] * rows
        picked = (iota((D, LANES), 0) == start + iota((D, LANES), 1)).astype(F32)
        own = lax.dot_general(
            jnp.broadcast_to(gain_total, (8, D)), picked, NN, precision=highest, preferred_element_type=F32
        )
        step(5, jnp.concatenate([own[0:1, :rows], narrow[small : small + 1, :rows]], axis=0))


def update(index, few, in_own, out_own, inner_own, outer_own, states, kinds, constant_count):
    steps = UPDATE_STEPS
    turn = lambda which, array: array.T if which in (2, 4) else array
    states = [[turn(which, array) for array in state] for which, state in enumerate(states)]
    half = steps // 2
    flat = [array for state in states for array in state]

    def spec(shape):
        if len(shape) == 3 and shape[2] == 2 * FF:
            return pl.BlockSpec((1, shape[1], shape[2] // steps), lambda step, index: (0, 0, step))
        if len(shape) == 3:
            return pl.BlockSpec((1, shape[1] // steps, shape[2]), lambda step, index: (0, step, 0))
        return pl.BlockSpec(shape, lambda step, index: (0, 0))

    out_shape = [jax.ShapeDtypeStruct((1, 1), F32)]
    for which in range(8):
        shape = states[which][0].shape
        kept = 3 if which in (0, 7) else 4
        out_shape += [jax.ShapeDtypeStruct(shape, F32)] * kept + [jax.ShapeDtypeStruct(shape, BF16)]
    results = pl.pallas_call(
        functools.partial(update_kernel, kinds=kinds, constant_count=constant_count),
        grid_spec=pltpu.PrefetchScalarGridSpec(
            num_scalar_prefetch=1,
            grid=(steps,),
            in_specs=[
                pl.BlockSpec(few.shape, lambda step, index: (0, 0, 0)),
                spec(in_own.shape),
                spec(out_own.shape),
                pl.BlockSpec(
                    (1, inner_own.shape[1], FF // half), lambda step, index: (step // half, 0, step % half)
                ),
                pl.BlockSpec((outer_own.shape[0] // steps, D), lambda step, index: (step, 0)),
            ]
            + [spec(array.shape) for array in flat],
            out_specs=[spec(leaf.shape) for leaf in out_shape],
        ),
        out_shape=out_shape,
        compiler_params=params(),
        cost_estimate=cost(40 * D * FF, 60 * D * FF // 2),
        name="update",
    )(index, few, in_own, out_own, inner_own, outer_own, *flat)
    norm, rest = results[0].reshape(()), list(results[1:])
    grads = {0: in_own, 7: outer_own[None]}
    ordered = []
    for which in range(8):
        taken = 4 if which in grads else 5
        ordered += [grads[which]] if which in grads else []
        ordered += [turn(which, array) for array in rest[:taken]]
        rest = rest[taken:]
    return norm, ordered


def body(
    hidden_in,
    gate_prior,
    routes,
    priority,
    segments,
    cotangent,
    attend_in,
    first_attend_in,
    second_attend_in,
    attend_out,
    first_attend_out,
    second_attend_out,
    router,
    first_router,
    second_router,
    gate_mix,
    first_gate_mix,
    second_gate_mix,
    constants,
    first_constants,
    second_constants,
    norm_gains,
    first_norm_gains,
    second_norm_gains,
    expert_in,
    first_expert_in,
    second_expert_in,
    expert_out,
    first_expert_out,
    second_expert_out,
):
    groups = lax.axis_size("expert")
    devices = lax.axis_size("dp") * groups
    kinds = gate_prior.shape[1]
    constant_count = constants.shape[1] // 3
    experts = kinds - 2 - constant_count
    token_count = hidden_in.shape[0]
    width_top = routes.shape[1]
    capacity = max(2, width_top * token_count // kinds // 8 * 8)
    slots = experts * capacity
    small_width = kinds + 3 * constant_count
    gate_end = kinds + 2 * constant_count

    expert_pieces = split_experts(expert_in, expert_out)
    mine = jnp.concatenate(
        [
            attend_in,
            attend_out,
            router,
            constants,
            norm_gains.T,
            jnp.zeros((attend_in.shape[0], LANES - small_width - 2), F32),
        ],
        axis=1,
    ).astype(BF16)
    targets = pair_targets(routes, priority[0], experts, kinds, capacity)
    target_rows = targets.T
    split = (groups, slots // groups, -1)
    placed = place_rows(cotangent, target_rows, slots).reshape(split)
    column = gather_far(mine)
    column, placed = lax.optimization_barrier((column, placed))
    gathered = gather_all(column)
    expert_inner, expert_outer = gather_experts(expert_pieces)
    gains = gathered[:, 4 * D + small_width : 4 * D + small_width + 2].astype(F32).T
    gain_first, gain_second = gains[0:1], gains[1:2]
    arrived_grad = exchange(placed, "expert").reshape(slots, D)
    route_rows = routes.T
    prior_rows = gate_prior.T
    extra = jnp.dot(gate_mix.astype(BF16).astype(F32).T, prior_rows, precision=highest)
    seg_row = segments
    seg_column = segments.reshape(token_count, 1)

    normed_first, packed, attended, logsum = attend_forward(
        hidden_in, gain_first, gathered, seg_column, seg_row
    )
    middle, normed_second, table, rows = route_tokens(
        hidden_in,
        attended,
        cotangent,
        extra,
        route_rows,
        target_rows,
        gain_second,
        gathered,
        experts,
        constant_count,
        slots,
    )
    arrived = exchange(rows.reshape(split), "expert").reshape(slots, D + LANES)
    grad_joined, active, produced, met, weighed = expert_forward(
        arrived, arrived_grad, expert_inner, expert_outer
    )
    outer_own = scatter_expert(outer_weights(active, weighed, lax.axis_size("dp")))
    met = exchange(met.reshape(groups, 1, slots // groups), "expert").reshape(1, slots)
    grad_rows = expert_backward(grad_joined, expert_inner)
    met, grad_rows, grad_joined = lax.optimization_barrier((met, grad_rows, grad_joined))
    grad_returned = exchange(grad_rows.reshape(split), "expert").reshape(slots, D)
    grad_inner = inner_weights(arrived, grad_joined, lax.axis_size("dp"))
    grad_returned, produced, grad_inner = lax.optimization_barrier((grad_returned, produced, grad_inner))
    inner_own = scatter_expert(grad_inner)
    core = (lax.axis_index("expert") % 2).reshape(1).astype(jnp.int32)
    grad_middle, grad_attended, grad_mixer, grad_out_and_small = middle_backward(
        core,
        grad_returned,
        met,
        targets,
        route_rows,
        prior_rows,
        table,
        middle,
        normed_second,
        cotangent,
        attended,
        gain_second,
        gathered,
        experts,
        constant_count,
        devices,
    )
    out_sum = scatter_side(grad_out_and_small)

    grad_packed, grad_weight_in = attend_backward(
        core, packed, grad_attended, logsum, seg_column, seg_row, normed_first, devices
    )
    grad_weight_in, out_sum = lax.optimization_barrier((grad_weight_in, out_sum))
    in_sum = scatter_side(grad_weight_in)
    out_shares = exchange(out_sum, "dp")
    in_sum, out_shares, produced = lax.optimization_barrier((in_sum, out_shares, produced))
    returned = exchange_apart(produced.reshape(split), "expert").reshape(slots, D)
    in_shares = exchange(in_sum, "dp")
    input_grad, grad_gain_first = input_backward(
        grad_packed, gathered, hidden_in, grad_middle, gain_first
    )
    activations = mix_branches(
        returned, targets, table, middle, normed_second, gathered, gate_end, constant_count
    )

    in_own, out_own, outer_own, few = own_sums(
        in_shares, out_shares, inner_own, outer_own, grad_gain_first, grad_mixer, devices
    )
    few = exchange(few, BOTH)
    index = lax.axis_index("dp") * groups + lax.axis_index("expert")
    states = (
        (attend_in, first_attend_in, second_attend_in),
        (attend_out, first_attend_out, second_attend_out),
        (router, first_router, second_router),
        (gate_mix, first_gate_mix, second_gate_mix),
        (constants, first_constants, second_constants),
        (norm_gains, first_norm_gains, second_norm_gains),
        (expert_in, first_expert_in, second_expert_in),
        (expert_out, first_expert_out, second_expert_out),
    )
    grad_norm, updated = update(
        index.reshape(1).astype(jnp.int32),
        few,
        in_own,
        out_own,
        inner_own,
        outer_own,
        states,
        kinds,
        constant_count,
    )
    return (activations, input_grad, grad_norm, *updated)


def solution(mesh):
    in_specs = (
        P(("dp", "expert"), None),
        P(("dp", "expert"), None),
        P(("dp", "expert"), None),
        P(("dp", "expert"), None),
        P(("dp", "expert"), None),
        P(("dp", "expert"), None),
        P(("dp", "expert"), None),
        P(("dp", "expert"), None),
        P(("dp", "expert"), None),
        P(("dp", "expert"), None),
        P(("dp", "expert"), None),
        P(("dp", "expert"), None),
        P(("dp", "expert"), None),
        P(("dp", "expert"), None),
        P(("dp", "expert"), None),
        P(),
        P(),
        P(),
        P(("dp", "expert"), None),
        P(("dp", "expert"), None),
        P(("dp", "expert"), None),
        P(None, ("dp", "expert")),
        P(None, ("dp", "expert")),
        P(None, ("dp", "expert")),
        P("expert", "dp", None),
        P("expert", "dp", None),
        P("expert", "dp", None),
        P("expert", "dp", None),
        P("expert", "dp", None),
        P("expert", "dp", None),
    )
    out_specs = (
        P(("dp", "expert"), None),
        P(("dp", "expert"), None),
        P(),
        P(("dp", "expert"), None),
        P(("dp", "expert"), None),
        P(("dp", "expert"), None),
        P(("dp", "expert"), None),
        P(("dp", "expert"), None),
        P(("dp", "expert"), None),
        P(("dp", "expert"), None),
        P(("dp", "expert"), None),
        P(("dp", "expert"), None),
        P(("dp", "expert"), None),
        P(("dp", "expert"), None),
        P(("dp", "expert"), None),
        P(("dp", "expert"), None),
        P(("dp", "expert"), None),
        P(("dp", "expert"), None),
        P(),
        P(),
        P(),
        P(),
        P(),
        P(("dp", "expert"), None),
        P(("dp", "expert"), None),
        P(("dp", "expert"), None),
        P(("dp", "expert"), None),
        P(("dp", "expert"), None),
        P(None, ("dp", "expert")),
        P(None, ("dp", "expert")),
        P(None, ("dp", "expert")),
        P(None, ("dp", "expert")),
        P(None, ("dp", "expert")),
        P("expert", "dp", None),
        P("expert", "dp", None),
        P("expert", "dp", None),
        P("expert", "dp", None),
        P("expert", "dp", None),
        P("expert", "dp", None),
        P("expert", "dp", None),
        P("expert", "dp", None),
        P("expert", "dp", None),
        P("expert", "dp", None),
    )
    return jax.shard_map(body, mesh=mesh, in_specs=in_specs, out_specs=out_specs, check_vma=False)
```

```python
import functools

import jax
import jax.numpy as jnp
from jax import lax
from jax.experimental import pallas as pl
from jax.experimental.pallas import tpu as pltpu
from jax.sharding import PartitionSpec as P

D = 768
FF = 2048
HEAD_DIM = 64
PAIR = 2 * HEAD_DIM
BLOCK = 256
LANES = 128
TOKENS = {'route': 512, 'mix': 512, 'middle': 512, 'input': 512}
BOTH = ("dp", "expert")

norm_epsilon = 1e-05
adam_epsilon = 1e-08
learn_rates = (0.01, 0.04, 0.01, 0.03, 0.01, 0.1, 0.01, 0.01)
decay_rate = 0.1
beta_moment = 0.5
step_number = 4.0
clip_limit = 1.0
score_scale = 0.125
masked_score = -1e30
highest = lax.Precision.HIGHEST
F32 = jnp.float32
BF16 = jnp.bfloat16

NN = (((1,), (0,)), ((), ()))
NT = (((1,), (1,)), ((), ()))
TN = (((0,), (0,)), ((), ()))

CHOSEN, COEF, SCALE, REST, BETA, GATE_GRAD, PROBS = 0, 2, 3, 4, 8, 16, 32
PIECES = 3
HINT = 64


def dot(left, right, form=NN):
    return lax.dot_general(left, right, form, preferred_element_type=F32)


def iota(shape, dim):
    return lax.broadcasted_iota(jnp.int32, shape, dim)


def row_scale(values):
    return lax.rsqrt(jnp.mean(values * values, axis=-1, keepdims=True) + norm_epsilon)


def params(mebibytes=56):
    return pltpu.CompilerParams(vmem_limit_bytes=mebibytes << 20)


def whole(shape):
    return pl.BlockSpec(shape, lambda *step: (0,) * len(shape))


def cost(flops, moved, transcendentals=0):
    share = HINT
    return pl.CostEstimate(
        flops=flops // share, bytes_accessed=moved // share, transcendentals=transcendentals // share
    )


def fill_bias(seg_column_ref, seg_row_ref, bias_ref, block):
    length = bias_ref.shape[0]
    for low in range(0, length, block):
        high = low + block
        columns = low + iota((high, block), 1)
        allowed = jnp.logical_and(
            seg_column_ref[:high, :] == seg_row_ref[:, low:high], iota((high, block), 0) <= columns
        )
        bias_ref[:high, low:high] = jnp.where(allowed, 0.0, masked_score)


def attend_forward_kernel(
    hidden_ref,
    gain_ref,
    query_weight_ref,
    key_weight_ref,
    value_weight_ref,
    seg_column_ref,
    seg_row_ref,
    normed_ref,
    packed_ref,
    out_ref,
    logsum_ref,
    bias_ref,
):
    length, block = hidden_ref.shape[0], BLOCK

    @pl.when(pl.program_id(0) == 0)
    def _():
        fill_bias(seg_column_ref, seg_row_ref, bias_ref, block)
        values = hidden_ref[...].astype(F32)
        normed_ref[...] = (values * row_scale(values) * gain_ref[...]).astype(BF16)

    weights = jnp.concatenate([query_weight_ref[...], key_weight_ref[...], value_weight_ref[...]], axis=1)
    packed = dot(normed_ref[...], weights).astype(BF16)
    for part in range(3):
        packed_ref[part] = packed[:, part * PAIR : (part + 1) * PAIR]
    for low in range(0, length, block):
        high = low + block
        for head in range(2):
            lanes = slice(head * HEAD_DIM, (head + 1) * HEAD_DIM)
            queries = packed_ref[0, low:high, lanes] * score_scale
            scores = dot(packed_ref[1, :high, lanes], queries, NT) + bias_ref[:high, low:high]
            maximum = jnp.max(scores, axis=0, keepdims=True)
            powers = jnp.exp(scores - maximum)
            totals = jnp.sum(powers, axis=0, keepdims=True)
            chances = (powers * (1.0 / totals)).astype(BF16)
            out_ref[low:high, lanes] = dot(chances, packed_ref[2, :high, lanes], TN).astype(BF16)
            logsum_ref[0, head : head + 1, low:high] = maximum + jnp.log(totals)


def attend_forward(hidden, gain, gathered, seg_column, seg_row):
    length = hidden.shape[0]
    pairs = D // PAIR
    return pl.pallas_call(
        attend_forward_kernel,
        grid=(pairs,),
        in_specs=[
            whole((length, D)),
            whole((1, D)),
            pl.BlockSpec((D, PAIR), lambda pair: (0, pair)),
            pl.BlockSpec((D, PAIR), lambda pair: (0, pairs + pair)),
            pl.BlockSpec((D, PAIR), lambda pair: (0, 2 * pairs + pair)),
            whole((length, 1)),
            whole((1, length)),
        ],
        out_specs=[
            whole((length, D)),
            pl.BlockSpec((3, length, PAIR), lambda pair: (0, 0, pair)),
            pl.BlockSpec((length, PAIR), lambda pair: (0, pair)),
            pl.BlockSpec((1, 2, length), lambda pair: (pair, 0, 0)),
        ],
        out_shape=[
            jax.ShapeDtypeStruct((length, D), BF16),
            jax.ShapeDtypeStruct((3, length, D), BF16),
            jax.ShapeDtypeStruct((length, D), BF16),
            jax.ShapeDtypeStruct((pairs, 2, length), F32),
        ],
        scratch_shapes=[pltpu.VMEM((length, length), F32)],
        compiler_params=params(),
        cost_estimate=cost(8 * length * length * D, 8 * length * D, length * length * 8),
        name="attend_forward",
    )(hidden, gain, gathered, gathered, gathered, seg_column, seg_row)


def part_rows(total, core, send_ref, keep_ref):
    rows = send_ref.shape[1]
    for k in range(send_ref.shape[0]):
        for ref, which in ((keep_ref, core), (send_ref, 1 - core)):
            start = pl.multiple_of((2 * k + which) * rows, 8)
            ref[k] = total[pl.ds(start, rows), :].astype(BF16)


def attend_backward_kernel(
    core_ref,
    query_ref,
    key_ref,
    value_ref,
    grad_ref,
    logsum_ref,
    seg_column_ref,
    seg_row_ref,
    normed_ref,
    out_ref,
    *refs,
):
    weight_refs, (bias_ref, key_sum, value_sum, turned, total, kept) = refs[:-6], refs[-6:]
    pair = pl.program_id(0)
    length, block = seg_row_ref.shape[1], BLOCK

    @pl.when(pl.program_id(0) == 0)
    def _():
        fill_bias(seg_column_ref, seg_row_ref, bias_ref, block)
        turned[...] = normed_ref[...].T

    def lanes(head):
        return slice(head * HEAD_DIM, (head + 1) * HEAD_DIM)

    def scores(low, head):
        high, here = low + block, lanes(head)
        queries = query_ref[0, low:high, here] * score_scale
        return (
            dot(key_ref[0, :high, here], queries, NT),
            dot(value_ref[0, :high, here], grad_ref[low:high, here], NT),
        )

    def chances(low, head, raw, grad_weights):
        high = low + block
        weights = jnp.exp(raw + bias_ref[:high, low:high] - logsum_ref[0, head : head + 1, low:high])
        centred = jnp.sum(weights * grad_weights, axis=0, keepdims=True)
        return weights.astype(BF16), (weights * (grad_weights - centred)).astype(BF16)

    def gradients(low, head, weights, grad_raw):
        high, here = low + block, lanes(head)
        grad_values = dot(weights, grad_ref[low:high, here])
        grad_keys = dot(grad_raw, query_ref[0, low:high, here] * score_scale)
        if high == length:
            key_sum[:, here] = grad_keys
            value_sum[:, here] = grad_values
        else:
            key_sum[:high, here] += grad_keys
            value_sum[:high, here] += grad_values
        keys = key_ref[0, :high, here] * score_scale
        out_ref[0, low:high, here] = dot(keys, grad_raw, TN).T.astype(BF16)

    blocks = [(low, head) for low in reversed(range(0, length, block)) for head in range(2)]
    ready, before = scores(*blocks[0]), None
    for index, place in enumerate(blocks):
        after = scores(*blocks[index + 1]) if index + 1 < len(blocks) else None
        now = chances(*place, *ready)
        if before is not None:
            gradients(*before)
        before, ready = (*place, *now), after
    gradients(*before)
    out_ref[1] = key_sum[...].astype(BF16)
    out_ref[2] = value_sum[...].astype(BF16)
    for part in range(3):
        kept[pair % 2, part] = out_ref[part]

    @pl.when(pair % 2 == 1)
    def _():
        both = jnp.concatenate([kept[which, part] for which in range(2) for part in range(3)], axis=1)
        weights = dot(turned[...], both)
        if len(weight_refs) == 1:
            weight_refs[0][...] = weights.astype(BF16)
        else:
            total[...] = weights
            part_rows(total, core_ref[0], *weight_refs)


def attend_backward(core, packed, grad, logsum, seg_column, seg_row, normed, shards):
    length = packed.shape[1]
    pairs = D // PAIR
    rows = D // shards
    spec = lambda shape, place: pl.BlockSpec(shape, lambda pair, core: place(pair))
    always = lambda shape: spec(shape, lambda pair: (0,) * len(shape))
    if rows % 8:
        weight_specs = [spec((D, 6 * PAIR), lambda pair: (0, pair // 2))]
        weight_shapes = [jax.ShapeDtypeStruct((D, 3 * D), BF16)]
    else:
        weight_specs = [spec((shards // 2, rows, 6 * PAIR), lambda pair: (0, 0, pair // 2))] * 2
        weight_shapes = [jax.ShapeDtypeStruct((shards // 2, rows, 3 * D), BF16)] * 2
    results = pl.pallas_call(
        attend_backward_kernel,
        grid_spec=pltpu.PrefetchScalarGridSpec(
            num_scalar_prefetch=1,
            grid=(pairs,),
            in_specs=[
                spec((1, length, PAIR), lambda pair: (0, 0, pair)),
                spec((1, length, PAIR), lambda pair: (1, 0, pair)),
                spec((1, length, PAIR), lambda pair: (2, 0, pair)),
                spec((length, PAIR), lambda pair: (0, pair)),
                spec((1, 2, length), lambda pair: (pair, 0, 0)),
                always((length, 1)),
                always((1, length)),
                always((length, D)),
            ],
            out_specs=[spec((3, length, PAIR), lambda pair: (0, 0, pair)), *weight_specs],
            scratch_shapes=[
                pltpu.VMEM((length, length), F32),
                pltpu.VMEM((length, PAIR), F32),
                pltpu.VMEM((length, PAIR), F32),
                pltpu.VMEM((D, length), BF16),
                pltpu.VMEM((D, 6 * PAIR), F32),
                pltpu.VMEM((2, 3, length, PAIR), BF16),
            ],
        ),
        out_shape=[jax.ShapeDtypeStruct((3, length, D), BF16), *weight_shapes],
        compiler_params=params(),
        cost_estimate=cost(20 * length * length * D, 14 * length * D, length * length * 8),
        name="attend_backward",
    )(core, packed, packed, packed, grad, logsum, seg_column, seg_row, normed)
    return results[0], results[1:]


def route_kernel(
    hidden_ref,
    attended_ref,
    upstream_ref,
    extra_ref,
    routes_ref,
    targets_ref,
    gain_ref,
    weight_ref,
    small_ref,
    middle_ref,
    normed_ref,
    table_ref,
    rows_ref,
    normed_all,
    first_all,
    second_all,
    work,
    *,
    token_steps,
    experts,
    constant_count,
    slot_block,
):
    step = pl.program_id(0)
    block = hidden_ref.shape[0]
    kinds = extra_ref.shape[0]
    gate_end = kinds + 2 * constant_count

    @pl.when(step < token_steps)
    def _():
        middle = hidden_ref[...].astype(F32) + dot(attended_ref[...], weight_ref[...])
        scale = row_scale(middle)
        normed = (middle * scale * gain_ref[...]).astype(BF16)
        middle_ref[...] = middle
        normed_ref[...] = normed
        upstream = upstream_ref[...]
        wide = upstream.astype(F32)
        inner = jnp.sum(wide * normed.astype(F32), axis=1, keepdims=True)
        lane = iota((block, LANES), 1)
        small = jnp.where(lane >= gate_end, dot(upstream, small_ref[...]), dot(normed, small_ref[...]))
        small = jnp.where(lane == LANES - 1, inner, jnp.where(lane == LANES - 2, scale, small)).T
        inner = small[LANES - 1 : LANES]
        logits = small[:kinds] + extra_ref[...]
        powers = jnp.exp(logits - jnp.max(logits, axis=0, keepdims=True))
        probs = powers / jnp.sum(powers, axis=0, keepdims=True)
        places = iota((kinds, block), 0)
        work[...] = jnp.zeros_like(work)
        work[PROBS : PROBS + kinds] = probs
        work[SCALE : SCALE + 1] = small[LANES - 2 : LANES - 1]
        shares = []
        for which in range(constant_count):
            left = small[kinds + 2 * which : kinds + 2 * which + 1]
            right = small[kinds + 2 * which + 1 : kinds + 2 * which + 2]
            top = jnp.maximum(left, right)
            left, right = jnp.exp(left - top), jnp.exp(right - top)
            both = left + right
            shares.append((left / both, right / both))
        met = [small[gate_end + which : gate_end + which + 1] for which in range(constant_count)]
        nothing = jnp.zeros((1, block), F32)
        coef = nothing
        betas = [nothing] * constant_count
        amounts = [nothing] * constant_count
        for route in range(2):
            kind = routes_ref[route : route + 1, :]
            chosen = jnp.sum(jnp.where(places == kind, probs, 0.0), axis=0, keepdims=True)
            work[CHOSEN + route : CHOSEN + route + 1] = chosen
            part = jnp.where(kind == experts + 1, 1.0, 0.0)
            rest = nothing
            for which in range(constant_count):
                here = kind == experts + 2 + which
                part = part + jnp.where(here, shares[which][0], 0.0)
                rest = rest + jnp.where(here, shares[which][1] * met[which], 0.0)
                betas[which] = betas[which] + jnp.where(here, chosen * shares[which][1], 0.0)
                amounts[which] = amounts[which] + jnp.where(here, chosen, 0.0)
            coef = coef + chosen * part
            work[REST + route : REST + route + 1] = chosen * (rest + part * inner)
        work[COEF : COEF + 1] = coef
        for which in range(constant_count):
            work[BETA + which : BETA + which + 1] = betas[which]
            grad_left = amounts[which] * inner
            grad_right = amounts[which] * met[which]
            mean = shares[which][0] * grad_left + shares[which][1] * grad_right
            place = GATE_GRAD + 2 * which
            work[place : place + 1] = shares[which][0] * (grad_left - mean)
            work[place + 1 : place + 2] = shares[which][1] * (grad_right - mean)
        table = work[...].T
        table_ref[...] = table
        rows = pl.ds(pl.multiple_of(step * block, block), block)
        normed_all[rows, :] = normed
        for route, kept in enumerate((first_all, second_all)):
            rest = jnp.broadcast_to(table[:, CHOSEN + route : CHOSEN + route + 1], (block, LANES))
            pieces = jnp.zeros((block, LANES), F32)
            for piece in range(PIECES):
                upper = rest.astype(BF16).astype(F32)
                pieces = jnp.where(lane == piece, upper, pieces)
                rest = rest - upper
            kept[rows, :] = pieces.astype(BF16)

    @pl.when(step >= token_steps)
    def _():
        tokens = normed_all.shape[0]
        slots = (step - token_steps) * slot_block + iota((slot_block, tokens), 0)
        first = jnp.where(slots == targets_ref[0:1, :], 1.0, 0.0)
        second = jnp.where(slots == targets_ref[1:2, :], 1.0, 0.0)
        rows_ref[:, :D] = dot((first + second).astype(BF16), normed_all[...]).astype(BF16)
        rows_ref[:, D:] = (
            dot(first.astype(BF16), first_all[...]) + dot(second.astype(BF16), second_all[...])
        ).astype(BF16)


def place_kernel(rows_ref, targets_ref, out_ref):
    slot_block, tokens = out_ref.shape[0], rows_ref.shape[0]
    slots = pl.program_id(0) * slot_block + iota((slot_block, tokens), 0)
    hot = jnp.where(slots == targets_ref[0:1, :], 1.0, 0.0) + jnp.where(
        slots == targets_ref[1:2, :], 1.0, 0.0
    )
    out_ref[...] = dot(hot.astype(BF16), rows_ref[...]).astype(BF16)


def place_rows(rows, targets, slots):
    tokens = rows.shape[0]
    return pl.pallas_call(
        place_kernel,
        grid=(4,),
        in_specs=[whole((tokens, D)), whole((2, tokens))],
        out_specs=pl.BlockSpec((slots // 4, D), lambda step: (step, 0)),
        out_shape=jax.ShapeDtypeStruct((slots, D), BF16),
        compiler_params=params(),
        cost_estimate=cost(2 * tokens * D * slots, 4 * tokens * D),
        name="place_rows",
    )(rows, targets)


def route_tokens(
    hidden, attended, upstream, extra, routes, targets, gain, gathered, experts, constant_count, slots
):
    tokens = hidden.shape[0]
    kinds = extra.shape[0]
    block = TOKENS['route']
    steps = tokens // block
    slot_block = slots // 4
    token_block = lambda width: pl.BlockSpec(
        (block, width), lambda step: (jnp.minimum(step, steps - 1), 0)
    )
    token_lanes = lambda height: pl.BlockSpec(
        (height, block), lambda step: (0, jnp.minimum(step, steps - 1))
    )
    slot_rows = pl.BlockSpec((slot_block, D + LANES), lambda step: (jnp.maximum(step - steps, 0), 0))
    kernel = functools.partial(
        route_kernel,
        token_steps=steps,
        experts=experts,
        constant_count=constant_count,
        slot_block=slot_block,
    )
    return pl.pallas_call(
        kernel,
        grid=(steps + 4,),
        in_specs=[
            token_block(D),
            token_block(D),
            token_block(D),
            token_lanes(kinds),
            token_lanes(2),
            whole((2, tokens)),
            whole((1, D)),
            pl.BlockSpec((D, D), lambda step: (0, 3)),
            pl.BlockSpec((D, LANES), lambda step: (0, 4 * D // LANES)),
        ],
        out_specs=[
            token_block(D),
            token_block(D),
            token_block(LANES),
            slot_rows,
        ],
        out_shape=[
            jax.ShapeDtypeStruct((tokens, D), F32),
            jax.ShapeDtypeStruct((tokens, D), BF16),
            jax.ShapeDtypeStruct((tokens, LANES), F32),
            jax.ShapeDtypeStruct((slots, D + LANES), BF16),
        ],
        scratch_shapes=[
            pltpu.VMEM((tokens, D), BF16),
            pltpu.VMEM((tokens, LANES), BF16),
            pltpu.VMEM((tokens, LANES), BF16),
            pltpu.VMEM((LANES, block), F32),
        ],
        compiler_params=params(),
        cost_estimate=cost(2 * tokens * D * (D + slots), 20 * tokens * D),
        name="route_tokens",
    )(hidden, attended, upstream, extra, routes, targets, gain, gathered, gathered)


def inner_spec(weights, pieces, column):
    if weights.ndim == 2:
        return pl.BlockSpec((D, pieces * BLOCK), lambda step: (0, column(step)))
    shards = weights.shape[0]
    return pl.BlockSpec((shards, pieces * D // shards, BLOCK), lambda step: (0, column(step), 0))


def read_inner(ref):
    if len(ref.shape) == 2:
        return ref[...]
    shards = ref.shape[0]
    rows = D // shards
    pieces = [
        jnp.concatenate([ref[position(shards, k), low : low + rows, :] for k in range(shards)], axis=0)
        for low in range(0, ref.shape[1], rows)
    ]
    return jnp.concatenate(pieces, axis=1)


def outer_specs(weights, pieces):
    if weights.ndim == 2:
        return [pl.BlockSpec((pieces * BLOCK, D), lambda step: (step, 0))]
    shards = weights.shape[0]
    first = weights.shape[1] // BLOCK - D // BLOCK
    even = lambda c: pl.BlockSpec((1, BLOCK, BLOCK), lambda step: (step, first + c, 0))
    odd = lambda c: pl.BlockSpec((1, BLOCK, BLOCK), lambda step: (shards - 1 - step, first + c, 0))
    return [even(c) for c in range(D // BLOCK)] + [odd(c) for c in range(D // BLOCK)]


def read_outer(refs):
    if len(refs) == 1:
        return refs[0][...]
    half = len(refs) // 2
    return jnp.concatenate(
        [jnp.concatenate([ref[0] for ref in some], axis=1) for some in (refs[:half], refs[half:])], axis=0
    )


def expert_kernel(rows_ref, grads_ref, gate_ref, up_ref, *refs, outers):
    outer_refs, refs = refs[:outers], refs[outers:]
    joined_ref, active_ref, produced_ref, met_ref, weighed_ref, total = refs
    step = pl.program_id(0)

    @pl.when(step == 0)
    def _():
        chosen = jnp.sum(rows_ref[:, D:].astype(F32), axis=1, keepdims=True)
        weighed_ref[...] = (chosen * grads_ref[...].astype(F32)).astype(BF16)

    outer = read_outer(outer_refs)
    gates, ups = read_inner(gate_ref), read_inner(up_ref)
    parts = [slice(low, low + BLOCK) for low in range(0, outer.shape[0], BLOCK)]

    def enter(part):
        return (
            dot(rows_ref[:, :D], gates[:, part]),
            dot(rows_ref[:, :D], ups[:, part]),
            dot(weighed_ref[...], outer[part], NT),
        )

    part_total = 0.0
    entered = enter(parts[0])
    for index, part in enumerate(parts):
        gate, up, grad_active = entered
        if index + 1 < len(parts):
            entered = enter(parts[index + 1])
        sigmoid = 1.0 / (1.0 + jnp.exp(-gate))
        silu = gate * sigmoid
        active = (silu * up).astype(BF16)
        active_ref[:, part] = active
        slope = sigmoid * (1.0 + gate * (1.0 - sigmoid))
        joined_ref[0, :, part] = (grad_active * up * slope).astype(BF16)
        joined_ref[1, :, part] = (grad_active * silu).astype(BF16)
        part_total = part_total + dot(active, outer[part])
    total[...] = jnp.where(step == 0, part_total, total[...] + part_total)

    @pl.when(step == pl.num_programs(0) - 1)
    def _():
        produced = total[...].astype(BF16)
        produced_ref[...] = produced
        met = weighed_ref[...].astype(F32) * produced.astype(F32)
        met = sum(met[:, low : low + LANES] for low in range(0, D, LANES))
        met_ref[...] = jnp.sum(met.T, axis=0, keepdims=True)


def expert_forward(rows, grads, inner, outer):
    count = rows.shape[0]
    pieces = 2
    width = pieces * BLOCK
    steps = FF // width
    outers = outer_specs(outer, pieces)
    return pl.pallas_call(
        functools.partial(expert_kernel, outers=len(outers)),
        grid=(steps,),
        in_specs=[
            whole((count, D + LANES)),
            whole((count, D)),
            inner_spec(inner, pieces, lambda step: step),
            inner_spec(inner, pieces, lambda step: steps + step),
            *outers,
        ],
        out_specs=[
            pl.BlockSpec((2, count, width), lambda step: (0, 0, step)),
            pl.BlockSpec((count, width), lambda step: (0, step)),
            whole((count, D)),
            whole((1, count)),
            whole((count, D)),
        ],
        out_shape=[
            jax.ShapeDtypeStruct((2, count, FF), BF16),
            jax.ShapeDtypeStruct((count, FF), BF16),
            jax.ShapeDtypeStruct((count, D), BF16),
            jax.ShapeDtypeStruct((1, count), F32),
            jax.ShapeDtypeStruct((count, D), BF16),
        ],
        scratch_shapes=[pltpu.VMEM((count, D), F32)],
        compiler_params=params(),
        cost_estimate=cost(8 * count * D * FF, 6 * count * FF + 6 * D * FF, count * FF),
        name="expert_forward",
    )(rows, grads, inner, inner, *[outer] * len(outers))


def outer_weights_kernel(*refs):
    *active_refs, weighed_ref, out_ref = refs
    active = jnp.concatenate([ref[...] for ref in active_refs], axis=1)
    out_ref[...] = dot(active, weighed_ref[...], TN).astype(BF16).reshape(out_ref.shape)


def outer_weights(active, weighed, shards):
    count = active.shape[0]
    width = FF // shards
    if width % LANES:
        lanes, taken, places = LANES, LANES // width, [lambda step: step]
    else:
        lanes, taken = width, 4
        place = lambda at: jnp.where(at < shards // 2, 2 * at, 2 * (shards - 1 - at) + 1)
        places = [lambda step, k=k: place(4 * step + k) for k in range(4)]
    out = pl.pallas_call(
        outer_weights_kernel,
        grid=(shards // taken,),
        in_specs=[
            pl.BlockSpec((count, lanes), lambda step, place=place: (0, place(step))) for place in places
        ]
        + [whole((count, D))],
        out_specs=pl.BlockSpec((taken, width, D), lambda step: (step, 0, 0)),
        out_shape=jax.ShapeDtypeStruct((shards, width, D), BF16),
        compiler_params=params(),
        cost_estimate=cost(2 * count * D * FF, 2 * count * FF + 2 * D * FF),
        name="outer_weights",
    )(*[active] * len(places), weighed)
    if width % LANES:
        out = jnp.concatenate([out[k : k + 1] for k in around(shards)], axis=0)
    return out


def inner_weights_kernel(rows_ref, joined_ref, out_ref, turned):
    @pl.when(pl.program_id(0) == 0)
    def _():
        turned[...] = rows_ref[...].T

    shards, _, share, _ = out_ref.shape
    for half in range(2):
        grads = dot(turned[...], joined_ref[half]).astype(BF16)
        for k in range(shards):
            out_ref[position(shards, k), half] = grads[k * share : (k + 1) * share]


def inner_weights(rows, joined, shards):
    count = rows.shape[0]
    width = 2 * BLOCK
    share = D // shards
    return pl.pallas_call(
        inner_weights_kernel,
        grid=(FF // width,),
        in_specs=[
            pl.BlockSpec((count, D), lambda step: (0, 0)),
            pl.BlockSpec((2, count, width), lambda step: (0, 0, step)),
        ],
        out_specs=pl.BlockSpec((shards, 2, share, width), lambda step: (0, 0, 0, step)),
        out_shape=jax.ShapeDtypeStruct((shards, 2, share, FF), BF16),
        scratch_shapes=[pltpu.VMEM((D, count), BF16)],
        compiler_params=params(),
        cost_estimate=cost(4 * count * D * FF, 4 * count * FF + 4 * D * FF),
        name="inner_weights",
    )(rows, joined)


def expert_backward_kernel(joined_ref, inner_ref, grads_ref, total):
    step = pl.program_id(0)
    part = dot(joined_ref[0], read_inner(inner_ref), NT)
    total[...] = jnp.where(step == 0, part, total[...] + part)

    @pl.when(step == pl.num_programs(0) - 1)
    def _():
        grads_ref[...] = total[...].astype(BF16)


def expert_backward(joined, inner):
    count = joined.shape[1]
    pieces = 4
    width = pieces * BLOCK
    half = FF // width
    return pl.pallas_call(
        expert_backward_kernel,
        grid=(2 * half,),
        in_specs=[
            pl.BlockSpec((1, count, width), lambda step: (step // half, 0, step % half)),
            inner_spec(inner, pieces, lambda step: step),
        ],
        out_specs=whole((count, D)),
        out_shape=jax.ShapeDtypeStruct((count, D), BF16),
        scratch_shapes=[pltpu.VMEM((count, D), F32)],
        compiler_params=params(),
        cost_estimate=cost(4 * count * D * FF, 4 * count * FF + 4 * D * FF),
        name="expert_backward",
    )(joined, inner)


def mix_kernel(
    returned_ref,
    targets_ref,
    table_ref,
    middle_ref,
    normed_ref,
    small_ref,
    out_ref,
    *,
    value_place,
    constant_count,
):
    block = middle_ref.shape[0]
    slots = returned_ref.shape[0]
    table = table_ref[...]
    columns = iota((block, slots), 1)
    lane = iota((block, LANES), 1)
    blended = normed_ref[...].astype(F32) * table[:, COEF : COEF + 1]
    for route in range(2):
        hot = jnp.where(columns == targets_ref[:, route : route + 1], 1.0, 0.0).astype(BF16)
        paired = dot(hot, returned_ref[...])
        blended = blended + table[:, CHOSEN + route : CHOSEN + route + 1] * paired
    values = jnp.zeros((block, LANES), F32)
    for which in range(constant_count):
        place = BETA + which
        values = jnp.where(lane == value_place + which, table[:, place : place + 1], values)
    upper = values.astype(BF16)
    lower = (values - upper.astype(F32)).astype(BF16)
    blended = blended + (dot(upper, small_ref[...], NT) + dot(lower, small_ref[...], NT))
    out_ref[...] = (middle_ref[...] + blended).astype(BF16)


def mix_branches(returned, targets, table, middle, normed, gathered, value_place, constant_count):
    block = TOKENS["mix"]
    tokens = middle.shape[0]
    slots = returned.shape[0]
    token_block = lambda width: pl.BlockSpec((block, width), lambda step: (step, 0))
    return pl.pallas_call(
        functools.partial(mix_kernel, value_place=value_place, constant_count=constant_count),
        grid=(tokens // block,),
        in_specs=[
            whole((slots, D)),
            token_block(2),
            token_block(LANES),
            token_block(D),
            token_block(D),
            pl.BlockSpec((D, LANES), lambda step: (0, 4 * D // LANES)),
        ],
        out_specs=token_block(D),
        out_shape=jax.ShapeDtypeStruct((tokens, D), BF16),
        compiler_params=params(62),
        cost_estimate=cost(4 * tokens * D * slots, 12 * tokens * D),
        name="mix_branches",
    )(returned, targets, table, middle, normed, gathered)


def middle_kernel(
    core_ref,
    returned_ref,
    met_ref,
    targets_ref,
    routes_ref,
    prior_ref,
    table_ref,
    middle_ref,
    normed_ref,
    upstream_ref,
    attended_ref,
    small_ref,
    gain_ref,
    weight_ref,
    grad_middle_ref,
    grad_attended_ref,
    mixer_ref,
    *refs,
    experts,
    constant_count,
):
    weight_refs, (work, grad_gain, grad_small, grad_weight) = refs[:-4], refs[-4:]
    block = middle_ref.shape[0]
    slots = returned_ref.shape[0]
    kinds = prior_ref.shape[0]
    gates = 2 * constant_count
    first = pl.program_id(0) == 0
    table = table_ref[...]
    wide = upstream_ref[...].astype(F32)
    columns = iota((block, slots), 1)
    hot = jnp.where(columns == targets_ref[:, 0:1], 1.0, 0.0) + jnp.where(
        columns == targets_ref[:, 1:2], 1.0, 0.0
    )
    hot = hot.astype(BF16)
    total = dot(hot, returned_ref[...]) + wide * table[:, COEF : COEF + 1]
    met = met_ref[...]
    upper = met.astype(BF16).astype(F32)
    here = iota((LANES, slots), 1) // (slots // experts) == iota((LANES, slots), 0) % experts
    halves = jnp.where(iota((LANES, slots), 0) < experts, upper, met - upper)
    met = jnp.where(jnp.logical_and(here, iota((LANES, slots), 0) < 2 * experts), halves, 0.0)
    met = dot(hot, met.astype(BF16), NT)
    met = met.T
    turned = table.T
    probs = turned[PROBS : PROBS + kinds]
    places = iota((kinds, block), 0)
    met = met[:experts] + met[experts : 2 * experts]
    work[...] = jnp.zeros_like(work)
    work[:experts] = met
    weighed = work[:kinds]
    for route in range(2):
        rest = turned[REST + route : REST + route + 1]
        weighed = weighed + jnp.where(places == routes_ref[route : route + 1, :], rest, 0.0)
    grad_logits = weighed - probs * jnp.sum(weighed, axis=0, keepdims=True)
    part = lax.dot_general(
        prior_ref[...], grad_logits, NT, precision=highest, preferred_element_type=F32
    )
    mixer_ref[...] = jnp.where(first, part, mixer_ref[...] + part)
    work[:kinds] = grad_logits
    work[kinds : kinds + gates] = turned[GATE_GRAD : GATE_GRAD + gates]
    work[kinds + gates : kinds + gates + constant_count] = turned[BETA : BETA + constant_count]
    values = work[...].T
    upper = values.astype(BF16)
    lower = (values - upper.astype(F32)).astype(BF16)
    is_small = iota((block, LANES), 1) < kinds + gates
    nothing = jnp.zeros((block, LANES), BF16)
    total = total + (
        dot(jnp.where(is_small, upper, nothing), small_ref[...], NT)
        + dot(jnp.where(is_small, lower, nothing), small_ref[...], NT)
    )
    both = jnp.concatenate([upper, lower], axis=1)
    part = jnp.where(
        iota((1, 2 * LANES), 1) % LANES < kinds + gates,
        dot(normed_ref[...], both, TN),
        dot(upstream_ref[...], both, TN),
    )
    part = part[:, :LANES] + part[:, LANES:]
    grad_small[...] = jnp.where(first, part, grad_small[...] + part)

    scale = table[:, SCALE : SCALE + 1]
    unit = middle_ref[...] * scale
    part = jnp.sum(total * unit, axis=0, keepdims=True)
    grad_gain[...] = jnp.where(first, part, grad_gain[...] + part)
    inner = total * gain_ref[...]
    grad_middle = wide + scale * (inner - unit * jnp.mean(inner * unit, axis=1, keepdims=True))
    grad_middle_ref[...] = grad_middle
    rounded = grad_middle.astype(BF16)
    grad_attended_ref[...] = dot(rounded, weight_ref[...], NT).astype(BF16)
    part = dot(attended_ref[...], rounded, TN)
    grad_weight[:, :D] = jnp.where(first, part, grad_weight[:, :D] + part)

    @pl.when(pl.program_id(0) == pl.num_programs(0) - 1)
    def _():
        column = jnp.broadcast_to(grad_gain[...], (LANES, D)).T
        place = kinds + gates + constant_count
        grad_weight[:, D:] = jnp.where(iota((D, LANES), 1) == place, column, grad_small[...])
        if len(weight_refs) == 1:
            weight_refs[0][...] = grad_weight[...].astype(BF16)
        else:
            part_rows(grad_weight, core_ref[0], *weight_refs)


def middle_backward(
    core,
    returned,
    met,
    targets,
    routes,
    prior,
    table,
    middle,
    normed,
    upstream,
    attended,
    gain,
    gathered,
    experts,
    constant_count,
    shards,
):
    block = TOKENS["middle"]
    tokens = middle.shape[0]
    slots = returned.shape[0]
    kinds = prior.shape[0]
    rows = D // shards
    spec = lambda shape, place: pl.BlockSpec(shape, lambda step, core: place(step))
    always = lambda shape: spec(shape, lambda step: (0,) * len(shape))
    token_block = lambda width: spec((block, width), lambda step: (step, 0))
    token_lanes = lambda height: spec((height, block), lambda step: (0, step))
    if rows % 8:
        weights = [(D, D + LANES)]
    else:
        weights = [(shards // 2, rows, D + LANES)] * 2
    results = pl.pallas_call(
        functools.partial(middle_kernel, experts=experts, constant_count=constant_count),
        grid_spec=pltpu.PrefetchScalarGridSpec(
            num_scalar_prefetch=1,
            grid=(tokens // block,),
            in_specs=[
                always((slots, D)),
                always((1, slots)),
                token_block(2),
                token_lanes(2),
                token_lanes(kinds),
                token_block(LANES),
                token_block(D),
                token_block(D),
                token_block(D),
                token_block(D),
                spec((D, LANES), lambda step: (0, 4 * D // LANES)),
                always((1, D)),
                spec((D, D), lambda step: (0, 3)),
            ],
            out_specs=[token_block(D), token_block(D), always((kinds, kinds))]
            + [always(shape) for shape in weights],
            scratch_shapes=[
                pltpu.VMEM((LANES, block), F32),
                pltpu.VMEM((1, D), F32),
                pltpu.VMEM((D, LANES), F32),
                pltpu.VMEM((D, D + LANES), F32),
            ],
        ),
        out_shape=[
            jax.ShapeDtypeStruct((tokens, D), F32),
            jax.ShapeDtypeStruct((tokens, D), BF16),
            jax.ShapeDtypeStruct((kinds, kinds), F32),
        ]
        + [jax.ShapeDtypeStruct(shape, BF16) for shape in weights],
        compiler_params=params(62),
        cost_estimate=cost(2 * tokens * D * (slots + 2 * D), 18 * tokens * D),
        name="middle_backward",
    )(
        core,
        returned,
        met,
        targets,
        routes,
        prior,
        table,
        middle,
        normed,
        upstream,
        attended,
        gathered,
        gain,
        gathered,
    )
    return *results[:3], results[3:]


def input_kernel(packed_ref, weight_ref, hidden_ref, grad_middle_ref, gain_ref, out_ref, grad_gain_ref):
    total = sum(dot(packed_ref[c], weight_ref[:, c * D : (c + 1) * D], NT) for c in range(3))
    values = hidden_ref[...].astype(F32)
    scale = row_scale(values)
    unit = values * scale
    part = jnp.sum(total * unit, axis=0, keepdims=True)
    grad_gain_ref[...] = jnp.where(pl.program_id(0) == 0, part, grad_gain_ref[...] + part)
    inner = total * gain_ref[...]
    out_ref[...] = grad_middle_ref[...] + scale * (
        inner - unit * jnp.mean(inner * unit, axis=1, keepdims=True)
    )


def input_backward(grad_packed, gathered, hidden, grad_middle, gain):
    block = TOKENS['input']
    tokens = hidden.shape[0]
    token_block = lambda width: pl.BlockSpec((block, width), lambda step: (step, 0))
    return pl.pallas_call(
        input_kernel,
        grid=(tokens // block,),
        in_specs=[
            pl.BlockSpec((3, block, D), lambda step: (0, step, 0)),
            pl.BlockSpec((D, 3 * D), lambda step: (0, 0)),
            token_block(D),
            token_block(D),
            whole((1, D)),
        ],
        out_specs=[token_block(D), whole((1, D))],
        out_shape=[
            jax.ShapeDtypeStruct((tokens, D), F32),
            jax.ShapeDtypeStruct((1, D), F32),
        ],
        compiler_params=params(),
        cost_estimate=cost(6 * tokens * D * D, 16 * tokens * D),
        name="input_backward",
    )(grad_packed, gathered, hidden, grad_middle, gain)


def pair_targets(routes, priority, experts, total_kinds, capacity):
    kind_ids = jnp.arange(total_kinds, dtype=jnp.int32)
    hot = [(routes[:, k : k + 1] == kind_ids[None, :]).astype(F32) for k in range(2)]
    earlier = (priority[None, :] < priority[:, None]).astype(BF16)
    before = dot(earlier, (hot[0] + hot[1]).astype(BF16))
    slots = jnp.stack([jnp.sum(before * one, axis=1) for one in hot], axis=1).astype(jnp.int32)
    kept_pairs = jnp.logical_and(routes < experts, slots < capacity)
    return jnp.where(kept_pairs, routes * capacity + slots, experts * capacity)


def exchange(blocks, axis):
    return lax.all_to_all(blocks, axis, split_axis=0, concat_axis=0, tiled=True)


def exchange_apart(blocks, axis):
    count, me = lax.axis_size(axis), lax.axis_index(axis)
    out = jnp.zeros_like(blocks)
    for step in range(count):
        block = pick(blocks, (me + step) % count, 0)
        if step:
            block = lax.ppermute(block, axis, [(i, (i + step) % count) for i in range(count)])
        out = lax.dynamic_update_slice(out, block[None], ((me - step) % count,) + (0,) * block.ndim)
    return out


def flip(axis):
    return [(i, i ^ 1) for i in range(lax.axis_size(axis))]


def shift(axis, step):
    count = lax.axis_size(axis)
    return [(i, (i + 2 * step) % count) for i in range(count)]


def gather_far(mine):
    far, depth = lax.axis_size("dp") // 2, lax.axis_index("dp") // 2
    column = jnp.zeros((far, *mine.shape), mine.dtype)
    for step in range(far):
        came = mine if step == 0 else lax.ppermute(mine, "dp", shift("dp", step))
        column = lax.dynamic_update_slice(column, came[None], ((depth - step) % far, 0, 0))
    return column


def gather_all(column):
    far, rows, width = column.shape
    wide, side = lax.axis_size("expert") // 2, lax.axis_index("dp") % 2
    place, core = lax.axis_index("expert") // 2, lax.axis_index("expert") % 2
    near = [column, lax.ppermute(column, "dp", flip("dp"))]
    total = jnp.zeros((far, 2, wide, 2, rows, width), column.dtype)
    for step in range(wide):
        for other in range(2):
            piece = near[other]
            if step:
                piece = lax.ppermute(piece, "expert", shift("expert", step))
            twin = lax.ppermute(piece, "expert", flip("expert"))
            spot = (0, side ^ other, (place - step) % wide)
            shaped = (far, 1, 1, 1, rows, width)
            total = lax.dynamic_update_slice(total, piece.reshape(shaped), (*spot, core, 0, 0))
            total = lax.dynamic_update_slice(total, twin.reshape(shaped), (*spot, 1 - core, 0, 0))
    return total.reshape(-1, width)


def pick(array, index, axis):
    return lax.dynamic_index_in_dim(array, index, axis, keepdims=False)


def scatter_side(parted):
    wide = lax.axis_size("expert") // 2
    place, core = lax.axis_index("expert") // 2, lax.axis_index("expert") % 2
    if len(parted) == 1:
        terms = parted[0].reshape(lax.axis_size("dp") * wide, 2, -1, parted[0].shape[1])
        parted = (pick(terms, 1 - core, 1), pick(terms, core, 1))
    send, keep = parted
    came = lax.ppermute(send, "expert", flip("expert"))
    pair = (keep.astype(F32) + came.astype(F32)).astype(BF16)
    pair = pair.reshape(lax.axis_size("dp"), wide, *pair.shape[1:])
    total = pick(pair, place, 1).astype(F32)
    for step in range(1, wide):
        came = lax.ppermute(pick(pair, (place + step) % wide, 1), "expert", shift("expert", step))
        total = total + came.astype(F32)
    return total.astype(BF16)


def around(count):
    return list(range(0, count, 2)) + list(range(count - 1, 0, -2))


def position(count, place):
    return place // 2 if place % 2 == 0 else count - 1 - place // 2


def split_experts(expert_in, expert_out):
    inner, outer = expert_in[0].astype(BF16), expert_out[0].astype(BF16)
    if inner.shape[0] % 16 or outer.shape[0] != BLOCK:
        return [inner, outer]
    pieces = [
        array.reshape(array.shape[0], -1, BLOCK).transpose(1, 0, 2).reshape(-1, BLOCK)
        for array in (inner, outer)
    ]
    return [jnp.concatenate(pieces, axis=0)]


def gather_experts(pieces):
    ring = [around(lax.axis_size("dp"))]
    if len(pieces) == 1:
        both = lax.all_gather(pieces[0], "dp", axis=0, axis_index_groups=ring)
        return both, both
    return [lax.all_gather(piece, "dp", axis=0, tiled=True) for piece in pieces]


def scatter_expert(grads):
    ring = [around(lax.axis_size("dp"))]
    return lax.psum_scatter(grads, "dp", scatter_dimension=0, tiled=True, axis_index_groups=ring)[0]


def own_kernel(
    in_ref, shares_ref, inner_ref, outer_ref, gain_ref, mixer_ref, own_ref, out_ref, own_outer_ref, few_ref, *, kinds
):
    total = jnp.sum(in_ref[...].astype(F32), axis=0)
    out = jnp.sum(shares_ref[...].astype(F32), axis=0)
    for pair in range(D // PAIR):
        for part in range(3):
            low, place = (3 * pair + part) * PAIR, part * D + pair * PAIR
            own_ref[:, place : place + PAIR] = total[:, low : low + PAIR]
    out_ref[...] = out
    inner, outer = inner_ref[...].astype(F32), outer_ref[...].astype(F32)
    own_outer_ref[...] = outer
    width = few_ref.shape[2]
    square = jnp.sum(jnp.sum(inner * inner, axis=0), axis=(0, 1), keepdims=True)
    for member in (total, out, outer):
        square = square + jnp.sum(member * member, axis=(0, 1), keepdims=True)
    few = few_ref.at[0]
    few[...] = jnp.zeros_like(few)
    few[0:1, :D] = gain_ref[...]
    for row in range(kinds):
        place = D + row * kinds
        few[0:1, place : place + kinds] = mixer_ref[row : row + 1, :]
    few[0:1, width - LANES :] = jnp.broadcast_to(square, (1, LANES))
    row = few[...]
    for device in range(1, few_ref.shape[0]):
        few_ref[device] = row


def own_sums(in_shares, out_shares, inner, outer, grad_gain, grad_mixer, devices):
    kinds = grad_mixer.shape[0]
    width = D + (-(-kinds * kinds // LANES) + 1) * LANES
    rows = in_shares.shape[1]
    return pl.pallas_call(
        functools.partial(own_kernel, kinds=kinds),
        out_shape=[
            jax.ShapeDtypeStruct((rows, 3 * D), F32),
            jax.ShapeDtypeStruct((rows, D + LANES), F32),
            jax.ShapeDtypeStruct(outer.shape, F32),
            jax.ShapeDtypeStruct((devices, 1, width), F32),
        ],
        compiler_params=params(62),
        cost_estimate=cost(6 * D * FF, 3 * D * FF),
        name="own_sums",
    )(in_shares, out_shares, inner, outer, grad_gain, grad_mixer)


def adam(master, first, second, grad, factor, step_rate):
    clipped = grad * factor
    first_new = beta_moment * first + (1.0 - beta_moment) * clipped
    second_new = beta_moment * second + (1.0 - beta_moment) * clipped * clipped
    correct = 1.0 - beta_moment**step_number
    update = (
        first_new / correct / (jnp.sqrt(second_new / correct) + adam_epsilon) + decay_rate * master
    )
    return (master - step_rate * update, first_new, second_new)


def update_kernel(*refs, kinds, constant_count):
    index_ref, few_ref, in_ref, out_ref, inner_ref, outer_ref = refs[:6]
    states = [refs[6 + 3 * which : 9 + 3 * which] for which in range(8)]
    norm_ref, results = refs[30], refs[31:]
    width = out_ref.shape[1]
    few = jnp.sum(few_ref[...], axis=0)
    gain_total = few[:, :D]
    mixer_total = few[:, D : D + kinds * kinds]
    square = (
        few[:, few.shape[1] - 1 :]
        + jnp.sum(gain_total * gain_total, axis=1, keepdims=True)
        + jnp.sum(mixer_total * mixer_total, axis=1, keepdims=True)
    )
    norm = jnp.sqrt(square)
    factor = clip_limit / jnp.maximum(norm, clip_limit)
    places = iter(results)
    slots = [[next(places) for _ in range(4 if which in (0, 7) else 5)] for which in range(8)]

    def step(which, grad):
        master, first, second = states[which]
        outs = slots[which]
        if len(outs) == 5:
            outs[0][...] = grad.reshape(outs[0].shape)
            outs = outs[1:]
        shape = outs[0].shape
        lay = lambda value: value.reshape(grad.shape)
        new = adam(lay(master[...]), lay(first[...]), lay(second[...]), grad, factor, learn_rates[which])
        for ref, value in zip(outs, new + (new[0],)):
            ref[...] = value.reshape(shape).astype(ref.dtype)

    step(6, inner_ref[0].astype(F32))
    step(7, outer_ref[...])

    @pl.when(pl.program_id(0) == 0)
    def _():
        norm_ref[...] = norm
        step(0, in_ref[...])
        step(1, out_ref[:, :D])
        rows = out_ref.shape[0]
        narrow = jnp.pad(out_ref[:, D:], ((0, LANES - rows), (0, 0))).T
        step(2, narrow[:kinds, :rows])
        step(3, jnp.concatenate([mixer_total[:, k * kinds : (k + 1) * kinds] for k in range(kinds)], axis=0))
        small = kinds + 3 * constant_count
        step(4, narrow[kinds:small, :rows])
        start = index_ref[0] * rows
        picked = (iota((D, LANES), 0) == start + iota((D, LANES), 1)).astype(F32)
        own = lax.dot_general(
            jnp.broadcast_to(gain_total, (8, D)), picked, NN, precision=highest, preferred_element_type=F32
        )
        step(5, jnp.concatenate([own[0:1, :rows], narrow[small : small + 1, :rows]], axis=0))


def update(index, few, in_own, out_own, inner_own, outer_own, states, kinds, constant_count):
    steps = 2
    turn = lambda which, array: array.T if which in (2, 4) else array
    states = [[turn(which, array) for array in state] for which, state in enumerate(states)]
    half = steps // 2
    flat = [array for state in states for array in state]

    def spec(shape):
        if len(shape) == 3 and shape[2] == 2 * FF:
            return pl.BlockSpec((1, shape[1], shape[2] // steps), lambda step, index: (0, 0, step))
        if len(shape) == 3:
            return pl.BlockSpec((1, shape[1] // steps, shape[2]), lambda step, index: (0, step, 0))
        return pl.BlockSpec(shape, lambda step, index: (0, 0))

    out_shape = [jax.ShapeDtypeStruct((1, 1), F32)]
    for which in range(8):
        shape = states[which][0].shape
        kept = 3 if which in (0, 7) else 4
        out_shape += [jax.ShapeDtypeStruct(shape, F32)] * kept + [jax.ShapeDtypeStruct(shape, BF16)]
    results = pl.pallas_call(
        functools.partial(update_kernel, kinds=kinds, constant_count=constant_count),
        grid_spec=pltpu.PrefetchScalarGridSpec(
            num_scalar_prefetch=1,
            grid=(steps,),
            in_specs=[
                pl.BlockSpec(few.shape, lambda step, index: (0, 0, 0)),
                spec(in_own.shape),
                spec(out_own.shape),
                pl.BlockSpec(
                    (1, inner_own.shape[1], FF // half), lambda step, index: (step // half, 0, step % half)
                ),
                pl.BlockSpec((outer_own.shape[0] // steps, D), lambda step, index: (step, 0)),
            ]
            + [spec(array.shape) for array in flat],
            out_specs=[spec(leaf.shape) for leaf in out_shape],
        ),
        out_shape=out_shape,
        compiler_params=params(),
        cost_estimate=cost(40 * D * FF, 60 * D * FF // 2),
        name="update",
    )(index, few, in_own, out_own, inner_own, outer_own, *flat)
    norm, rest = results[0].reshape(()), list(results[1:])
    grads = {0: in_own, 7: outer_own[None]}
    ordered = []
    for which in range(8):
        taken = 4 if which in grads else 5
        ordered += [grads[which]] if which in grads else []
        ordered += [turn(which, array) for array in rest[:taken]]
        rest = rest[taken:]
    return norm, ordered


def body(
    hidden_in,
    gate_prior,
    routes,
    priority,
    segments,
    cotangent,
    attend_in,
    first_attend_in,
    second_attend_in,
    attend_out,
    first_attend_out,
    second_attend_out,
    router,
    first_router,
    second_router,
    gate_mix,
    first_gate_mix,
    second_gate_mix,
    constants,
    first_constants,
    second_constants,
    norm_gains,
    first_norm_gains,
    second_norm_gains,
    expert_in,
    first_expert_in,
    second_expert_in,
    expert_out,
    first_expert_out,
    second_expert_out,
):
    groups = lax.axis_size("expert")
    devices = lax.axis_size("dp") * groups
    kinds = gate_prior.shape[1]
    constant_count = constants.shape[1] // 3
    experts = kinds - 2 - constant_count
    token_count = hidden_in.shape[0]
    width_top = routes.shape[1]
    capacity = max(2, width_top * token_count // kinds // 8 * 8)
    slots = experts * capacity
    small_width = kinds + 3 * constant_count
    gate_end = kinds + 2 * constant_count

    expert_pieces = split_experts(expert_in, expert_out)
    mine = jnp.concatenate(
        [
            attend_in,
            attend_out,
            router,
            constants,
            norm_gains.T,
            jnp.zeros((attend_in.shape[0], LANES - small_width - 2), F32),
        ],
        axis=1,
    ).astype(BF16)
    targets = pair_targets(routes, priority[0], experts, kinds, capacity)
    target_rows = targets.T
    split = (groups, slots // groups, -1)
    placed = place_rows(cotangent, target_rows, slots).reshape(split)
    mine, expert_pieces = lax.optimization_barrier((mine, expert_pieces))
    column = gather_far(mine)
    column, placed, expert_pieces = lax.optimization_barrier((column, placed, expert_pieces))
    gathered = gather_all(column)
    expert_inner, expert_outer = gather_experts(expert_pieces)
    gains = gathered[:, 4 * D + small_width : 4 * D + small_width + 2].astype(F32).T
    gains, placed = lax.optimization_barrier((gains, placed))
    gain_first, gain_second = gains[0:1], gains[1:2]
    arrived_grad = exchange(placed, "expert").reshape(slots, D)
    route_rows = routes.T
    prior_rows = gate_prior.T
    extra = jnp.dot(gate_mix.astype(BF16).astype(F32).T, prior_rows, precision=highest)
    seg_row = segments
    seg_column = segments.reshape(token_count, 1)

    normed_first, packed, attended, logsum = attend_forward(
        hidden_in, gain_first, gathered, seg_column, seg_row
    )
    middle, normed_second, table, rows = route_tokens(
        hidden_in,
        attended,
        cotangent,
        extra,
        route_rows,
        target_rows,
        gain_second,
        gathered,
        experts,
        constant_count,
        slots,
    )
    arrived = exchange(rows.reshape(split), "expert").reshape(slots, D + LANES)
    grad_joined, active, produced, met, weighed = expert_forward(
        arrived, arrived_grad, expert_inner, expert_outer
    )
    outer_own = scatter_expert(outer_weights(active, weighed, lax.axis_size("dp")))
    met = exchange(met.reshape(groups, 1, slots // groups), "expert").reshape(1, slots)
    grad_rows = expert_backward(grad_joined, expert_inner)
    met, grad_rows, grad_joined = lax.optimization_barrier((met, grad_rows, grad_joined))
    grad_returned = exchange(grad_rows.reshape(split), "expert").reshape(slots, D)
    grad_inner = inner_weights(arrived, grad_joined, lax.axis_size("dp"))
    grad_returned, produced, grad_inner = lax.optimization_barrier((grad_returned, produced, grad_inner))
    inner_own = scatter_expert(grad_inner)
    core = (lax.axis_index("expert") % 2).reshape(1).astype(jnp.int32)
    grad_middle, grad_attended, grad_mixer, grad_out_and_small = middle_backward(
        core,
        grad_returned,
        met,
        targets,
        route_rows,
        prior_rows,
        table,
        middle,
        normed_second,
        cotangent,
        attended,
        gain_second,
        gathered,
        experts,
        constant_count,
        devices,
    )
    out_sum = scatter_side(grad_out_and_small)

    grad_packed, grad_weight_in = attend_backward(
        core, packed, grad_attended, logsum, seg_column, seg_row, normed_first, devices
    )
    grad_weight_in, out_sum = lax.optimization_barrier((grad_weight_in, out_sum))
    in_sum = scatter_side(grad_weight_in)
    out_shares = exchange(out_sum, "dp")
    in_sum, out_shares, produced = lax.optimization_barrier((in_sum, out_shares, produced))
    returned = exchange_apart(produced.reshape(split), "expert").reshape(slots, D)
    in_shares = exchange(in_sum, "dp")
    input_grad, grad_gain_first = input_backward(
        grad_packed, gathered, hidden_in, grad_middle, gain_first
    )
    activations = mix_branches(
        returned, targets, table, middle, normed_second, gathered, gate_end, constant_count
    )

    in_own, out_own, outer_own, few = own_sums(
        in_shares, out_shares, inner_own, outer_own, grad_gain_first, grad_mixer, devices
    )
    few = exchange(few, BOTH)
    index = lax.axis_index("dp") * groups + lax.axis_index("expert")
    states = (
        (attend_in, first_attend_in, second_attend_in),
        (attend_out, first_attend_out, second_attend_out),
        (router, first_router, second_router),
        (gate_mix, first_gate_mix, second_gate_mix),
        (constants, first_constants, second_constants),
        (norm_gains, first_norm_gains, second_norm_gains),
        (expert_in, first_expert_in, second_expert_in),
        (expert_out, first_expert_out, second_expert_out),
    )
    grad_norm, updated = update(
        index.reshape(1).astype(jnp.int32),
        few,
        in_own,
        out_own,
        inner_own,
        outer_own,
        states,
        kinds,
        constant_count,
    )
    return (activations, input_grad, grad_norm, *updated)


def solution(mesh):
    in_specs = (
        P(("dp", "expert"), None),
        P(("dp", "expert"), None),
        P(("dp", "expert"), None),
        P(("dp", "expert"), None),
        P(("dp", "expert"), None),
        P(("dp", "expert"), None),
        P(("dp", "expert"), None),
        P(("dp", "expert"), None),
        P(("dp", "expert"), None),
        P(("dp", "expert"), None),
        P(("dp", "expert"), None),
        P(("dp", "expert"), None),
        P(("dp", "expert"), None),
        P(("dp", "expert"), None),
        P(("dp", "expert"), None),
        P(),
        P(),
        P(),
        P(("dp", "expert"), None),
        P(("dp", "expert"), None),
        P(("dp", "expert"), None),
        P(None, ("dp", "expert")),
        P(None, ("dp", "expert")),
        P(None, ("dp", "expert")),
        P("expert", "dp", None),
        P("expert", "dp", None),
        P("expert", "dp", None),
        P("expert", "dp", None),
        P("expert", "dp", None),
        P("expert", "dp", None),
    )
    out_specs = (
        P(("dp", "expert"), None),
        P(("dp", "expert"), None),
        P(),
        P(("dp", "expert"), None),
        P(("dp", "expert"), None),
        P(("dp", "expert"), None),
        P(("dp", "expert"), None),
        P(("dp", "expert"), None),
        P(("dp", "expert"), None),
        P(("dp", "expert"), None),
        P(("dp", "expert"), None),
        P(("dp", "expert"), None),
        P(("dp", "expert"), None),
        P(("dp", "expert"), None),
        P(("dp", "expert"), None),
        P(("dp", "expert"), None),
        P(("dp", "expert"), None),
        P(("dp", "expert"), None),
        P(),
        P(),
        P(),
        P(),
        P(),
        P(("dp", "expert"), None),
        P(("dp", "expert"), None),
        P(("dp", "expert"), None),
        P(("dp", "expert"), None),
        P(("dp", "expert"), None),
        P(None, ("dp", "expert")),
        P(None, ("dp", "expert")),
        P(None, ("dp", "expert")),
        P(None, ("dp", "expert")),
        P(None, ("dp", "expert")),
        P("expert", "dp", None),
        P("expert", "dp", None),
        P("expert", "dp", None),
        P("expert", "dp", None),
        P("expert", "dp", None),
        P("expert", "dp", None),
        P("expert", "dp", None),
        P("expert", "dp", None),
        P("expert", "dp", None),
        P("expert", "dp", None),
    )
    return jax.shard_map(body, mesh=mesh, in_specs=in_specs, out_specs=out_specs, check_vma=False)
```

```python
import functools

import jax
import jax.numpy as jnp
from jax import lax
from jax.experimental import pallas as pl
from jax.experimental.pallas import tpu as pltpu
from jax.sharding import PartitionSpec as P

D = 768
FF = 2048
HEAD_DIM = 64
PAIR = 2 * HEAD_DIM
BLOCK = 256
LANES = 128
TOKENS = {'route': 512, 'mix': 512, 'middle': 512, 'input': 512}
BOTH = ("dp", "expert")

norm_epsilon = 1e-05
adam_epsilon = 1e-08
learn_rates = (0.01, 0.04, 0.01, 0.03, 0.01, 0.1, 0.01, 0.01)
decay_rate = 0.1
beta_moment = 0.5
step_number = 4.0
clip_limit = 1.0
score_scale = 0.125
masked_score = -1e30
highest = lax.Precision.HIGHEST
F32 = jnp.float32
BF16 = jnp.bfloat16

NN = (((1,), (0,)), ((), ()))
NT = (((1,), (1,)), ((), ()))
TN = (((0,), (0,)), ((), ()))

CHOSEN, COEF, SCALE, REST, BETA, GATE_GRAD, PROBS = 0, 2, 3, 4, 8, 16, 32
PIECES = 3
HINT = 64


def dot(left, right, form=NN):
    return lax.dot_general(left, right, form, preferred_element_type=F32)


def iota(shape, dim):
    return lax.broadcasted_iota(jnp.int32, shape, dim)


def row_scale(values):
    return lax.rsqrt(jnp.mean(values * values, axis=-1, keepdims=True) + norm_epsilon)


def params(mebibytes=56):
    return pltpu.CompilerParams(vmem_limit_bytes=mebibytes << 20)


def whole(shape):
    return pl.BlockSpec(shape, lambda *step: (0,) * len(shape))


def cost(flops, moved, transcendentals=0):
    share = HINT
    return pl.CostEstimate(
        flops=flops // share, bytes_accessed=moved // share, transcendentals=transcendentals // share
    )


def fill_bias(seg_column_ref, seg_row_ref, bias_ref, block):
    length = bias_ref.shape[0]
    for low in range(0, length, block):
        high = low + block
        columns = low + iota((high, block), 1)
        allowed = jnp.logical_and(
            seg_column_ref[:high, :] == seg_row_ref[:, low:high], iota((high, block), 0) <= columns
        )
        bias_ref[:high, low:high] = jnp.where(allowed, 0.0, masked_score)


def attend_forward_kernel(
    hidden_ref,
    gain_ref,
    query_weight_ref,
    key_weight_ref,
    value_weight_ref,
    seg_column_ref,
    seg_row_ref,
    normed_ref,
    packed_ref,
    out_ref,
    logsum_ref,
    bias_ref,
):
    length, block = hidden_ref.shape[0], BLOCK

    @pl.when(pl.program_id(0) == 0)
    def _():
        fill_bias(seg_column_ref, seg_row_ref, bias_ref, block)
        values = hidden_ref[...].astype(F32)
        normed_ref[...] = (values * row_scale(values) * gain_ref[...]).astype(BF16)

    weights = jnp.concatenate([query_weight_ref[...], key_weight_ref[...], value_weight_ref[...]], axis=1)
    packed = dot(normed_ref[...], weights).astype(BF16)
    for part in range(3):
        packed_ref[part] = packed[:, part * PAIR : (part + 1) * PAIR]
    for low in range(0, length, block):
        high = low + block
        for head in range(2):
            lanes = slice(head * HEAD_DIM, (head + 1) * HEAD_DIM)
            queries = packed_ref[0, low:high, lanes] * score_scale
            scores = dot(packed_ref[1, :high, lanes], queries, NT) + bias_ref[:high, low:high]
            maximum = jnp.max(scores, axis=0, keepdims=True)
            powers = jnp.exp(scores - maximum)
            totals = jnp.sum(powers, axis=0, keepdims=True)
            chances = (powers * (1.0 / totals)).astype(BF16)
            out_ref[low:high, lanes] = dot(chances, packed_ref[2, :high, lanes], TN).astype(BF16)
            logsum_ref[0, head : head + 1, low:high] = maximum + jnp.log(totals)


def attend_forward(hidden, gain, gathered, seg_column, seg_row):
    length = hidden.shape[0]
    pairs = D // PAIR
    return pl.pallas_call(
        attend_forward_kernel,
        grid=(pairs,),
        in_specs=[
            whole((length, D)),
            whole((1, D)),
            pl.BlockSpec((D, PAIR), lambda pair: (0, pair)),
            pl.BlockSpec((D, PAIR), lambda pair: (0, pairs + pair)),
            pl.BlockSpec((D, PAIR), lambda pair: (0, 2 * pairs + pair)),
            whole((length, 1)),
            whole((1, length)),
        ],
        out_specs=[
            whole((length, D)),
            pl.BlockSpec((3, length, PAIR), lambda pair: (0, 0, pair)),
            pl.BlockSpec((length, PAIR), lambda pair: (0, pair)),
            pl.BlockSpec((1, 2, length), lambda pair: (pair, 0, 0)),
        ],
        out_shape=[
            jax.ShapeDtypeStruct((length, D), BF16),
            jax.ShapeDtypeStruct((3, length, D), BF16),
            jax.ShapeDtypeStruct((length, D), BF16),
            jax.ShapeDtypeStruct((pairs, 2, length), F32),
        ],
        scratch_shapes=[pltpu.VMEM((length, length), F32)],
        compiler_params=params(),
        cost_estimate=cost(8 * length * length * D, 8 * length * D, length * length * 8),
        name="attend_forward",
    )(hidden, gain, gathered, gathered, gathered, seg_column, seg_row)


def part_rows(total, core, send_ref, keep_ref):
    rows = send_ref.shape[1]
    for k in range(send_ref.shape[0]):
        for ref, which in ((keep_ref, core), (send_ref, 1 - core)):
            start = pl.multiple_of((2 * k + which) * rows, 8)
            ref[k] = total[pl.ds(start, rows), :].astype(BF16)


def attend_backward_kernel(
    core_ref,
    query_ref,
    key_ref,
    value_ref,
    grad_ref,
    logsum_ref,
    seg_column_ref,
    seg_row_ref,
    normed_ref,
    out_ref,
    *refs,
):
    weight_refs, (bias_ref, key_sum, value_sum, turned, total, kept) = refs[:-6], refs[-6:]
    pair = pl.program_id(0)
    length, block = seg_row_ref.shape[1], BLOCK

    @pl.when(pl.program_id(0) == 0)
    def _():
        fill_bias(seg_column_ref, seg_row_ref, bias_ref, block)
        turned[...] = normed_ref[...].T

    def lanes(head):
        return slice(head * HEAD_DIM, (head + 1) * HEAD_DIM)

    def scores(low, head):
        high, here = low + block, lanes(head)
        queries = query_ref[0, low:high, here] * score_scale
        return (
            dot(key_ref[0, :high, here], queries, NT),
            dot(value_ref[0, :high, here], grad_ref[low:high, here], NT),
        )

    def chances(low, head, raw, grad_weights):
        high = low + block
        weights = jnp.exp(raw + bias_ref[:high, low:high] - logsum_ref[0, head : head + 1, low:high])
        centred = jnp.sum(weights * grad_weights, axis=0, keepdims=True)
        return weights.astype(BF16), (weights * (grad_weights - centred)).astype(BF16)

    def gradients(low, head, weights, grad_raw):
        high, here = low + block, lanes(head)
        grad_values = dot(weights, grad_ref[low:high, here])
        grad_keys = dot(grad_raw, query_ref[0, low:high, here] * score_scale)
        if high == length:
            key_sum[:, here] = grad_keys
            value_sum[:, here] = grad_values
        else:
            key_sum[:high, here] += grad_keys
            value_sum[:high, here] += grad_values
        keys = key_ref[0, :high, here] * score_scale
        out_ref[0, low:high, here] = dot(keys, grad_raw, TN).T.astype(BF16)

    blocks = [(low, head) for low in reversed(range(0, length, block)) for head in range(2)]
    ready, before = scores(*blocks[0]), None
    for index, place in enumerate(blocks):
        after = scores(*blocks[index + 1]) if index + 1 < len(blocks) else None
        now = chances(*place, *ready)
        if before is not None:
            gradients(*before)
        before, ready = (*place, *now), after
    gradients(*before)
    out_ref[1] = key_sum[...].astype(BF16)
    out_ref[2] = value_sum[...].astype(BF16)
    for part in range(3):
        kept[pair % 2, part] = out_ref[part]

    @pl.when(pair % 2 == 1)
    def _():
        both = jnp.concatenate([kept[which, part] for which in range(2) for part in range(3)], axis=1)
        weights = dot(turned[...], both)
        if len(weight_refs) == 1:
            weight_refs[0][...] = weights.astype(BF16)
        else:
            total[...] = weights
            part_rows(total, core_ref[0], *weight_refs)


def attend_backward(core, packed, grad, logsum, seg_column, seg_row, normed, shards):
    length = packed.shape[1]
    pairs = D // PAIR
    rows = D // shards
    spec = lambda shape, place: pl.BlockSpec(shape, lambda pair, core: place(pair))
    always = lambda shape: spec(shape, lambda pair: (0,) * len(shape))
    if rows % 8:
        weight_specs = [spec((D, 6 * PAIR), lambda pair: (0, pair // 2))]
        weight_shapes = [jax.ShapeDtypeStruct((D, 3 * D), BF16)]
    else:
        weight_specs = [spec((shards // 2, rows, 6 * PAIR), lambda pair: (0, 0, pair // 2))] * 2
        weight_shapes = [jax.ShapeDtypeStruct((shards // 2, rows, 3 * D), BF16)] * 2
    results = pl.pallas_call(
        attend_backward_kernel,
        grid_spec=pltpu.PrefetchScalarGridSpec(
            num_scalar_prefetch=1,
            grid=(pairs,),
            in_specs=[
                spec((1, length, PAIR), lambda pair: (0, 0, pair)),
                spec((1, length, PAIR), lambda pair: (1, 0, pair)),
                spec((1, length, PAIR), lambda pair: (2, 0, pair)),
                spec((length, PAIR), lambda pair: (0, pair)),
                spec((1, 2, length), lambda pair: (pair, 0, 0)),
                always((length, 1)),
                always((1, length)),
                always((length, D)),
            ],
            out_specs=[spec((3, length, PAIR), lambda pair: (0, 0, pair)), *weight_specs],
            scratch_shapes=[
                pltpu.VMEM((length, length), F32),
                pltpu.VMEM((length, PAIR), F32),
                pltpu.VMEM((length, PAIR), F32),
                pltpu.VMEM((D, length), BF16),
                pltpu.VMEM((D, 6 * PAIR), F32),
                pltpu.VMEM((2, 3, length, PAIR), BF16),
            ],
        ),
        out_shape=[jax.ShapeDtypeStruct((3, length, D), BF16), *weight_shapes],
        compiler_params=params(),
        cost_estimate=cost(20 * length * length * D, 14 * length * D, length * length * 8),
        name="attend_backward",
    )(core, packed, packed, packed, grad, logsum, seg_column, seg_row, normed)
    return results[0], results[1:]


def route_kernel(
    hidden_ref,
    attended_ref,
    upstream_ref,
    extra_ref,
    routes_ref,
    targets_ref,
    gain_ref,
    weight_ref,
    small_ref,
    middle_ref,
    normed_ref,
    table_ref,
    rows_ref,
    normed_all,
    first_all,
    second_all,
    work,
    *,
    token_steps,
    experts,
    constant_count,
    slot_block,
):
    step = pl.program_id(0)
    block = hidden_ref.shape[0]
    kinds = extra_ref.shape[0]
    gate_end = kinds + 2 * constant_count

    @pl.when(step < token_steps)
    def _():
        middle = hidden_ref[...].astype(F32) + dot(attended_ref[...], weight_ref[...])
        scale = row_scale(middle)
        normed = (middle * scale * gain_ref[...]).astype(BF16)
        middle_ref[...] = middle
        normed_ref[...] = normed
        upstream = upstream_ref[...]
        wide = upstream.astype(F32)
        inner = jnp.sum(wide * normed.astype(F32), axis=1, keepdims=True)
        lane = iota((block, LANES), 1)
        small = jnp.where(lane >= gate_end, dot(upstream, small_ref[...]), dot(normed, small_ref[...]))
        small = jnp.where(lane == LANES - 1, inner, jnp.where(lane == LANES - 2, scale, small)).T
        inner = small[LANES - 1 : LANES]
        logits = small[:kinds] + extra_ref[...]
        powers = jnp.exp(logits - jnp.max(logits, axis=0, keepdims=True))
        probs = powers / jnp.sum(powers, axis=0, keepdims=True)
        places = iota((kinds, block), 0)
        work[...] = jnp.zeros_like(work)
        work[PROBS : PROBS + kinds] = probs
        work[SCALE : SCALE + 1] = small[LANES - 2 : LANES - 1]
        shares = []
        for which in range(constant_count):
            left = small[kinds + 2 * which : kinds + 2 * which + 1]
            right = small[kinds + 2 * which + 1 : kinds + 2 * which + 2]
            top = jnp.maximum(left, right)
            left, right = jnp.exp(left - top), jnp.exp(right - top)
            both = left + right
            shares.append((left / both, right / both))
        met = [small[gate_end + which : gate_end + which + 1] for which in range(constant_count)]
        nothing = jnp.zeros((1, block), F32)
        coef = nothing
        betas = [nothing] * constant_count
        amounts = [nothing] * constant_count
        for route in range(2):
            kind = routes_ref[route : route + 1, :]
            chosen = jnp.sum(jnp.where(places == kind, probs, 0.0), axis=0, keepdims=True)
            work[CHOSEN + route : CHOSEN + route + 1] = chosen
            part = jnp.where(kind == experts + 1, 1.0, 0.0)
            rest = nothing
            for which in range(constant_count):
                here = kind == experts + 2 + which
                part = part + jnp.where(here, shares[which][0], 0.0)
                rest = rest + jnp.where(here, shares[which][1] * met[which], 0.0)
                betas[which] = betas[which] + jnp.where(here, chosen * shares[which][1], 0.0)
                amounts[which] = amounts[which] + jnp.where(here, chosen, 0.0)
            coef = coef + chosen * part
            work[REST + route : REST + route + 1] = chosen * (rest + part * inner)
        work[COEF : COEF + 1] = coef
        for which in range(constant_count):
            work[BETA + which : BETA + which + 1] = betas[which]
            grad_left = amounts[which] * inner
            grad_right = amounts[which] * met[which]
            mean = shares[which][0] * grad_left + shares[which][1] * grad_right
            place = GATE_GRAD + 2 * which
            work[place : place + 1] = shares[which][0] * (grad_left - mean)
            work[place + 1 : place + 2] = shares[which][1] * (grad_right - mean)
        table = work[...].T
        table_ref[...] = table
        rows = pl.ds(pl.multiple_of(step * block, block), block)
        normed_all[rows, :] = normed
        for route, kept in enumerate((first_all, second_all)):
            rest = jnp.broadcast_to(table[:, CHOSEN + route : CHOSEN + route + 1], (block, LANES))
            pieces = jnp.zeros((block, LANES), F32)
            for piece in range(PIECES):
                upper = rest.astype(BF16).astype(F32)
                pieces = jnp.where(lane == piece, upper, pieces)
                rest = rest - upper
            kept[rows, :] = pieces.astype(BF16)

    @pl.when(step >= token_steps)
    def _():
        tokens = normed_all.shape[0]
        slots = (step - token_steps) * slot_block + iota((slot_block, tokens), 0)
        first = jnp.where(slots == targets_ref[0:1, :], 1.0, 0.0)
        second = jnp.where(slots == targets_ref[1:2, :], 1.0, 0.0)
        rows_ref[:, :D] = dot((first + second).astype(BF16), normed_all[...]).astype(BF16)
        rows_ref[:, D:] = (
            dot(first.astype(BF16), first_all[...]) + dot(second.astype(BF16), second_all[...])
        ).astype(BF16)


def place_kernel(rows_ref, targets_ref, out_ref):
    slot_block, tokens = out_ref.shape[0], rows_ref.shape[0]
    slots = pl.program_id(0) * slot_block + iota((slot_block, tokens), 0)
    hot = jnp.where(slots == targets_ref[0:1, :], 1.0, 0.0) + jnp.where(
        slots == targets_ref[1:2, :], 1.0, 0.0
    )
    out_ref[...] = dot(hot.astype(BF16), rows_ref[...]).astype(BF16)


def place_rows(rows, targets, slots):
    tokens = rows.shape[0]
    return pl.pallas_call(
        place_kernel,
        grid=(4,),
        in_specs=[whole((tokens, D)), whole((2, tokens))],
        out_specs=pl.BlockSpec((slots // 4, D), lambda step: (step, 0)),
        out_shape=jax.ShapeDtypeStruct((slots, D), BF16),
        compiler_params=params(),
        cost_estimate=cost(2 * tokens * D * slots, 4 * tokens * D),
        name="place_rows",
    )(rows, targets)


def route_tokens(
    hidden, attended, upstream, extra, routes, targets, gain, gathered, experts, constant_count, slots
):
    tokens = hidden.shape[0]
    kinds = extra.shape[0]
    block = TOKENS['route']
    steps = tokens // block
    slot_block = slots // 4
    token_block = lambda width: pl.BlockSpec(
        (block, width), lambda step: (jnp.minimum(step, steps - 1), 0)
    )
    token_lanes = lambda height: pl.BlockSpec(
        (height, block), lambda step: (0, jnp.minimum(step, steps - 1))
    )
    slot_rows = pl.BlockSpec((slot_block, D + LANES), lambda step: (jnp.maximum(step - steps, 0), 0))
    kernel = functools.partial(
        route_kernel,
        token_steps=steps,
        experts=experts,
        constant_count=constant_count,
        slot_block=slot_block,
    )
    return pl.pallas_call(
        kernel,
        grid=(steps + 4,),
        in_specs=[
            token_block(D),
            token_block(D),
            token_block(D),
            token_lanes(kinds),
            token_lanes(2),
            whole((2, tokens)),
            whole((1, D)),
            pl.BlockSpec((D, D), lambda step: (0, 3)),
            pl.BlockSpec((D, LANES), lambda step: (0, 4 * D // LANES)),
        ],
        out_specs=[
            token_block(D),
            token_block(D),
            token_block(LANES),
            slot_rows,
        ],
        out_shape=[
            jax.ShapeDtypeStruct((tokens, D), F32),
            jax.ShapeDtypeStruct((tokens, D), BF16),
            jax.ShapeDtypeStruct((tokens, LANES), F32),
            jax.ShapeDtypeStruct((slots, D + LANES), BF16),
        ],
        scratch_shapes=[
            pltpu.VMEM((tokens, D), BF16),
            pltpu.VMEM((tokens, LANES), BF16),
            pltpu.VMEM((tokens, LANES), BF16),
            pltpu.VMEM((LANES, block), F32),
        ],
        compiler_params=params(),
        cost_estimate=cost(2 * tokens * D * (D + slots), 20 * tokens * D),
        name="route_tokens",
    )(hidden, attended, upstream, extra, routes, targets, gain, gathered, gathered)


def inner_spec(weights, pieces, column):
    if weights.ndim == 2:
        return pl.BlockSpec((D, pieces * BLOCK), lambda step: (0, column(step)))
    shards = weights.shape[0]
    return pl.BlockSpec((shards, pieces * D // shards, BLOCK), lambda step: (0, column(step), 0))


def read_inner(ref):
    if len(ref.shape) == 2:
        return ref[...]
    shards = ref.shape[0]
    rows = D // shards
    pieces = [
        jnp.concatenate([ref[position(shards, k), low : low + rows, :] for k in range(shards)], axis=0)
        for low in range(0, ref.shape[1], rows)
    ]
    return jnp.concatenate(pieces, axis=1)


def outer_specs(weights, pieces):
    if weights.ndim == 2:
        return [pl.BlockSpec((pieces * BLOCK, D), lambda step: (step, 0))]
    shards = weights.shape[0]
    first = weights.shape[1] // BLOCK - D // BLOCK
    even = lambda c: pl.BlockSpec((1, BLOCK, BLOCK), lambda step: (step, first + c, 0))
    odd = lambda c: pl.BlockSpec((1, BLOCK, BLOCK), lambda step: (shards - 1 - step, first + c, 0))
    return [even(c) for c in range(D // BLOCK)] + [odd(c) for c in range(D // BLOCK)]


def read_outer(refs):
    if len(refs) == 1:
        return refs[0][...]
    half = len(refs) // 2
    return jnp.concatenate(
        [jnp.concatenate([ref[0] for ref in some], axis=1) for some in (refs[:half], refs[half:])], axis=0
    )


def expert_kernel(rows_ref, grads_ref, gate_ref, up_ref, *refs, outers):
    outer_refs, refs = refs[:outers], refs[outers:]
    joined_ref, active_ref, produced_ref, met_ref, weighed_ref, total = refs
    step = pl.program_id(0)

    @pl.when(step == 0)
    def _():
        chosen = jnp.sum(rows_ref[:, D:].astype(F32), axis=1, keepdims=True)
        weighed_ref[...] = (chosen * grads_ref[...].astype(F32)).astype(BF16)

    outer = read_outer(outer_refs)
    gates, ups = read_inner(gate_ref), read_inner(up_ref)
    parts = [slice(low, low + BLOCK) for low in range(0, outer.shape[0], BLOCK)]

    def enter(part):
        return (
            dot(rows_ref[:, :D], gates[:, part]),
            dot(rows_ref[:, :D], ups[:, part]),
            dot(weighed_ref[...], outer[part], NT),
        )

    part_total = 0.0
    entered = enter(parts[0])
    for index, part in enumerate(parts):
        gate, up, grad_active = entered
        if index + 1 < len(parts):
            entered = enter(parts[index + 1])
        sigmoid = 1.0 / (1.0 + jnp.exp(-gate))
        silu = gate * sigmoid
        active = (silu * up).astype(BF16)
        active_ref[:, part] = active
        slope = sigmoid * (1.0 + gate * (1.0 - sigmoid))
        joined_ref[0, :, part] = (grad_active * up * slope).astype(BF16)
        joined_ref[1, :, part] = (grad_active * silu).astype(BF16)
        part_total = part_total + dot(active, outer[part])
    total[...] = jnp.where(step == 0, part_total, total[...] + part_total)

    @pl.when(step == pl.num_programs(0) - 1)
    def _():
        produced = total[...].astype(BF16)
        produced_ref[...] = produced
        met = weighed_ref[...].astype(F32) * produced.astype(F32)
        met = sum(met[:, low : low + LANES] for low in range(0, D, LANES))
        met_ref[...] = jnp.sum(met.T, axis=0, keepdims=True)


def expert_forward(rows, grads, inner, outer):
    count = rows.shape[0]
    pieces = 2
    width = pieces * BLOCK
    steps = FF // width
    outers = outer_specs(outer, pieces)
    return pl.pallas_call(
        functools.partial(expert_kernel, outers=len(outers)),
        grid=(steps,),
        in_specs=[
            whole((count, D + LANES)),
            whole((count, D)),
            inner_spec(inner, pieces, lambda step: step),
            inner_spec(inner, pieces, lambda step: steps + step),
            *outers,
        ],
        out_specs=[
            pl.BlockSpec((2, count, width), lambda step: (0, 0, step)),
            pl.BlockSpec((count, width), lambda step: (0, step)),
            whole((count, D)),
            whole((1, count)),
            whole((count, D)),
        ],
        out_shape=[
            jax.ShapeDtypeStruct((2, count, FF), BF16),
            jax.ShapeDtypeStruct((count, FF), BF16),
            jax.ShapeDtypeStruct((count, D), BF16),
            jax.ShapeDtypeStruct((1, count), F32),
            jax.ShapeDtypeStruct((count, D), BF16),
        ],
        scratch_shapes=[pltpu.VMEM((count, D), F32)],
        compiler_params=params(),
        cost_estimate=cost(8 * count * D * FF, 6 * count * FF + 6 * D * FF, count * FF),
        name="expert_forward",
    )(rows, grads, inner, inner, *[outer] * len(outers))


def outer_weights_kernel(*refs):
    *active_refs, weighed_ref, out_ref = refs
    active = jnp.concatenate([ref[...] for ref in active_refs], axis=1)
    out_ref[...] = dot(active, weighed_ref[...], TN).astype(BF16).reshape(out_ref.shape)


def outer_weights(active, weighed, shards):
    count = active.shape[0]
    width = FF // shards
    if width % LANES:
        lanes, taken, places = LANES, LANES // width, [lambda step: step]
    else:
        lanes, taken = width, 4
        place = lambda at: jnp.where(at < shards // 2, 2 * at, 2 * (shards - 1 - at) + 1)
        places = [lambda step, k=k: place(4 * step + k) for k in range(4)]
    out = pl.pallas_call(
        outer_weights_kernel,
        grid=(shards // taken,),
        in_specs=[
            pl.BlockSpec((count, lanes), lambda step, place=place: (0, place(step))) for place in places
        ]
        + [whole((count, D))],
        out_specs=pl.BlockSpec((taken, width, D), lambda step: (step, 0, 0)),
        out_shape=jax.ShapeDtypeStruct((shards, width, D), BF16),
        compiler_params=params(),
        cost_estimate=cost(2 * count * D * FF, 2 * count * FF + 2 * D * FF),
        name="outer_weights",
    )(*[active] * len(places), weighed)
    if width % LANES:
        out = jnp.concatenate([out[k : k + 1] for k in around(shards)], axis=0)
    return out


def inner_weights_kernel(rows_ref, joined_ref, out_ref, turned):
    @pl.when(pl.program_id(0) == 0)
    def _():
        turned[...] = rows_ref[...].T

    shards, _, share, _ = out_ref.shape
    for half in range(2):
        grads = dot(turned[...], joined_ref[half]).astype(BF16)
        for k in range(shards):
            out_ref[position(shards, k), half] = grads[k * share : (k + 1) * share]


def inner_weights(rows, joined, shards):
    count = rows.shape[0]
    width = 2 * BLOCK
    share = D // shards
    return pl.pallas_call(
        inner_weights_kernel,
        grid=(FF // width,),
        in_specs=[
            pl.BlockSpec((count, D), lambda step: (0, 0)),
            pl.BlockSpec((2, count, width), lambda step: (0, 0, step)),
        ],
        out_specs=pl.BlockSpec((shards, 2, share, width), lambda step: (0, 0, 0, step)),
        out_shape=jax.ShapeDtypeStruct((shards, 2, share, FF), BF16),
        scratch_shapes=[pltpu.VMEM((D, count), BF16)],
        compiler_params=params(),
        cost_estimate=cost(4 * count * D * FF, 4 * count * FF + 4 * D * FF),
        name="inner_weights",
    )(rows, joined)


def expert_backward_kernel(joined_ref, inner_ref, grads_ref, total):
    step = pl.program_id(0)
    part = dot(joined_ref[0], read_inner(inner_ref), NT)
    total[...] = jnp.where(step == 0, part, total[...] + part)

    @pl.when(step == pl.num_programs(0) - 1)
    def _():
        grads_ref[...] = total[...].astype(BF16)


def expert_backward(joined, inner):
    count = joined.shape[1]
    pieces = 4
    width = pieces * BLOCK
    half = FF // width
    return pl.pallas_call(
        expert_backward_kernel,
        grid=(2 * half,),
        in_specs=[
            pl.BlockSpec((1, count, width), lambda step: (step // half, 0, step % half)),
            inner_spec(inner, pieces, lambda step: step),
        ],
        out_specs=whole((count, D)),
        out_shape=jax.ShapeDtypeStruct((count, D), BF16),
        scratch_shapes=[pltpu.VMEM((count, D), F32)],
        compiler_params=params(),
        cost_estimate=cost(4 * count * D * FF, 4 * count * FF + 4 * D * FF),
        name="expert_backward",
    )(joined, inner)


def mix_kernel(
    targets_ref,
    table_ref,
    middle_ref,
    normed_ref,
    small_ref,
    *refs,
    value_place,
    constant_count,
):
    block = middle_ref.shape[0]
    *returned_refs, out_ref = refs
    returned = jnp.concatenate([ref[...] for ref in returned_refs], axis=0)
    slots = returned.shape[0]
    table = table_ref[...]
    columns = iota((block, slots), 1)
    lane = iota((block, LANES), 1)
    blended = normed_ref[...].astype(F32) * table[:, COEF : COEF + 1]
    for route in range(2):
        hot = jnp.where(columns == targets_ref[:, route : route + 1], 1.0, 0.0).astype(BF16)
        paired = dot(hot, returned)
        blended = blended + table[:, CHOSEN + route : CHOSEN + route + 1] * paired
    values = jnp.zeros((block, LANES), F32)
    for which in range(constant_count):
        place = BETA + which
        values = jnp.where(lane == value_place + which, table[:, place : place + 1], values)
    upper = values.astype(BF16)
    lower = (values - upper.astype(F32)).astype(BF16)
    blended = blended + (dot(upper, small_ref[...], NT) + dot(lower, small_ref[...], NT))
    out_ref[...] = (middle_ref[...] + blended).astype(BF16)


def mix_branches(returned, targets, table, middle, normed, gathered, value_place, constant_count):
    block = TOKENS["mix"]
    tokens = middle.shape[0]
    slots = sum(block.shape[0] for block in returned)
    token_block = lambda width: pl.BlockSpec((block, width), lambda step: (step, 0))
    return pl.pallas_call(
        functools.partial(mix_kernel, value_place=value_place, constant_count=constant_count),
        grid=(tokens // block,),
        in_specs=[
            token_block(2),
            token_block(LANES),
            token_block(D),
            token_block(D),
            pl.BlockSpec((D, LANES), lambda step: (0, 4 * D // LANES)),
            *[whole(array.shape) for array in returned],
        ],
        out_specs=token_block(D),
        out_shape=jax.ShapeDtypeStruct((tokens, D), BF16),
        compiler_params=params(62),
        cost_estimate=cost(4 * tokens * D * slots, 12 * tokens * D),
        name="mix_branches",
    )(targets, table, middle, normed, gathered, *returned)


def middle_kernel(
    core_ref,
    returned_ref,
    met_ref,
    targets_ref,
    routes_ref,
    prior_ref,
    table_ref,
    middle_ref,
    normed_ref,
    upstream_ref,
    attended_ref,
    small_ref,
    gain_ref,
    weight_ref,
    grad_middle_ref,
    grad_attended_ref,
    mixer_ref,
    *refs,
    experts,
    constant_count,
):
    weight_refs, (work, grad_gain, grad_small, grad_weight) = refs[:-4], refs[-4:]
    block = middle_ref.shape[0]
    slots = returned_ref.shape[0]
    kinds = prior_ref.shape[0]
    gates = 2 * constant_count
    first = pl.program_id(0) == 0
    table = table_ref[...]
    wide = upstream_ref[...].astype(F32)
    columns = iota((block, slots), 1)
    hot = jnp.where(columns == targets_ref[:, 0:1], 1.0, 0.0) + jnp.where(
        columns == targets_ref[:, 1:2], 1.0, 0.0
    )
    hot = hot.astype(BF16)
    total = dot(hot, returned_ref[...]) + wide * table[:, COEF : COEF + 1]
    met = met_ref[...]
    upper = met.astype(BF16).astype(F32)
    here = iota((LANES, slots), 1) // (slots // experts) == iota((LANES, slots), 0) % experts
    halves = jnp.where(iota((LANES, slots), 0) < experts, upper, met - upper)
    met = jnp.where(jnp.logical_and(here, iota((LANES, slots), 0) < 2 * experts), halves, 0.0)
    met = dot(hot, met.astype(BF16), NT)
    met = met.T
    turned = table.T
    probs = turned[PROBS : PROBS + kinds]
    places = iota((kinds, block), 0)
    met = met[:experts] + met[experts : 2 * experts]
    work[...] = jnp.zeros_like(work)
    work[:experts] = met
    weighed = work[:kinds]
    for route in range(2):
        rest = turned[REST + route : REST + route + 1]
        weighed = weighed + jnp.where(places == routes_ref[route : route + 1, :], rest, 0.0)
    grad_logits = weighed - probs * jnp.sum(weighed, axis=0, keepdims=True)
    part = lax.dot_general(
        prior_ref[...], grad_logits, NT, precision=highest, preferred_element_type=F32
    )
    mixer_ref[...] = jnp.where(first, part, mixer_ref[...] + part)
    work[:kinds] = grad_logits
    work[kinds : kinds + gates] = turned[GATE_GRAD : GATE_GRAD + gates]
    work[kinds + gates : kinds + gates + constant_count] = turned[BETA : BETA + constant_count]
    values = work[...].T
    upper = values.astype(BF16)
    lower = (values - upper.astype(F32)).astype(BF16)
    is_small = iota((block, LANES), 1) < kinds + gates
    nothing = jnp.zeros((block, LANES), BF16)
    total = total + (
        dot(jnp.where(is_small, upper, nothing), small_ref[...], NT)
        + dot(jnp.where(is_small, lower, nothing), small_ref[...], NT)
    )
    both = jnp.concatenate([upper, lower], axis=1)
    part = jnp.where(
        iota((1, 2 * LANES), 1) % LANES < kinds + gates,
        dot(normed_ref[...], both, TN),
        dot(upstream_ref[...], both, TN),
    )
    part = part[:, :LANES] + part[:, LANES:]
    grad_small[...] = jnp.where(first, part, grad_small[...] + part)

    scale = table[:, SCALE : SCALE + 1]
    unit = middle_ref[...] * scale
    part = jnp.sum(total * unit, axis=0, keepdims=True)
    grad_gain[...] = jnp.where(first, part, grad_gain[...] + part)
    inner = total * gain_ref[...]
    grad_middle = wide + scale * (inner - unit * jnp.mean(inner * unit, axis=1, keepdims=True))
    grad_middle_ref[...] = grad_middle
    rounded = grad_middle.astype(BF16)
    grad_attended_ref[...] = dot(rounded, weight_ref[...], NT).astype(BF16)
    part = dot(attended_ref[...], rounded, TN)
    grad_weight[:, :D] = jnp.where(first, part, grad_weight[:, :D] + part)

    @pl.when(pl.program_id(0) == pl.num_programs(0) - 1)
    def _():
        column = jnp.broadcast_to(grad_gain[...], (LANES, D)).T
        place = kinds + gates + constant_count
        grad_weight[:, D:] = jnp.where(iota((D, LANES), 1) == place, column, grad_small[...])
        if len(weight_refs) == 1:
            weight_refs[0][...] = grad_weight[...].astype(BF16)
        else:
            part_rows(grad_weight, core_ref[0], *weight_refs)


def middle_backward(
    core,
    returned,
    met,
    targets,
    routes,
    prior,
    table,
    middle,
    normed,
    upstream,
    attended,
    gain,
    gathered,
    experts,
    constant_count,
    shards,
):
    block = TOKENS["middle"]
    tokens = middle.shape[0]
    slots = returned.shape[0]
    kinds = prior.shape[0]
    rows = D // shards
    spec = lambda shape, place: pl.BlockSpec(shape, lambda step, core: place(step))
    always = lambda shape: spec(shape, lambda step: (0,) * len(shape))
    token_block = lambda width: spec((block, width), lambda step: (step, 0))
    token_lanes = lambda height: spec((height, block), lambda step: (0, step))
    if rows % 8:
        weights = [(D, D + LANES)]
    else:
        weights = [(shards // 2, rows, D + LANES)] * 2
    results = pl.pallas_call(
        functools.partial(middle_kernel, experts=experts, constant_count=constant_count),
        grid_spec=pltpu.PrefetchScalarGridSpec(
            num_scalar_prefetch=1,
            grid=(tokens // block,),
            in_specs=[
                always((slots, D)),
                always((1, slots)),
                token_block(2),
                token_lanes(2),
                token_lanes(kinds),
                token_block(LANES),
                token_block(D),
                token_block(D),
                token_block(D),
                token_block(D),
                spec((D, LANES), lambda step: (0, 4 * D // LANES)),
                always((1, D)),
                spec((D, D), lambda step: (0, 3)),
            ],
            out_specs=[token_block(D), token_block(D), always((kinds, kinds))]
            + [always(shape) for shape in weights],
            scratch_shapes=[
                pltpu.VMEM((LANES, block), F32),
                pltpu.VMEM((1, D), F32),
                pltpu.VMEM((D, LANES), F32),
                pltpu.VMEM((D, D + LANES), F32),
            ],
        ),
        out_shape=[
            jax.ShapeDtypeStruct((tokens, D), F32),
            jax.ShapeDtypeStruct((tokens, D), BF16),
            jax.ShapeDtypeStruct((kinds, kinds), F32),
        ]
        + [jax.ShapeDtypeStruct(shape, BF16) for shape in weights],
        compiler_params=params(62),
        cost_estimate=cost(2 * tokens * D * (slots + 2 * D), 18 * tokens * D),
        name="middle_backward",
    )(
        core,
        returned,
        met,
        targets,
        routes,
        prior,
        table,
        middle,
        normed,
        upstream,
        attended,
        gathered,
        gain,
        gathered,
    )
    return *results[:3], results[3:]


def input_kernel(packed_ref, weight_ref, hidden_ref, grad_middle_ref, gain_ref, out_ref, grad_gain_ref):
    total = sum(dot(packed_ref[c], weight_ref[:, c * D : (c + 1) * D], NT) for c in range(3))
    values = hidden_ref[...].astype(F32)
    scale = row_scale(values)
    unit = values * scale
    part = jnp.sum(total * unit, axis=0, keepdims=True)
    grad_gain_ref[...] = jnp.where(pl.program_id(0) == 0, part, grad_gain_ref[...] + part)
    inner = total * gain_ref[...]
    out_ref[...] = grad_middle_ref[...] + scale * (
        inner - unit * jnp.mean(inner * unit, axis=1, keepdims=True)
    )


def input_backward(grad_packed, gathered, hidden, grad_middle, gain):
    block = TOKENS['input']
    tokens = hidden.shape[0]
    token_block = lambda width: pl.BlockSpec((block, width), lambda step: (step, 0))
    return pl.pallas_call(
        input_kernel,
        grid=(tokens // block,),
        in_specs=[
            pl.BlockSpec((3, block, D), lambda step: (0, step, 0)),
            pl.BlockSpec((D, 3 * D), lambda step: (0, 0)),
            token_block(D),
            token_block(D),
            whole((1, D)),
        ],
        out_specs=[token_block(D), whole((1, D))],
        out_shape=[
            jax.ShapeDtypeStruct((tokens, D), F32),
            jax.ShapeDtypeStruct((1, D), F32),
        ],
        compiler_params=params(),
        cost_estimate=cost(6 * tokens * D * D, 16 * tokens * D),
        name="input_backward",
    )(grad_packed, gathered, hidden, grad_middle, gain)


def pair_targets(routes, priority, experts, total_kinds, capacity):
    kind_ids = jnp.arange(total_kinds, dtype=jnp.int32)
    hot = [(routes[:, k : k + 1] == kind_ids[None, :]).astype(F32) for k in range(2)]
    earlier = (priority[None, :] < priority[:, None]).astype(BF16)
    before = dot(earlier, (hot[0] + hot[1]).astype(BF16))
    slots = jnp.stack([jnp.sum(before * one, axis=1) for one in hot], axis=1).astype(jnp.int32)
    kept_pairs = jnp.logical_and(routes < experts, slots < capacity)
    return jnp.where(kept_pairs, routes * capacity + slots, experts * capacity)


def exchange(blocks, axis):
    return lax.all_to_all(blocks, axis, split_axis=0, concat_axis=0, tiled=True)


def exchange_apart(blocks, axis):
    count, me = lax.axis_size(axis), lax.axis_index(axis)
    came = []
    for step in range(count):
        block = pick(blocks, (me + step) % count, 0)
        if step:
            block = lax.ppermute(block, axis, [(i, (i + step) % count) for i in range(count)])
        came.append(block)
    return came


def flip(axis):
    return [(i, i ^ 1) for i in range(lax.axis_size(axis))]


def shift(axis, step):
    count = lax.axis_size(axis)
    return [(i, (i + 2 * step) % count) for i in range(count)]


def gather_far(mine):
    far, depth = lax.axis_size("dp") // 2, lax.axis_index("dp") // 2
    column = jnp.zeros((far, *mine.shape), mine.dtype)
    for step in range(far):
        came = mine if step == 0 else lax.ppermute(mine, "dp", shift("dp", step))
        column = lax.dynamic_update_slice(column, came[None], ((depth - step) % far, 0, 0))
    return column


def gather_all(column):
    far, rows, width = column.shape
    wide, side = lax.axis_size("expert") // 2, lax.axis_index("dp") % 2
    place, core = lax.axis_index("expert") // 2, lax.axis_index("expert") % 2
    near = [column, lax.ppermute(column, "dp", flip("dp"))]
    total = jnp.zeros((far, 2, wide, 2, rows, width), column.dtype)
    for step in range(wide):
        for other in range(2):
            piece = near[other]
            if step:
                piece = lax.ppermute(piece, "expert", shift("expert", step))
            twin = lax.ppermute(piece, "expert", flip("expert"))
            spot = (0, side ^ other, (place - step) % wide)
            shaped = (far, 1, 1, 1, rows, width)
            total = lax.dynamic_update_slice(total, piece.reshape(shaped), (*spot, core, 0, 0))
            total = lax.dynamic_update_slice(total, twin.reshape(shaped), (*spot, 1 - core, 0, 0))
    return total.reshape(-1, width)


def pick(array, index, axis):
    return lax.dynamic_index_in_dim(array, index, axis, keepdims=False)


def scatter_side(parted):
    wide = lax.axis_size("expert") // 2
    place, core = lax.axis_index("expert") // 2, lax.axis_index("expert") % 2
    if len(parted) == 1:
        terms = parted[0].reshape(lax.axis_size("dp") * wide, 2, -1, parted[0].shape[1])
        parted = (pick(terms, 1 - core, 1), pick(terms, core, 1))
    send, keep = parted
    came = lax.ppermute(send, "expert", flip("expert"))
    pair = (keep.astype(F32) + came.astype(F32)).astype(BF16)
    pair = pair.reshape(lax.axis_size("dp"), wide, *pair.shape[1:])
    total = pick(pair, place, 1).astype(F32)
    for step in range(1, wide):
        came = lax.ppermute(pick(pair, (place + step) % wide, 1), "expert", shift("expert", step))
        total = total + came.astype(F32)
    return total.astype(BF16)


def around(count):
    return list(range(0, count, 2)) + list(range(count - 1, 0, -2))


def position(count, place):
    return place // 2 if place % 2 == 0 else count - 1 - place // 2


def split_experts(expert_in, expert_out):
    inner, outer = expert_in[0].astype(BF16), expert_out[0].astype(BF16)
    if inner.shape[0] % 16 or outer.shape[0] != BLOCK:
        return [inner, outer]
    pieces = [
        array.reshape(array.shape[0], -1, BLOCK).transpose(1, 0, 2).reshape(-1, BLOCK)
        for array in (inner, outer)
    ]
    return [jnp.concatenate(pieces, axis=0)]


def gather_experts(pieces):
    ring = [around(lax.axis_size("dp"))]
    if len(pieces) == 1:
        both = lax.all_gather(pieces[0], "dp", axis=0, axis_index_groups=ring)
        return both, both
    return [lax.all_gather(piece, "dp", axis=0, tiled=True) for piece in pieces]


def scatter_expert(grads):
    ring = [around(lax.axis_size("dp"))]
    return lax.psum_scatter(grads, "dp", scatter_dimension=0, tiled=True, axis_index_groups=ring)[0]


def own_kernel(
    in_ref, shares_ref, inner_ref, outer_ref, gain_ref, mixer_ref, own_ref, out_ref, own_outer_ref, few_ref, *, kinds
):
    total = jnp.sum(in_ref[...].astype(F32), axis=0)
    out = jnp.sum(shares_ref[...].astype(F32), axis=0)
    for pair in range(D // PAIR):
        for part in range(3):
            low, place = (3 * pair + part) * PAIR, part * D + pair * PAIR
            own_ref[:, place : place + PAIR] = total[:, low : low + PAIR]
    out_ref[...] = out
    inner, outer = inner_ref[...].astype(F32), outer_ref[...].astype(F32)
    own_outer_ref[...] = outer
    width = few_ref.shape[2]
    square = jnp.sum(jnp.sum(inner * inner, axis=0), axis=(0, 1), keepdims=True)
    for member in (total, out, outer):
        square = square + jnp.sum(member * member, axis=(0, 1), keepdims=True)
    few = few_ref.at[0]
    few[...] = jnp.zeros_like(few)
    few[0:1, :D] = gain_ref[...]
    for row in range(kinds):
        place = D + row * kinds
        few[0:1, place : place + kinds] = mixer_ref[row : row + 1, :]
    few[0:1, width - LANES :] = jnp.broadcast_to(square, (1, LANES))
    row = few[...]
    for device in range(1, few_ref.shape[0]):
        few_ref[device] = row


def own_sums(in_shares, out_shares, inner, outer, grad_gain, grad_mixer, devices):
    kinds = grad_mixer.shape[0]
    width = D + (-(-kinds * kinds // LANES) + 1) * LANES
    rows = in_shares.shape[1]
    return pl.pallas_call(
        functools.partial(own_kernel, kinds=kinds),
        out_shape=[
            jax.ShapeDtypeStruct((rows, 3 * D), F32),
            jax.ShapeDtypeStruct((rows, D + LANES), F32),
            jax.ShapeDtypeStruct(outer.shape, F32),
            jax.ShapeDtypeStruct((devices, 1, width), F32),
        ],
        compiler_params=params(62),
        cost_estimate=cost(6 * D * FF, 3 * D * FF),
        name="own_sums",
    )(in_shares, out_shares, inner, outer, grad_gain, grad_mixer)


def adam(master, first, second, grad, factor, step_rate):
    clipped = grad * factor
    first_new = beta_moment * first + (1.0 - beta_moment) * clipped
    second_new = beta_moment * second + (1.0 - beta_moment) * clipped * clipped
    correct = 1.0 - beta_moment**step_number
    update = (
        first_new / correct / (jnp.sqrt(second_new / correct) + adam_epsilon) + decay_rate * master
    )
    return (master - step_rate * update, first_new, second_new)


def update_kernel(*refs, kinds, constant_count):
    index_ref, few_ref, in_ref, out_ref, inner_ref, outer_ref = refs[:6]
    states = [refs[6 + 3 * which : 9 + 3 * which] for which in range(8)]
    norm_ref, results = refs[30], refs[31:]
    width = out_ref.shape[1]
    few = jnp.sum(few_ref[...], axis=0)
    gain_total = few[:, :D]
    mixer_total = few[:, D : D + kinds * kinds]
    square = (
        few[:, few.shape[1] - 1 :]
        + jnp.sum(gain_total * gain_total, axis=1, keepdims=True)
        + jnp.sum(mixer_total * mixer_total, axis=1, keepdims=True)
    )
    norm = jnp.sqrt(square)
    factor = clip_limit / jnp.maximum(norm, clip_limit)
    places = iter(results)
    slots = [[next(places) for _ in range(4 if which in (0, 7) else 5)] for which in range(8)]

    def step(which, grad):
        master, first, second = states[which]
        outs = slots[which]
        if len(outs) == 5:
            outs[0][...] = grad.reshape(outs[0].shape)
            outs = outs[1:]
        shape = outs[0].shape
        lay = lambda value: value.reshape(grad.shape)
        new = adam(lay(master[...]), lay(first[...]), lay(second[...]), grad, factor, learn_rates[which])
        for ref, value in zip(outs, new + (new[0],)):
            ref[...] = value.reshape(shape).astype(ref.dtype)

    step(6, inner_ref[0].astype(F32))
    step(7, outer_ref[...])

    @pl.when(pl.program_id(0) == 0)
    def _():
        norm_ref[...] = norm
        step(0, in_ref[...])
        step(1, out_ref[:, :D])
        rows = out_ref.shape[0]
        narrow = jnp.pad(out_ref[:, D:], ((0, LANES - rows), (0, 0))).T
        step(2, narrow[:kinds, :rows])
        step(3, jnp.concatenate([mixer_total[:, k * kinds : (k + 1) * kinds] for k in range(kinds)], axis=0))
        small = kinds + 3 * constant_count
        step(4, narrow[kinds:small, :rows])
        start = index_ref[0] * rows
        picked = (iota((D, LANES), 0) == start + iota((D, LANES), 1)).astype(F32)
        own = lax.dot_general(
            jnp.broadcast_to(gain_total, (8, D)), picked, NN, precision=highest, preferred_element_type=F32
        )
        step(5, jnp.concatenate([own[0:1, :rows], narrow[small : small + 1, :rows]], axis=0))


def update(index, few, in_own, out_own, inner_own, outer_own, states, kinds, constant_count):
    steps = 2
    turn = lambda which, array: array.T if which in (2, 4) else array
    states = [[turn(which, array) for array in state] for which, state in enumerate(states)]
    half = steps // 2
    flat = [array for state in states for array in state]

    def spec(shape):
        if len(shape) == 3 and shape[2] == 2 * FF:
            return pl.BlockSpec((1, shape[1], shape[2] // steps), lambda step, index: (0, 0, step))
        if len(shape) == 3:
            return pl.BlockSpec((1, shape[1] // steps, shape[2]), lambda step, index: (0, step, 0))
        return pl.BlockSpec(shape, lambda step, index: (0, 0))

    out_shape = [jax.ShapeDtypeStruct((1, 1), F32)]
    for which in range(8):
        shape = states[which][0].shape
        kept = 3 if which in (0, 7) else 4
        out_shape += [jax.ShapeDtypeStruct(shape, F32)] * kept + [jax.ShapeDtypeStruct(shape, BF16)]
    results = pl.pallas_call(
        functools.partial(update_kernel, kinds=kinds, constant_count=constant_count),
        grid_spec=pltpu.PrefetchScalarGridSpec(
            num_scalar_prefetch=1,
            grid=(steps,),
            in_specs=[
                pl.BlockSpec(few.shape, lambda step, index: (0, 0, 0)),
                spec(in_own.shape),
                spec(out_own.shape),
                pl.BlockSpec(
                    (1, inner_own.shape[1], FF // half), lambda step, index: (step // half, 0, step % half)
                ),
                pl.BlockSpec((outer_own.shape[0] // steps, D), lambda step, index: (step, 0)),
            ]
            + [spec(array.shape) for array in flat],
            out_specs=[spec(leaf.shape) for leaf in out_shape],
        ),
        out_shape=out_shape,
        compiler_params=params(),
        cost_estimate=cost(40 * D * FF, 60 * D * FF // 2),
        name="update",
    )(index, few, in_own, out_own, inner_own, outer_own, *flat)
    norm, rest = results[0].reshape(()), list(results[1:])
    grads = {0: in_own, 7: outer_own[None]}
    ordered = []
    for which in range(8):
        taken = 4 if which in grads else 5
        ordered += [grads[which]] if which in grads else []
        ordered += [turn(which, array) for array in rest[:taken]]
        rest = rest[taken:]
    return norm, ordered


def body(
    hidden_in,
    gate_prior,
    routes,
    priority,
    segments,
    cotangent,
    attend_in,
    first_attend_in,
    second_attend_in,
    attend_out,
    first_attend_out,
    second_attend_out,
    router,
    first_router,
    second_router,
    gate_mix,
    first_gate_mix,
    second_gate_mix,
    constants,
    first_constants,
    second_constants,
    norm_gains,
    first_norm_gains,
    second_norm_gains,
    expert_in,
    first_expert_in,
    second_expert_in,
    expert_out,
    first_expert_out,
    second_expert_out,
):
    groups = lax.axis_size("expert")
    devices = lax.axis_size("dp") * groups
    kinds = gate_prior.shape[1]
    constant_count = constants.shape[1] // 3
    experts = kinds - 2 - constant_count
    token_count = hidden_in.shape[0]
    width_top = routes.shape[1]
    capacity = max(2, width_top * token_count // kinds // 8 * 8)
    slots = experts * capacity
    small_width = kinds + 3 * constant_count
    gate_end = kinds + 2 * constant_count

    expert_pieces = split_experts(expert_in, expert_out)
    mine = jnp.concatenate(
        [
            attend_in,
            attend_out,
            router,
            constants,
            norm_gains.T,
            jnp.zeros((attend_in.shape[0], LANES - small_width - 2), F32),
        ],
        axis=1,
    ).astype(BF16)
    targets = pair_targets(routes, priority[0], experts, kinds, capacity)
    target_rows = targets.T
    away = (lax.axis_index("expert") - targets // (slots // groups)) % groups
    near_targets = jnp.where(
        targets < slots, away * (slots // groups) + targets % (slots // groups), slots
    )
    split = (groups, slots // groups, -1)
    placed = place_rows(cotangent, target_rows, slots).reshape(split)
    mine, expert_pieces = lax.optimization_barrier((mine, expert_pieces))
    column = gather_far(mine)
    column, placed, expert_pieces = lax.optimization_barrier((column, placed, expert_pieces))
    gathered = gather_all(column)
    expert_inner, expert_outer = gather_experts(expert_pieces)
    gains = gathered[:, 4 * D + small_width : 4 * D + small_width + 2].astype(F32).T
    gains, placed = lax.optimization_barrier((gains, placed))
    gain_first, gain_second = gains[0:1], gains[1:2]
    arrived_grad = exchange(placed, "expert").reshape(slots, D)
    route_rows = routes.T
    prior_rows = gate_prior.T
    extra = jnp.dot(gate_mix.astype(BF16).astype(F32).T, prior_rows, precision=highest)
    seg_row = segments
    seg_column = segments.reshape(token_count, 1)

    normed_first, packed, attended, logsum = attend_forward(
        hidden_in, gain_first, gathered, seg_column, seg_row
    )
    middle, normed_second, table, rows = route_tokens(
        hidden_in,
        attended,
        cotangent,
        extra,
        route_rows,
        target_rows,
        gain_second,
        gathered,
        experts,
        constant_count,
        slots,
    )
    arrived = exchange(rows.reshape(split), "expert").reshape(slots, D + LANES)
    grad_joined, active, produced, met, weighed = expert_forward(
        arrived, arrived_grad, expert_inner, expert_outer
    )
    outer_own = scatter_expert(outer_weights(active, weighed, lax.axis_size("dp")))
    met = exchange(met.reshape(groups, 1, slots // groups), "expert").reshape(1, slots)
    grad_rows = expert_backward(grad_joined, expert_inner)
    met, grad_rows, grad_joined = lax.optimization_barrier((met, grad_rows, grad_joined))
    grad_returned = exchange(grad_rows.reshape(split), "expert").reshape(slots, D)
    grad_inner = inner_weights(arrived, grad_joined, lax.axis_size("dp"))
    grad_returned, produced, grad_inner = lax.optimization_barrier((grad_returned, produced, grad_inner))
    inner_own = scatter_expert(grad_inner)
    core = (lax.axis_index("expert") % 2).reshape(1).astype(jnp.int32)
    grad_middle, grad_attended, grad_mixer, grad_out_and_small = middle_backward(
        core,
        grad_returned,
        met,
        targets,
        route_rows,
        prior_rows,
        table,
        middle,
        normed_second,
        cotangent,
        attended,
        gain_second,
        gathered,
        experts,
        constant_count,
        devices,
    )
    out_sum = scatter_side(grad_out_and_small)

    grad_packed, grad_weight_in = attend_backward(
        core, packed, grad_attended, logsum, seg_column, seg_row, normed_first, devices
    )
    grad_weight_in, out_sum = lax.optimization_barrier((grad_weight_in, out_sum))
    in_sum = scatter_side(grad_weight_in)
    out_shares = exchange(out_sum, "dp")
    in_sum, out_shares, produced = lax.optimization_barrier((in_sum, out_shares, produced))
    returned = exchange_apart(produced.reshape(split), "expert")
    share = slots // groups
    if share % 16:
        returned = [jnp.concatenate(returned, axis=0)]
    in_shares = exchange(in_sum, "dp")
    input_grad, grad_gain_first = input_backward(
        grad_packed, gathered, hidden_in, grad_middle, gain_first
    )
    activations = mix_branches(
        returned, near_targets, table, middle, normed_second, gathered, gate_end, constant_count
    )

    in_own, out_own, outer_own, few = own_sums(
        in_shares, out_shares, inner_own, outer_own, grad_gain_first, grad_mixer, devices
    )
    few = exchange(few, BOTH)
    index = lax.axis_index("dp") * groups + lax.axis_index("expert")
    states = (
        (attend_in, first_attend_in, second_attend_in),
        (attend_out, first_attend_out, second_attend_out),
        (router, first_router, second_router),
        (gate_mix, first_gate_mix, second_gate_mix),
        (constants, first_constants, second_constants),
        (norm_gains, first_norm_gains, second_norm_gains),
        (expert_in, first_expert_in, second_expert_in),
        (expert_out, first_expert_out, second_expert_out),
    )
    grad_norm, updated = update(
        index.reshape(1).astype(jnp.int32),
        few,
        in_own,
        out_own,
        inner_own,
        outer_own,
        states,
        kinds,
        constant_count,
    )
    return (activations, input_grad, grad_norm, *updated)


def solution(mesh):
    in_specs = (
        P(("dp", "expert"), None),
        P(("dp", "expert"), None),
        P(("dp", "expert"), None),
        P(("dp", "expert"), None),
        P(("dp", "expert"), None),
        P(("dp", "expert"), None),
        P(("dp", "expert"), None),
        P(("dp", "expert"), None),
        P(("dp", "expert"), None),
        P(("dp", "expert"), None),
        P(("dp", "expert"), None),
        P(("dp", "expert"), None),
        P(("dp", "expert"), None),
        P(("dp", "expert"), None),
        P(("dp", "expert"), None),
        P(),
        P(),
        P(),
        P(("dp", "expert"), None),
        P(("dp", "expert"), None),
        P(("dp", "expert"), None),
        P(None, ("dp", "expert")),
        P(None, ("dp", "expert")),
        P(None, ("dp", "expert")),
        P("expert", "dp", None),
        P("expert", "dp", None),
        P("expert", "dp", None),
        P("expert", "dp", None),
        P("expert", "dp", None),
        P("expert", "dp", None),
    )
    out_specs = (
        P(("dp", "expert"), None),
        P(("dp", "expert"), None),
        P(),
        P(("dp", "expert"), None),
        P(("dp", "expert"), None),
        P(("dp", "expert"), None),
        P(("dp", "expert"), None),
        P(("dp", "expert"), None),
        P(("dp", "expert"), None),
        P(("dp", "expert"), None),
        P(("dp", "expert"), None),
        P(("dp", "expert"), None),
        P(("dp", "expert"), None),
        P(("dp", "expert"), None),
        P(("dp", "expert"), None),
        P(("dp", "expert"), None),
        P(("dp", "expert"), None),
        P(("dp", "expert"), None),
        P(),
        P(),
        P(),
        P(),
        P(),
        P(("dp", "expert"), None),
        P(("dp", "expert"), None),
        P(("dp", "expert"), None),
        P(("dp", "expert"), None),
        P(("dp", "expert"), None),
        P(None, ("dp", "expert")),
        P(None, ("dp", "expert")),
        P(None, ("dp", "expert")),
        P(None, ("dp", "expert")),
        P(None, ("dp", "expert")),
        P("expert", "dp", None),
        P("expert", "dp", None),
        P("expert", "dp", None),
        P("expert", "dp", None),
        P("expert", "dp", None),
        P("expert", "dp", None),
        P("expert", "dp", None),
        P("expert", "dp", None),
        P("expert", "dp", None),
        P("expert", "dp", None),
    )
    return jax.shard_map(body, mesh=mesh, in_specs=in_specs, out_specs=out_specs, check_vma=False)
```
